512 devices in a mesh: head: 8 (over x, y_lo), ctx: 64 (over y_hi, z, core).
Axes of the slice: x: 4, y: 8 (y_hi: 4, y_lo: 2; y = y_hi * 2 + y_lo), z: 8, core: 2. Of those that a mesh axis runs over, the one named last changes fastest.
Arguments:
- queries: bfloat16 [8192, 1024], P(('head', 'ctx')), may hold values from -30 to 30
- key_vecs: bfloat16 [8192, 128], P(('head', 'ctx')), may hold values from -10 to 10
- value_vecs: bfloat16 [8192, 128], P(('head', 'ctx')), may hold values from -6 to 6
- out_grad: bfloat16 [8192, 1024], P(('head', 'ctx')), may hold values from -6 to 6
- positions: int32 [8192], P(('head', 'ctx')), may hold values from 0 to 8191, as said below
- documents: int32 [8192], P(('head', 'ctx')), may hold values from 0 to 8, as said below
Outputs:
- grad_queries: float32 [8192, 1024], P(('head', 'ctx'))
- grad_keys: float32 [8192, 128], P(('head', 'ctx'))
- grad_values: float32 [8192, 128], P(('head', 'ctx'))
The draws below stay inside these ranges and needn't reach their ends.
Inputs may be any that keep to these rules, and one draw needn't show every extreme that they name: positions is a permutation of 0 to 8191; each aligned run of 16 rows holds 16 consecutive positions in rising order. `documents`: document ids never fall as positions rise, the token at position 0 has id 0, and every id up to the most occurs.
All inputs are finite; a program needn't handle non-finite values.
Results may differ from the reference program's by a relative error of at most 0.0059.
Values may be sent and summed in bfloat16 or wider, within the bound.
No kernel may reach another device: no remote copies, remote signals or barrier semaphores. Data moves between devices by JAX's collectives and lax.ppermute only.
A program may use at most 64 MiB of HBM per device.

```python
import math
import jax
import jax.numpy as jnp
from jax import lax

HD = 128
HEADS = 8
SEQ = 8192
RUN_LEN = 16


def draw_queries(key, part):
    sample = 1.5 * jnp.clip(jax.random.normal(jax.random.fold_in(key, 1), (SEQ, HEADS, HD), jnp.float32), -4.0, 4.0)
    return sample.reshape(SEQ, HEADS * HD).astype(jnp.bfloat16)


def draw_key_vecs(key, part):
    sample = jnp.clip(jax.random.normal(jax.random.fold_in(key, 2), (SEQ, HD), jnp.float32), -4.0, 4.0)
    return sample.astype(jnp.bfloat16)


def draw_positions(key, part):
    run_count = SEQ // RUN_LEN
    order = jax.random.permutation(jax.random.fold_in(key, 11), run_count).astype(jnp.int32)
    row_ids = jnp.arange(SEQ, dtype=jnp.int32)
    return (order[row_ids // RUN_LEN] * RUN_LEN + row_ids % RUN_LEN).astype(jnp.int32)


def draw_documents(key, part):
    placed = draw_positions(key, part)
    start_count = max(SEQ // 1024, 2)
    shuffled = jax.random.permutation(jax.random.fold_in(key, 13), SEQ - 1).astype(jnp.int32) + 1
    chosen = shuffled[:start_count]
    starts = jnp.zeros((SEQ,), jnp.int32).at[chosen].set(1)
    doc_at_position = jnp.cumsum(starts).astype(jnp.int32)
    return doc_at_position[placed].astype(jnp.int32)


def levels(rng, extent, split, least, top_value):
    gain = 1.0
    for position, parts in split:
        heights = jax.random.uniform(jax.random.fold_in(jax.random.fold_in(rng, 6), position), (parts,), jnp.float32, least / len(split), top_value / len(split))
        gain = gain * jnp.repeat(jnp.exp(heights), extent[position] // parts).reshape((-1,) + (1,) * (len(extent) - 1 - position))
    return gain


def normal_values(rng, extent, scale, most, shards=(), kind=jnp.bfloat16):
    drawn = scale * jax.random.normal(rng, extent, jnp.float32)
    if shards:
        drawn = drawn * levels(rng, extent, shards, -0.22, 0.18)
    return jnp.clip(drawn, -most, most).astype(kind)


def setup_inputs(seed: int = 0) -> dict:
    key_list = jax.random.split(jax.random.key(seed), 7)
    queries = draw_queries(jax.random.fold_in(key_list[6], 71), 0)
    key_vecs = draw_key_vecs(jax.random.fold_in(key_list[6], 71), 0)
    value_vecs = normal_values(key_list[2], (SEQ, HD), 1.0, 6.0, ((0, 512),))
    out_grad = normal_values(key_list[3], (SEQ, HEADS * HD), 1.0, 6.0, ((0, 512),))
    positions = draw_positions(jax.random.fold_in(key_list[6], 71), 0)
    documents = draw_documents(jax.random.fold_in(key_list[6], 71), 0)
    return {"queries": queries, "key_vecs": key_vecs, "value_vecs": value_vecs, "out_grad": out_grad, "positions": positions, "documents": documents}


NEG_BIG = -1e+30

def reference(queries, key_vecs, value_vecs, out_grad, positions, documents):
    seq_len = queries.shape[0]
    head_count = queries.shape[1] // HD
    inv_root = 1.0 / math.sqrt(HD)
    query_cube = queries.astype(jnp.float32).reshape(seq_len, head_count, HD)
    grad_cube = out_grad.astype(jnp.float32).reshape(seq_len, head_count, HD)
    key_full = key_vecs.astype(jnp.float32)
    value_full = value_vecs.astype(jnp.float32)
    block_len = 128
    block_count = seq_len // block_len

    def visit(running, block_index):
        key_acc, value_acc = running
        offset = (block_index * block_len).astype(jnp.int32)
        query_block = lax.dynamic_slice_in_dim(query_cube, offset, block_len, 0)
        grad_block = lax.dynamic_slice_in_dim(grad_cube, offset, block_len, 0)
        pos_query = lax.dynamic_slice_in_dim(positions, offset, block_len, 0)
        doc_query = lax.dynamic_slice_in_dim(documents, offset, block_len, 0)
        visible = (positions[None, :] <= pos_query[:, None]) & (documents[None, :] == doc_query[:, None])
        visible3 = visible[:, None, :]
        scores = jnp.where(visible3, jnp.einsum('thd,kd->thk', query_block, key_full) * inv_root, NEG_BIG)
        highest = lax.optimization_barrier(jnp.max(scores, axis=2))
        denoms = lax.optimization_barrier(jnp.sum(jnp.where(visible3, jnp.exp(scores - highest[:, :, None]), 0.0), axis=2))
        log_total = highest + jnp.log(denoms)
        weights = jnp.where(visible3, jnp.exp(scores - log_total[:, :, None]), 0.0)
        dprobs = jnp.einsum('thd,kd->thk', grad_block, value_full)
        row_dot = lax.optimization_barrier(jnp.sum(weights * dprobs, axis=2))
        dscores = lax.optimization_barrier((weights * (dprobs - row_dot[:, :, None])).astype(jnp.bfloat16)).astype(jnp.float32)
        weights_b = lax.optimization_barrier(weights.astype(jnp.bfloat16)).astype(jnp.float32)
        query_part = jnp.einsum('thk,kd->thd', dscores, key_full) * inv_root
        key_acc = key_acc + jnp.einsum('thk,thd->kd', dscores, query_block) * inv_root
        value_acc = value_acc + jnp.einsum('thk,thd->kd', weights_b, grad_block)
        return ((key_acc, value_acc), query_part)
    zero_rows = jnp.zeros((seq_len, HD), jnp.float32)
    (grad_keys, grad_values), query_parts = lax.scan(visit, (zero_rows, zero_rows), jnp.arange(block_count, dtype=jnp.int32))
    grad_queries = query_parts.reshape(seq_len, head_count * HD)
    return (grad_queries, grad_keys, grad_values)
```

```python
import functools
import math

import jax
import jax.numpy as jnp
from jax import lax
from jax.experimental import pallas as pl
from jax.experimental.pallas import tpu as pltpu
from jax.sharding import PartitionSpec as P

LOW = -1e30
FLOOR = -1e29
DOC_STEP = 8192.0
META = 8


def dot_rows(a, b):
    return lax.dot_general(a, b, (((1,), (1,)), ((), ())), preferred_element_type=jnp.float32)


def dot_plain(a, b):
    return lax.dot_general(a, b, (((1,), (0,)), ((), ())), preferred_element_type=jnp.float32)


def dot_cols(a, b):
    return lax.dot_general(a, b, (((0,), (0,)), ((), ())), preferred_element_type=jnp.float32)


def pack_kernel(pos_ref, doc_ref, q_ref, g_ref, k_ref, v_ref, qp_ref, kp_ref):
    run, hd = k_ref.shape
    heads = q_ref.shape[1] // hd
    n_q, n_k = qp_ref.shape[0], kp_ref.shape[0]
    rows = run * heads
    first = pos_ref[0] // run
    high, low = first // 16, first % 16
    row = lax.broadcasted_iota(jnp.int32, (META, hd), 0)
    lane = lax.broadcasted_iota(jnp.int32, (META, hd), 1)
    tok = lane % run
    docs = jnp.zeros((META, hd), jnp.int32)
    for t in range(run):
        docs = jnp.where(tok == t, doc_ref[t], docs)
    q_meta = jnp.where(row == 0, docs, jnp.where(row == 1, high, jnp.where(row == 2, low, 0)))
    half = hd // 2
    tok_here = jnp.where(lane >= half, row + META, row)
    docs = jnp.zeros((META, hd), jnp.int32)
    for t in range(run):
        docs = jnp.where(tok_here == t, doc_ref[t], docs)
    item = lane % half
    k_meta = jnp.where(item == 0, docs, jnp.where(item == 1, high, jnp.where(item == 2, low, 0)))
    q_meta = q_meta.astype(jnp.float32).astype(jnp.bfloat16)
    k_meta = k_meta.astype(jnp.float32).astype(jnp.bfloat16)
    for h in range(heads):
        q_h = q_ref[:, h * hd : (h + 1) * hd]
        g_h = g_ref[:, h * hd : (h + 1) * hd]
        for d in range(n_q):
            qp_ref[d, h * run : (h + 1) * run, :] = q_h
            qp_ref[d, rows + h * run : rows + (h + 1) * run, :] = g_h
    for d in range(n_q):
        qp_ref[d, 2 * rows : 2 * rows + META, :] = q_meta
    k, v = k_ref[...], v_ref[...]
    for d in range(n_k):
        kp_ref[d, 0:run, :] = k
        kp_ref[d, run : 2 * run, :] = v
        kp_ref[d, 2 * run : 2 * run + META, :] = k_meta


def key_codes(kp_ref, run):
    n_k, _, hd = kp_ref.shape
    meta = kp_ref[:, 2 * run : 2 * run + META, :].astype(jnp.float32).reshape(n_k * META, hd)
    src = lax.broadcasted_iota(jnp.int32, (hd, 2 * hd), 0)
    dst = lax.broadcasted_iota(jnp.int32, (hd, 2 * hd), 1)
    half = hd // 2
    item = src % half
    weight = jnp.where(
        item == 0, DOC_STEP, jnp.where(item == 1, run * 16.0, jnp.where(item == 2, run * 1.0, 0.0))
    )
    weight = jnp.where((src >= half) == (dst >= hd), weight, 0.0)
    codes = dot_plain(meta.astype(jnp.bfloat16), weight.astype(jnp.bfloat16))
    tok = lax.broadcasted_iota(jnp.int32, (n_k, META, hd), 1).astype(jnp.float32)
    lower = codes[:, :hd].reshape(n_k, META, hd) + tok
    upper = codes[:, hd:].reshape(n_k, META, hd) + (tok + META)
    return jnp.concatenate([lower, upper], axis=1).reshape(n_k * run, hd)


def query_codes(qp_ref, d, run):
    rows = (qp_ref.shape[1] - META) // 2
    meta = qp_ref[d, 2 * rows : 2 * rows + META, :].astype(jnp.float32)
    tok = (lax.broadcasted_iota(jnp.int32, (1, rows), 1) % run).astype(jnp.float32)
    base = meta[0:1] * DOC_STEP
    return base, base + meta[1:2] * (run * 16.0) + meta[2:3] * float(run) + tok


def stats_kernel(qp_ref, kp_ref, out_ref, code_ref, *, chunk):
    n_q, block, hd = qp_ref.shape
    n_k = kp_ref.shape[0]
    rows = (block - META) // 2
    run = (kp_ref.shape[1] - META) // 2
    scale = 1.0 / math.sqrt(hd)
    code_ref[...] = key_codes(kp_ref, run)
    per = chunk // run
    for d in range(0, n_q, 2):
        q = qp_ref[d : d + 2, 0:rows, :].reshape(2 * rows, hd)
        g = qp_ref[d : d + 2, rows : 2 * rows, :].reshape(2 * rows, hd)
        pairs = [query_codes(qp_ref, d + i, run) for i in range(2)]
        base = jnp.concatenate([p[0] for p in pairs], axis=1)
        top = jnp.concatenate([p[1] for p in pairs], axis=1)
        high = jnp.full((1, 2 * rows), FLOOR, jnp.float32)
        total = jnp.zeros((1, 2 * rows), jnp.float32)
        cross = jnp.zeros((1, 2 * rows), jnp.float32)
        for c in range(n_k // per):
            k = kp_ref[c * per : (c + 1) * per, 0:run, :].reshape(chunk, hd)
            v = kp_ref[c * per : (c + 1) * per, run : 2 * run, :].reshape(chunk, hd)
            code = code_ref[c * chunk : (c + 1) * chunk, :]
            code = jnp.concatenate([code] * (2 * rows // hd), axis=1)
            seen = (code <= top) & (code >= base)
            s = jnp.where(seen, dot_rows(k, q) * scale, LOW)
            dp = dot_rows(v, g)
            new = jnp.maximum(high, jnp.max(s, axis=0, keepdims=True))
            w = jnp.exp(s - new)
            keep = jnp.exp(high - new)
            total = total * keep + jnp.sum(w, axis=0, keepdims=True)
            cross = cross * keep + jnp.sum(w * dp, axis=0, keepdims=True)
            high = new
        some = total > 0.0
        safe = jnp.where(some, total, 1.0)
        log_total = jnp.where(some, high + jnp.log(safe), LOW)
        row_dot = jnp.where(some, cross / safe, 0.0)
        for i in range(2):
            for to in range(n_q):
                lo, hi = i * rows, (i + 1) * rows
                out_ref[to, d + i : d + i + 1, :] = log_total[:, lo:hi]
                out_ref[to, n_q + d + i : n_q + d + i + 1, :] = row_dot[:, lo:hi]


def grads_kernel(qp_ref, kp_ref, st_ref, gq_ref, gkv_ref, code_ref, log_ref, dot_ref, acc_ref, *, chunk):
    n_q, block, hd = qp_ref.shape
    n_k = kp_ref.shape[0]
    rows = (block - META) // 2
    run = (kp_ref.shape[1] - META) // 2
    scale = 1.0 / math.sqrt(hd)
    code_ref[...] = key_codes(kp_ref, run)
    logs = st_ref[:, 0:n_q, :]
    high = jnp.max(logs, axis=0)
    log_total = high + jnp.log(jnp.sum(jnp.exp(logs - high[None]), axis=0))
    log_ref[...] = log_total
    dot_ref[...] = jnp.sum(jnp.exp(logs - log_total[None]) * st_ref[:, n_q:, :], axis=0)
    per = chunk // run
    for d in range(0, n_q, 2):
        q = qp_ref[d : d + 2, 0:rows, :].reshape(2 * rows, hd)
        g = qp_ref[d : d + 2, rows : 2 * rows, :].reshape(2 * rows, hd)
        pairs = [query_codes(qp_ref, d + i, run) for i in range(2)]
        base = jnp.concatenate([p[0] for p in pairs], axis=1)
        top = jnp.concatenate([p[1] for p in pairs], axis=1)
        log_row = jnp.concatenate([log_ref[d + i : d + i + 1, :] for i in range(2)], axis=1)
        dot_row = jnp.concatenate([dot_ref[d + i : d + i + 1, :] for i in range(2)], axis=1)
        gq = jnp.zeros((2 * rows, hd), jnp.float32)
        for c in range(n_k // per):
            k = kp_ref[c * per : (c + 1) * per, 0:run, :].reshape(chunk, hd)
            v = kp_ref[c * per : (c + 1) * per, run : 2 * run, :].reshape(chunk, hd)
            code = code_ref[c * chunk : (c + 1) * chunk, :]
            code = jnp.concatenate([code] * (2 * rows // hd), axis=1)
            seen = (code <= top) & (code >= base)
            w = jnp.exp(jnp.where(seen, dot_rows(k, q) * scale, LOW) - log_row)
            ds = (w * (dot_rows(v, g) - dot_row)).astype(jnp.bfloat16)
            gq = gq + dot_cols(ds, k)
            gk = dot_plain(ds, q)
            gv = dot_plain(w.astype(jnp.bfloat16), g)
            at = pl.ds(c * chunk, chunk)
            if d == 0:
                acc_ref[0, at, :] = gk
                acc_ref[1, at, :] = gv
            else:
                acc_ref[0, at, :] += gk
                acc_ref[1, at, :] += gv
        gq_ref[d : d + 2] = (gq * scale).reshape(2, rows, hd).astype(gq_ref.dtype)
    gkv_ref[:, 0:run, :] = (acc_ref[0] * scale).reshape(n_k, run, hd).astype(gkv_ref.dtype)
    gkv_ref[:, run:, :] = acc_ref[1].reshape(n_k, run, hd).astype(gkv_ref.dtype)


def finish_kernel(gq_ref, gkv_ref, oq_ref, ok_ref, ov_ref):
    run, hd = ok_ref.shape
    gq = jnp.sum(gq_ref[...].astype(jnp.float32), axis=0)
    for h in range(oq_ref.shape[1] // hd):
        oq_ref[:, h * hd : (h + 1) * hd] = gq[h * run : (h + 1) * run, :]
    gkv = jnp.sum(gkv_ref[...].astype(jnp.float32), axis=0)
    ok_ref[...] = gkv[:run]
    ov_ref[...] = gkv[run:]


VMEM = pl.BlockSpec(memory_space=pltpu.VMEM)
SMEM = pl.BlockSpec(memory_space=pltpu.SMEM)


def call(kernel, in_specs, outs, scratch=()):
    return pl.pallas_call(
        kernel,
        in_specs=in_specs,
        out_specs=[VMEM] * len(outs),
        out_shape=outs,
        scratch_shapes=list(scratch),
        compiler_params=pltpu.CompilerParams(vmem_limit_bytes=48 * 1024 * 1024),
    )


def on_device(queries, key_vecs, value_vecs, out_grad, positions, documents):
    n_q, n_k = lax.axis_size("head"), lax.axis_size("ctx")
    run, hd = key_vecs.shape
    heads = queries.shape[1] // hd
    rows = run * heads
    bf, f32 = jnp.bfloat16, jnp.float32
    keys = n_k * run
    chunk = min(256, keys)
    struct = jax.ShapeDtypeStruct

    def swap(x, axis):
        return lax.all_to_all(x, axis, split_axis=0, concat_axis=0, tiled=True)

    qp, kp = call(
        pack_kernel,
        [SMEM, SMEM] + [VMEM] * 4,
        [struct((n_q, 2 * rows + META, hd), bf), struct((n_k, 2 * run + META, hd), bf)],
    )(positions, documents, queries, out_grad, key_vecs, value_vecs)
    kp = swap(kp, "ctx")
    qp = swap(qp, "head")
    (st,) = call(
        functools.partial(stats_kernel, chunk=chunk),
        [VMEM] * 2,
        [struct((n_q, 2 * n_q, rows), f32)],
        [pltpu.VMEM((keys, hd), f32)],
    )(qp, kp)
    st = swap(st, "head")
    gq, gkv = call(
        functools.partial(grads_kernel, chunk=chunk),
        [VMEM] * 3,
        [struct((n_q, rows, hd), f32), struct((n_k, 2 * run, hd), bf)],
        [
            pltpu.VMEM((keys, hd), f32),
            pltpu.VMEM((n_q, rows), f32),
            pltpu.VMEM((n_q, rows), f32),
            pltpu.VMEM((2, keys, hd), f32),
        ],
    )(qp, kp, st)
    gkv = swap(gkv, "ctx")
    gq = swap(gq, "head")
    return tuple(
        call(
            finish_kernel,
            [VMEM] * 2,
            [struct((run, heads * hd), f32), struct((run, hd), f32), struct((run, hd), f32)],
        )(gq, gkv)
    )


def solution(mesh):
    tok = P(("head", "ctx"))
    two = P(("head", "ctx"), None)
    return jax.shard_map(
        on_device,
        mesh=mesh,
        in_specs=(two, two, two, two, tok, tok),
        out_specs=(two, two, two),
        check_vma=False,
    )
```

```python
import functools
import math

import jax
import jax.numpy as jnp
from jax import lax
from jax.experimental import pallas as pl
from jax.experimental.pallas import tpu as pltpu
from jax.sharding import Mesh
from jax.sharding import PartitionSpec as P

GRANT = 60 * 1024 * 1024
LOW = -1e30
FLOOR = -1e29
DOC_STEP = 8192.0
META = 8


def dot_rows(a, b):
    return lax.dot_general(a, b, (((1,), (1,)), ((), ())), preferred_element_type=jnp.float32)


def dot_plain(a, b):
    return lax.dot_general(a, b, (((1,), (0,)), ((), ())), preferred_element_type=jnp.float32)


def dot_cols(a, b):
    return lax.dot_general(a, b, (((0,), (0,)), ((), ())), preferred_element_type=jnp.float32)


def pack_kernel(pos_any, doc_any, q_any, g_any, k_any, v_any, qp_ref, kp_ref, *scratch):
    bufs, sems = scratch[:6], scratch[6]
    hbm = (pos_any, doc_any, q_any, g_any, k_any, v_any)
    copies = [pltpu.make_async_copy(src, dst, sems.at[i]) for i, (src, dst) in enumerate(zip(hbm, bufs))]
    for copy in copies:
        copy.start()
    for copy in copies:
        copy.wait()
    pos_ref, doc_ref, q_ref, g_ref, k_ref, v_ref = bufs
    run, hd = k_ref.shape
    heads = q_ref.shape[1] // hd
    n_q, n_k = qp_ref.shape[0], kp_ref.shape[0]
    rows = run * heads
    first = pos_ref[0] // run
    high, low = first // 16, first % 16
    row = lax.broadcasted_iota(jnp.int32, (META, hd), 0)
    lane = lax.broadcasted_iota(jnp.int32, (META, hd), 1)
    tok = lane % run
    docs = jnp.zeros((META, hd), jnp.int32)
    for t in range(run):
        docs = jnp.where(tok == t, doc_ref[t], docs)
    q_meta = jnp.where(row == 0, docs, jnp.where(row == 1, high, jnp.where(row == 2, low, 0)))
    half = hd // 2
    tok_here = jnp.where(lane >= half, row + META, row)
    docs = jnp.zeros((META, hd), jnp.int32)
    for t in range(run):
        docs = jnp.where(tok_here == t, doc_ref[t], docs)
    item = lane % half
    k_meta = jnp.where(item == 0, docs, jnp.where(item == 1, high, jnp.where(item == 2, low, 0)))
    q_meta = q_meta.astype(jnp.float32).astype(jnp.bfloat16)
    k_meta = k_meta.astype(jnp.float32).astype(jnp.bfloat16)
    for h in range(heads):
        q_h = q_ref[:, h * hd : (h + 1) * hd]
        g_h = g_ref[:, h * hd : (h + 1) * hd]
        for d in range(n_q):
            qp_ref[d, h * run : (h + 1) * run, :] = q_h
            qp_ref[d, rows + h * run : rows + (h + 1) * run, :] = g_h
    for d in range(n_q):
        qp_ref[d, 2 * rows : 2 * rows + META, :] = q_meta
    k, v = k_ref[...], v_ref[...]
    for d in range(n_k):
        kp_ref[d, 0:run, :] = k
        kp_ref[d, run : 2 * run, :] = v
        kp_ref[d, 2 * run : 2 * run + META, :] = k_meta


def key_codes(kp_ref, run):
    n_k, _, hd = kp_ref.shape
    meta = kp_ref[:, 2 * run : 2 * run + META, :].astype(jnp.float32).reshape(n_k * META, hd)
    src = lax.broadcasted_iota(jnp.int32, (hd, 2 * hd), 0)
    dst = lax.broadcasted_iota(jnp.int32, (hd, 2 * hd), 1)
    half = hd // 2
    item = src % half
    weight = jnp.where(
        item == 0, DOC_STEP, jnp.where(item == 1, run * 16.0, jnp.where(item == 2, run * 1.0, 0.0))
    )
    weight = jnp.where((src >= half) == (dst >= hd), weight, 0.0)
    codes = dot_plain(meta.astype(jnp.bfloat16), weight.astype(jnp.bfloat16))
    tok = lax.broadcasted_iota(jnp.int32, (n_k, META, hd), 1).astype(jnp.float32)
    lower = codes[:, :hd].reshape(n_k, META, hd) + tok
    upper = codes[:, hd:].reshape(n_k, META, hd) + (tok + META)
    return jnp.concatenate([lower, upper], axis=1).reshape(n_k * run, hd)


def query_codes(qp_ref, d, run):
    rows = (qp_ref.shape[1] - META) // 2
    meta = qp_ref[d, 2 * rows : 2 * rows + META, :].astype(jnp.float32)
    tok = (lax.broadcasted_iota(jnp.int32, (1, rows), 1) % run).astype(jnp.float32)
    base = meta[0:1] * DOC_STEP
    return base, base + meta[1:2] * (run * 16.0) + meta[2:3] * float(run) + tok


def stats_kernel(side_ref, qa_ref, qb_ref, kp_ref, out_ref, code_ref, *, chunk):
    n_q, block, hd = qa_ref.shape
    n_k = kp_ref.shape[0]
    rows = (block - META) // 2
    run = (kp_ref.shape[1] - META) // 2
    scale = 1.0 / math.sqrt(hd)
    side = side_ref[0]
    code_ref[...] = key_codes(kp_ref, run)
    per = chunk // run
    for d in range(0, 2 * n_q, 2):
        qp_ref, at = (qa_ref, d) if d < n_q else (qb_ref, d - n_q)
        home = (side if d < n_q else 1 - side) * n_q + at
        q = qp_ref[at : at + 2, 0:rows, :].reshape(2 * rows, hd)
        g = qp_ref[at : at + 2, rows : 2 * rows, :].reshape(2 * rows, hd)
        pairs = [query_codes(qp_ref, at + i, run) for i in range(2)]
        base = jnp.concatenate([p[0] for p in pairs], axis=1)
        top = jnp.concatenate([p[1] for p in pairs], axis=1)
        high = jnp.full((1, 2 * rows), FLOOR, jnp.float32)
        total = jnp.zeros((1, 2 * rows), jnp.float32)
        cross = jnp.zeros((1, 2 * rows), jnp.float32)
        for c in range(n_k // per):
            k = kp_ref[c * per : (c + 1) * per, 0:run, :].reshape(chunk, hd)
            v = kp_ref[c * per : (c + 1) * per, run : 2 * run, :].reshape(chunk, hd)
            code = code_ref[c * chunk : (c + 1) * chunk, :]
            code = jnp.concatenate([code] * (2 * rows // hd), axis=1)
            seen = (code <= top) & (code >= base)
            s = jnp.where(seen, dot_rows(k, q) * scale, LOW)
            dp = dot_rows(v, g)
            new = jnp.maximum(high, jnp.max(s, axis=0, keepdims=True))
            w = jnp.exp(s - new)
            keep = jnp.exp(high - new)
            total = total * keep + jnp.sum(w, axis=0, keepdims=True)
            cross = cross * keep + jnp.sum(w * dp, axis=0, keepdims=True)
            high = new
        some = total > 0.0
        safe = jnp.where(some, total, 1.0)
        log_total = jnp.where(some, high + jnp.log(safe), LOW)
        row_dot = jnp.where(some, cross / safe, 0.0)
        for i in range(2):
            for to in range(out_ref.shape[0]):
                lo, hi = i * rows, (i + 1) * rows
                out_ref[to, pl.ds(home + i, 1), :] = log_total[:, lo:hi]
                out_ref[to, pl.ds(2 * n_q + home + i, 1), :] = row_dot[:, lo:hi]


def grads_kernel(
    side_ref, qa_ref, qb_ref, kp_ref, st_ref, own_ref, oth_ref, gkv_ref, code_ref, log_ref, dot_ref, acc_ref, *, chunk
):
    n_q, block, hd = qa_ref.shape
    n_k = kp_ref.shape[0]
    rows = (block - META) // 2
    run = (kp_ref.shape[1] - META) // 2
    scale = 1.0 / math.sqrt(hd)
    side = side_ref[0]
    code_ref[...] = key_codes(kp_ref, run)
    logs = st_ref[:, 0 : 2 * n_q, :]
    high = jnp.max(logs, axis=0)
    log_total = high + jnp.log(jnp.sum(jnp.exp(logs - high[None]), axis=0))
    log_ref[...] = log_total
    dot_ref[...] = jnp.sum(jnp.exp(logs - log_total[None]) * st_ref[:, 2 * n_q :, :], axis=0)
    per = chunk // run
    for d in range(0, 2 * n_q, 2):
        qp_ref, at, gq_ref = (qa_ref, d, own_ref) if d < n_q else (qb_ref, d - n_q, oth_ref)
        home = (side if d < n_q else 1 - side) * n_q + at
        q = qp_ref[at : at + 2, 0:rows, :].reshape(2 * rows, hd)
        g = qp_ref[at : at + 2, rows : 2 * rows, :].reshape(2 * rows, hd)
        pairs = [query_codes(qp_ref, at + i, run) for i in range(2)]
        base = jnp.concatenate([p[0] for p in pairs], axis=1)
        top = jnp.concatenate([p[1] for p in pairs], axis=1)
        log_row = jnp.concatenate([log_ref[pl.ds(home + i, 1), :] for i in range(2)], axis=1)
        dot_row = jnp.concatenate([dot_ref[pl.ds(home + i, 1), :] for i in range(2)], axis=1)
        gq = jnp.zeros((2 * rows, hd), jnp.float32)
        for c in range(n_k // per):
            k = kp_ref[c * per : (c + 1) * per, 0:run, :].reshape(chunk, hd)
            v = kp_ref[c * per : (c + 1) * per, run : 2 * run, :].reshape(chunk, hd)
            code = code_ref[c * chunk : (c + 1) * chunk, :]
            code = jnp.concatenate([code] * (2 * rows // hd), axis=1)
            seen = (code <= top) & (code >= base)
            w = jnp.exp(jnp.where(seen, dot_rows(k, q) * scale, LOW) - log_row)
            ds = (w * (dot_rows(v, g) - dot_row)).astype(jnp.bfloat16)
            gq = gq + dot_cols(ds, k)
            gk = dot_plain(ds, q)
            gv = dot_plain(w.astype(jnp.bfloat16), g)
            where = pl.ds(c * chunk, chunk)
            if d == 0:
                acc_ref[0, where, :] = gk
                acc_ref[1, where, :] = gv
            else:
                acc_ref[0, where, :] += gk
                acc_ref[1, where, :] += gv
        gq_ref[at : at + 2] = (gq * scale).reshape(2, rows, hd).astype(gq_ref.dtype)
    gkv_ref[:, 0:run, :] = (acc_ref[0] * scale).reshape(n_k, run, hd).astype(gkv_ref.dtype)
    gkv_ref[:, run:, :] = acc_ref[1].reshape(n_k, run, hd).astype(gkv_ref.dtype)


def finish_kernel(gq_ref, gkv_ref, oq_ref, ok_ref, ov_ref):
    run, hd = ok_ref.shape
    gq = jnp.sum(gq_ref[...].astype(jnp.float32), axis=0)
    for h in range(oq_ref.shape[1] // hd):
        oq_ref[:, h * hd : (h + 1) * hd] = gq[h * run : (h + 1) * run, :]
    gkv = jnp.sum(gkv_ref[...].astype(jnp.float32), axis=0)
    ok_ref[...] = gkv[:run]
    ov_ref[...] = gkv[run:]


VMEM = pl.BlockSpec(memory_space=pltpu.VMEM)
SMEM = pl.BlockSpec(memory_space=pltpu.SMEM)
HBM = pl.BlockSpec(memory_space=pltpu.HBM)


def call(kernel, in_specs, outs, scratch=(), grant=48 * 1024 * 1024):
    return pl.pallas_call(
        kernel,
        in_specs=in_specs,
        out_specs=[VMEM] * len(outs),
        out_shape=outs,
        scratch_shapes=list(scratch),
        compiler_params=pltpu.CompilerParams(vmem_limit_bytes=grant),
    )


def on_device(queries, key_vecs, value_vecs, out_grad, positions, documents):
    n_q, n_k, sides = lax.axis_size("head"), lax.axis_size("far"), lax.axis_size("core")
    run, hd = key_vecs.shape
    heads = queries.shape[1] // hd
    rows = run * heads
    bf, f32 = jnp.bfloat16, jnp.float32
    keys = n_k * run
    chunk = min(256, keys)
    struct = jax.ShapeDtypeStruct

    def swap(x, axis):
        return lax.all_to_all(x, axis, split_axis=0, concat_axis=0, tiled=True)

    def other(x):
        return lax.ppermute(x, "core", [(0, 1), (1, 0)])

    side = lax.axis_index("core").astype(jnp.int32).reshape(1)
    args = (positions, documents, queries, out_grad, key_vecs, value_vecs)
    qp, kp = call(
        pack_kernel,
        [HBM] * 6,
        [struct((n_q, 2 * rows + META, hd), bf), struct((n_k, 2 * run + META, hd), bf)],
        [(pltpu.SMEM if a.ndim == 1 else pltpu.VMEM)(a.shape, a.dtype) for a in args]
        + [pltpu.SemaphoreType.DMA((6,))],
        grant=GRANT,
    )(*args)
    qa = swap(qp, "head")
    qb = other(qa)
    kp = swap(kp, "far")
    (st,) = call(
        functools.partial(stats_kernel, chunk=chunk),
        [SMEM] + [VMEM] * 3,
        [struct((sides * n_q, 2 * sides * n_q, rows), f32)],
        [pltpu.VMEM((keys, hd), f32)],
    )(side, qa, qb, kp)
    st = swap(st, ("head", "core"))
    own, oth, gkv = call(
        functools.partial(grads_kernel, chunk=chunk),
        [SMEM] + [VMEM] * 4,
        [struct((n_q, rows, hd), f32), struct((n_q, rows, hd), bf), struct((n_k, 2 * run, hd), bf)],
        [
            pltpu.VMEM((keys, hd), f32),
            pltpu.VMEM((sides * n_q, rows), f32),
            pltpu.VMEM((sides * n_q, rows), f32),
            pltpu.VMEM((2, keys, hd), f32),
        ],
    )(side, qa, qb, kp, st)
    oth = other(oth)
    gkv = swap(gkv, "far")
    gq = (own + oth.astype(f32)).astype(bf)
    gq = swap(gq, "head")
    return tuple(
        call(
            finish_kernel,
            [VMEM] * 2,
            [struct((run, heads * hd), f32), struct((run, hd), f32), struct((run, hd), f32)],
        )(gq, gkv)
    )


def solution(mesh):
    n_head, n_ctx = mesh.devices.shape
    fine = Mesh(mesh.devices.reshape(n_head, n_ctx // 2, 2), ("head", "far", "core"))
    tok = P(("head", "far", "core"))
    two = P(("head", "far", "core"), None)
    return jax.shard_map(
        on_device,
        mesh=fine,
        in_specs=(two, two, two, two, tok, tok),
        out_specs=(two, two, two),
        check_vma=False,
    )
```

```python
import functools
import math

import jax
import jax.numpy as jnp
from jax import lax
from jax.experimental import pallas as pl
from jax.experimental.pallas import tpu as pltpu
from jax.sharding import Mesh
from jax.sharding import PartitionSpec as P

GRANT = 60 * 1024 * 1024
LOW = -1e30
FLOOR = -1e29
DOC_STEP = 8192.0
META = 8


def dot_rows(a, b):
    return lax.dot_general(a, b, (((1,), (1,)), ((), ())), preferred_element_type=jnp.float32)


def dot_plain(a, b):
    return lax.dot_general(a, b, (((1,), (0,)), ((), ())), preferred_element_type=jnp.float32)


def dot_cols(a, b):
    return lax.dot_general(a, b, (((0,), (0,)), ((), ())), preferred_element_type=jnp.float32)


def pack_kernel(pos_any, doc_any, q_any, g_any, k_any, v_any, qp_ref, kp_ref, *scratch):
    bufs, sems = scratch[:6], scratch[6]
    hbm = (pos_any, doc_any, q_any, g_any, k_any, v_any)
    copies = [pltpu.make_async_copy(src, dst, sems.at[i]) for i, (src, dst) in enumerate(zip(hbm, bufs))]
    for copy in copies:
        copy.start()
    for copy in copies:
        copy.wait()
    pos_ref, doc_ref, q_ref, g_ref, k_ref, v_ref = bufs
    run, hd = k_ref.shape
    heads = q_ref.shape[1] // hd
    n_k = kp_ref.shape[0]
    rows = run * heads
    first = pos_ref[0] // run
    high, low = first // 16, first % 16
    row = lax.broadcasted_iota(jnp.int32, (META, hd), 0)
    lane = lax.broadcasted_iota(jnp.int32, (META, hd), 1)
    tok = lane % run
    docs = jnp.zeros((META, hd), jnp.int32)
    for t in range(run):
        docs = jnp.where(tok == t, doc_ref[t], docs)
    q_meta = jnp.where(row == 0, docs, jnp.where(row == 1, high, jnp.where(row == 2, low, 0)))
    half = hd // 2
    tok_here = jnp.where(lane >= half, row + META, row)
    docs = jnp.zeros((META, hd), jnp.int32)
    for t in range(run):
        docs = jnp.where(tok_here == t, doc_ref[t], docs)
    item = lane % half
    k_meta = jnp.where(item == 0, docs, jnp.where(item == 1, high, jnp.where(item == 2, low, 0)))
    q_meta = q_meta.astype(jnp.float32).astype(jnp.bfloat16)
    k_meta = k_meta.astype(jnp.float32).astype(jnp.bfloat16)
    for h in range(heads):
        q_h = q_ref[:, h * hd : (h + 1) * hd]
        g_h = g_ref[:, h * hd : (h + 1) * hd]
        qp_ref[0, h * run : (h + 1) * run, :] = q_h
        qp_ref[0, rows + h * run : rows + (h + 1) * run, :] = g_h
    qp_ref[0, 2 * rows : 2 * rows + META, :] = q_meta
    k, v = k_ref[...], v_ref[...]
    for d in range(n_k):
        kp_ref[d, 0:run, :] = k
        kp_ref[d, run : 2 * run, :] = v
        kp_ref[d, 2 * run : 2 * run + META, :] = k_meta


def key_codes(kp_ref, run):
    n_k, _, hd = kp_ref.shape
    meta = kp_ref[:, 2 * run : 2 * run + META, :].astype(jnp.float32).reshape(n_k * META, hd)
    src = lax.broadcasted_iota(jnp.int32, (hd, 2 * hd), 0)
    dst = lax.broadcasted_iota(jnp.int32, (hd, 2 * hd), 1)
    half = hd // 2
    item = src % half
    weight = jnp.where(
        item == 0, DOC_STEP, jnp.where(item == 1, run * 16.0, jnp.where(item == 2, run * 1.0, 0.0))
    )
    weight = jnp.where((src >= half) == (dst >= hd), weight, 0.0)
    codes = dot_plain(meta.astype(jnp.bfloat16), weight.astype(jnp.bfloat16))
    tok = lax.broadcasted_iota(jnp.int32, (n_k, META, hd), 1).astype(jnp.float32)
    lower = codes[:, :hd].reshape(n_k, META, hd) + tok
    upper = codes[:, hd:].reshape(n_k, META, hd) + (tok + META)
    return jnp.concatenate([lower, upper], axis=1).reshape(n_k * run, hd)


def query_codes(qp_ref, d, run):
    rows = (qp_ref.shape[1] - META) // 2
    meta = qp_ref[d, 2 * rows : 2 * rows + META, :].astype(jnp.float32)
    tok = (lax.broadcasted_iota(jnp.int32, (1, rows), 1) % run).astype(jnp.float32)
    base = meta[0:1] * DOC_STEP
    return base, base + meta[1:2] * (run * 16.0) + meta[2:3] * float(run) + tok


def home_of(place_ref, part, at, n_x):
    place = place_ref[0]
    side, y, x = place % 2, (place // 2) % 2, place // 4
    far_y, far_side = part % 2, part // 2
    y = 1 - y if far_y else y
    side = 1 - side if far_side else side
    return (lax.rem(x + n_x - at, n_x) * 2 + y) * 2 + side


def tiles(place_ref, parts, log_ref=None):
    n_x = parts[0].shape[0]
    for p, ref in enumerate(parts):
        for at in range(0, n_x, 2):
            yield p, ref, at, [home_of(place_ref, p, at + i, n_x) for i in range(2)]


def stats_kernel(place_ref, *refs, chunk):
    parts, kp_ref, out_ref, code_ref = refs[:4], refs[4], refs[5], refs[6]
    n_x, block, hd = parts[0].shape
    n_dev = out_ref.shape[0]
    n_k = kp_ref.shape[0]
    rows = (block - META) // 2
    run = (kp_ref.shape[1] - META) // 2
    scale = 1.0 / math.sqrt(hd)
    code_ref[...] = key_codes(kp_ref, run)
    per = chunk // run
    for _, qp_ref, at, homes in tiles(place_ref, parts):
        q = qp_ref[at : at + 2, 0:rows, :].reshape(2 * rows, hd)
        g = qp_ref[at : at + 2, rows : 2 * rows, :].reshape(2 * rows, hd)
        pairs = [query_codes(qp_ref, at + i, run) for i in range(2)]
        base = jnp.concatenate([p[0] for p in pairs], axis=1)
        top = jnp.concatenate([p[1] for p in pairs], axis=1)
        high = jnp.full((1, 2 * rows), FLOOR, jnp.float32)
        total = jnp.zeros((1, 2 * rows), jnp.float32)
        cross = jnp.zeros((1, 2 * rows), jnp.float32)
        for c in range(n_k // per):
            k = kp_ref[c * per : (c + 1) * per, 0:run, :].reshape(chunk, hd)
            v = kp_ref[c * per : (c + 1) * per, run : 2 * run, :].reshape(chunk, hd)
            code = code_ref[c * chunk : (c + 1) * chunk, :]
            code = jnp.concatenate([code] * (2 * rows // hd), axis=1)
            seen = (code <= top) & (code >= base)
            s = jnp.where(seen, dot_rows(k, q) * scale, LOW)
            dp = dot_rows(v, g)
            new = jnp.maximum(high, jnp.max(s, axis=0, keepdims=True))
            w = jnp.exp(s - new)
            keep = jnp.exp(high - new)
            total = total * keep + jnp.sum(w, axis=0, keepdims=True)
            cross = cross * keep + jnp.sum(w * dp, axis=0, keepdims=True)
            high = new
        some = total > 0.0
        safe = jnp.where(some, total, 1.0)
        log_total = jnp.where(some, high + jnp.log(safe), LOW)
        row_dot = jnp.where(some, cross / safe, 0.0)
        for i, home in enumerate(homes):
            lo, hi = i * rows, (i + 1) * rows
            for to in range(n_dev):
                out_ref[to, pl.ds(home, 1), :] = log_total[:, lo:hi]
                out_ref[to, pl.ds(n_dev + home, 1), :] = row_dot[:, lo:hi]


def grads_kernel(place_ref, *refs, chunk):
    parts, kp_ref, st_ref = refs[:4], refs[4], refs[5]
    own_ref, near_ref, far_ref, gkv_ref = refs[6:10]
    code_ref, log_ref, dot_ref, acc_ref = refs[10:]
    n_x, block, hd = parts[0].shape
    n_dev = st_ref.shape[0]
    n_k = kp_ref.shape[0]
    rows = (block - META) // 2
    run = (kp_ref.shape[1] - META) // 2
    scale = 1.0 / math.sqrt(hd)
    code_ref[...] = key_codes(kp_ref, run)
    logs = st_ref[:, 0:n_dev, :]
    high = jnp.max(logs, axis=0)
    log_total = high + jnp.log(jnp.sum(jnp.exp(logs - high[None]), axis=0))
    log_ref[...] = log_total
    dot_ref[...] = jnp.sum(jnp.exp(logs - log_total[None]) * st_ref[:, n_dev:, :], axis=0)
    per = chunk // run
    first = True
    for p, qp_ref, at, homes in tiles(place_ref, parts):
        gq_ref, to = ((own_ref, at), (near_ref, at), (far_ref, at), (far_ref, n_x + at))[p]
        q = qp_ref[at : at + 2, 0:rows, :].reshape(2 * rows, hd)
        g = qp_ref[at : at + 2, rows : 2 * rows, :].reshape(2 * rows, hd)
        pairs = [query_codes(qp_ref, at + i, run) for i in range(2)]
        base = jnp.concatenate([p[0] for p in pairs], axis=1)
        top = jnp.concatenate([p[1] for p in pairs], axis=1)
        log_row = jnp.concatenate([log_ref[pl.ds(home, 1), :] for home in homes], axis=1)
        dot_row = jnp.concatenate([dot_ref[pl.ds(home, 1), :] for home in homes], axis=1)
        gq = jnp.zeros((2 * rows, hd), jnp.float32)
        for c in range(n_k // per):
            k = kp_ref[c * per : (c + 1) * per, 0:run, :].reshape(chunk, hd)
            v = kp_ref[c * per : (c + 1) * per, run : 2 * run, :].reshape(chunk, hd)
            code = code_ref[c * chunk : (c + 1) * chunk, :]
            code = jnp.concatenate([code] * (2 * rows // hd), axis=1)
            seen = (code <= top) & (code >= base)
            w = jnp.exp(jnp.where(seen, dot_rows(k, q) * scale, LOW) - log_row)
            ds = (w * (dot_rows(v, g) - dot_row)).astype(jnp.bfloat16)
            gq = gq + dot_cols(ds, k)
            gk = dot_plain(ds, q)
            gv = dot_plain(w.astype(jnp.bfloat16), g)
            where = pl.ds(c * chunk, chunk)
            if first:
                acc_ref[0, where, :] = gk
                acc_ref[1, where, :] = gv
            else:
                acc_ref[0, where, :] += gk
                acc_ref[1, where, :] += gv
        first = False
        gq_ref[to : to + 2] = (gq * scale).reshape(2, rows, hd).astype(gq_ref.dtype)
    gkv_ref[:, 0:run, :] = (acc_ref[0] * scale).reshape(n_k, run, hd).astype(gkv_ref.dtype)
    gkv_ref[:, run:, :] = acc_ref[1].reshape(n_k, run, hd).astype(gkv_ref.dtype)


def finish_kernel(*refs):
    pieces, gkv_ref, (oq_ref, ok_ref, ov_ref) = refs[:-4], refs[-4], refs[-3:]
    run, hd = ok_ref.shape
    gq = pieces[0][...]
    for piece in pieces[1:]:
        gq = gq + piece[...].astype(jnp.float32)
    for h in range(oq_ref.shape[1] // hd):
        oq_ref[:, h * hd : (h + 1) * hd] = gq[h * run : (h + 1) * run, :]
    gkv = jnp.sum(gkv_ref[...].astype(jnp.float32), axis=0)
    ok_ref[...] = gkv[:run]
    ov_ref[...] = gkv[run:]


VMEM = pl.BlockSpec(memory_space=pltpu.VMEM)
SMEM = pl.BlockSpec(memory_space=pltpu.SMEM)
HBM = pl.BlockSpec(memory_space=pltpu.HBM)


def call(kernel, in_specs, outs, scratch=(), grant=48 * 1024 * 1024):
    return pl.pallas_call(
        kernel,
        in_specs=in_specs,
        out_specs=[VMEM] * len(outs),
        out_shape=outs,
        scratch_shapes=list(scratch),
        compiler_params=pltpu.CompilerParams(vmem_limit_bytes=grant),
    )


def on_device(queries, key_vecs, value_vecs, out_grad, positions, documents):
    n_x, n_k = lax.axis_size("x"), lax.axis_size("far")
    n_dev = 4 * n_x
    run, hd = key_vecs.shape
    heads = queries.shape[1] // hd
    rows = run * heads
    bf, f32 = jnp.bfloat16, jnp.float32
    keys = n_k * run
    chunk = min(256, keys)
    struct = jax.ShapeDtypeStruct

    def swap(x, axis):
        return lax.all_to_all(x, axis, split_axis=0, concat_axis=0, tiled=True)

    def shift(x, axis, by):
        n = lax.axis_size(axis)
        return lax.ppermute(x, axis, [(i, (i + by) % n) for i in range(n)])

    place = lax.axis_index(("x", "near", "core")).astype(jnp.int32).reshape(1)
    args = (positions, documents, queries, out_grad, key_vecs, value_vecs)
    qp, kp = call(
        pack_kernel,
        [HBM] * 6,
        [struct((1, 2 * rows + META, hd), bf), struct((n_k, 2 * run + META, hd), bf)],
        [(pltpu.SMEM if a.ndim == 1 else pltpu.VMEM)(a.shape, a.dtype) for a in args]
        + [pltpu.SemaphoreType.DMA((6,))],
        grant=GRANT,
    )(*args)
    kp = swap(kp, "far")
    q_here = jnp.concatenate([qp] + [shift(qp, "x", d) for d in range(1, n_x)], axis=0)
    q_near = shift(q_here, "near", 1)
    parts = (q_here, q_near, shift(q_here, "core", 1), shift(q_near, "core", 1))
    (st,) = call(
        functools.partial(stats_kernel, chunk=chunk),
        [SMEM] + [VMEM] * 5,
        [struct((n_dev, 2 * n_dev, rows), f32)],
        [pltpu.VMEM((keys, hd), f32)],
    )(place, *parts, kp)
    st = swap(st, ("x", "near", "core"))
    own, near, far, gkv = call(
        functools.partial(grads_kernel, chunk=chunk),
        [SMEM] + [VMEM] * 6,
        [
            struct((n_x, rows, hd), f32),
            struct((n_x, rows, hd), f32),
            struct((2 * n_x, rows, hd), bf),
            struct((n_k, 2 * run, hd), bf),
        ],
        [
            pltpu.VMEM((keys, hd), f32),
            pltpu.VMEM((n_dev, rows), f32),
            pltpu.VMEM((n_dev, rows), f32),
            pltpu.VMEM((2, keys, hd), f32),
        ],
    )(place, *parts, kp, st)
    gkv = swap(gkv, "far")
    far = shift(far, "core", 1).astype(f32)
    near = shift((near + far[n_x:]).astype(bf), "near", 1).astype(f32)
    own = own + far[:n_x] + near
    pieces = [own[0]] + [shift(own[d].astype(bf), "x", -d) for d in range(1, n_x)]
    return tuple(
        call(
            finish_kernel,
            [VMEM] * (n_x + 1),
            [struct((run, heads * hd), f32), struct((run, hd), f32), struct((run, hd), f32)],
        )(*pieces, gkv)
    )


def solution(mesh):
    n_head, n_ctx = mesh.devices.shape
    fine = Mesh(mesh.devices.reshape(n_head // 2, 2, n_ctx // 2, 2), ("x", "near", "far", "core"))
    every = ("x", "near", "far", "core")
    tok, two = P(every), P(every, None)
    return jax.shard_map(
        on_device,
        mesh=fine,
        in_specs=(two, two, two, two, tok, tok),
        out_specs=(two, two, two),
        check_vma=False,
    )
```

```python
import math

import jax
import jax.numpy as jnp
from jax import lax
from jax.experimental import pallas as pl
from jax.experimental.pallas import tpu as pltpu
from jax.sharding import Mesh
from jax.sharding import PartitionSpec as P

GRANT = 60 * 1024 * 1024
LOW = -1e30
FLOOR = -1e29
DOC_STEP = 8192.0
META = 8


def dot_rows(a, b):
    return lax.dot_general(a, b, (((1,), (1,)), ((), ())), preferred_element_type=jnp.float32)


def dot_plain(a, b):
    return lax.dot_general(a, b, (((1,), (0,)), ((), ())), preferred_element_type=jnp.float32)


def dot_cols(a, b):
    return lax.dot_general(a, b, (((0,), (0,)), ((), ())), preferred_element_type=jnp.float32)


def pack_kernel(pos_any, doc_any, q_any, g_any, k_any, v_any, qp_ref, kp_ref, *scratch):
    bufs, sems = scratch[:6], scratch[6]
    hbm = (pos_any, doc_any, q_any, g_any, k_any, v_any)
    copies = [pltpu.make_async_copy(src, dst, sems.at[i]) for i, (src, dst) in enumerate(zip(hbm, bufs))]
    for copy in copies:
        copy.start()
    for copy in copies:
        copy.wait()
    pos_ref, doc_ref, q_ref, g_ref, k_ref, v_ref = bufs
    run, hd = k_ref.shape
    heads = q_ref.shape[1] // hd
    n_q, n_k = qp_ref.shape[0], kp_ref.shape[0]
    rows = run * heads
    first = pos_ref[0] // run
    high, low = first // 16, first % 16
    row = lax.broadcasted_iota(jnp.int32, (META, hd), 0)
    lane = lax.broadcasted_iota(jnp.int32, (META, hd), 1)
    tok = lane % run
    docs = jnp.zeros((META, hd), jnp.int32)
    for t in range(run):
        docs = jnp.where(tok == t, doc_ref[t], docs)
    q_meta = jnp.where(row == 0, docs, jnp.where(row == 1, high, jnp.where(row == 2, low, 0)))
    half = hd // 2
    tok_here = jnp.where(lane >= half, row + META, row)
    docs = jnp.zeros((META, hd), jnp.int32)
    for t in range(run):
        docs = jnp.where(tok_here == t, doc_ref[t], docs)
    item = lane % half
    k_meta = jnp.where(item == 0, docs, jnp.where(item == 1, high, jnp.where(item == 2, low, 0)))
    q_meta = q_meta.astype(jnp.float32).astype(jnp.bfloat16)
    k_meta = k_meta.astype(jnp.float32).astype(jnp.bfloat16)
    for h in range(heads):
        q_h = q_ref[:, h * hd : (h + 1) * hd]
        g_h = g_ref[:, h * hd : (h + 1) * hd]
        for d in range(n_q):
            qp_ref[d, h * run : (h + 1) * run, :] = q_h
            qp_ref[d, rows + h * run : rows + (h + 1) * run, :] = g_h
    for d in range(n_q):
        qp_ref[d, 2 * rows : 2 * rows + META, :] = q_meta
    k, v = k_ref[...], v_ref[...]
    for d in range(n_k):
        kp_ref[d, 0:run, :] = k
        kp_ref[d, run : 2 * run, :] = v
        kp_ref[d, 2 * run : 2 * run + META, :] = k_meta


def key_codes(kp_ref, run):
    n_k, _, hd = kp_ref.shape
    meta = kp_ref[:, 2 * run : 2 * run + META, :].astype(jnp.float32).reshape(n_k * META, hd)
    src = lax.broadcasted_iota(jnp.int32, (hd, 2 * hd), 0)
    dst = lax.broadcasted_iota(jnp.int32, (hd, 2 * hd), 1)
    half = hd // 2
    item = src % half
    weight = jnp.where(
        item == 0, DOC_STEP, jnp.where(item == 1, run * 16.0, jnp.where(item == 2, run * 1.0, 0.0))
    )
    weight = jnp.where((src >= half) == (dst >= hd), weight, 0.0)
    codes = dot_plain(meta.astype(jnp.bfloat16), weight.astype(jnp.bfloat16))
    tok = lax.broadcasted_iota(jnp.int32, (n_k, META, hd), 1).astype(jnp.float32)
    lower = codes[:, :hd].reshape(n_k, META, hd) + tok
    upper = codes[:, hd:].reshape(n_k, META, hd) + (tok + META)
    return jnp.concatenate([lower, upper], axis=1).reshape(n_k * run, hd)


def query_codes(qp_ref, d, run):
    rows = (qp_ref.shape[1] - META) // 2
    meta = qp_ref[d, 2 * rows : 2 * rows + META, :].astype(jnp.float32)
    tok = (lax.broadcasted_iota(jnp.int32, (1, rows), 1) % run).astype(jnp.float32)
    base = meta[0:1] * DOC_STEP
    return base, base + meta[1:2] * (run * 16.0) + meta[2:3] * float(run) + tok


def blocks(qa_ref, qb_ref, side):
    n_q = qa_ref.shape[0]
    for d in range(0, 2 * n_q, 2):
        ref, at = (qa_ref, d) if d < n_q else (qb_ref, d - n_q)
        yield ref, at, d, (side if d < n_q else 1 - side) * n_q + at


def stats_kernel(side_ref, qa_ref, qb_ref, kp_ref, out_ref, e_ref, dp_ref, top_ref, code_ref):
    n_q, block, hd = qa_ref.shape
    n_k = kp_ref.shape[0]
    rows = (block - META) // 2
    run = (kp_ref.shape[1] - META) // 2
    scale = 1.0 / math.sqrt(hd)
    code_ref[...] = key_codes(kp_ref, run)
    k = kp_ref[:, 0:run, :].reshape(n_k * run, hd)
    v = kp_ref[:, run : 2 * run, :].reshape(n_k * run, hd)
    for qp_ref, at, d, home in blocks(qa_ref, qb_ref, side_ref[0]):
        q = qp_ref[at : at + 2, 0:rows, :].reshape(2 * rows, hd)
        g = qp_ref[at : at + 2, rows : 2 * rows, :].reshape(2 * rows, hd)
        pairs = [query_codes(qp_ref, at + i, run) for i in range(2)]
        base = jnp.concatenate([p[0] for p in pairs], axis=1)
        top = jnp.concatenate([p[1] for p in pairs], axis=1)
        code = jnp.concatenate([code_ref[...]] * (2 * rows // hd), axis=1)
        seen = (code <= top) & (code >= base)
        s = jnp.where(seen, dot_rows(k, q) * scale, LOW)
        dp = dot_rows(v, g)
        high = jnp.maximum(jnp.max(s, axis=0, keepdims=True), FLOOR)
        e = jnp.exp(s - high)
        cols = slice(d * rows, (d + 2) * rows)
        e_ref[:, cols] = e
        dp_ref[:, cols] = dp
        total = jnp.sum(e, axis=0, keepdims=True)
        cross = jnp.sum(e * dp, axis=0, keepdims=True)
        some = total > 0.0
        safe = jnp.where(some, total, 1.0)
        log_total = jnp.where(some, high + jnp.log(safe), LOW)
        row_dot = jnp.where(some, cross / safe, 0.0)
        for i in range(2):
            lo, hi = i * rows, (i + 1) * rows
            top_ref[d + i : d + i + 1, :] = high[:, lo:hi]
            for to in range(out_ref.shape[0]):
                out_ref[to, pl.ds(home + i, 1), :] = log_total[:, lo:hi]
                out_ref[to, pl.ds(2 * n_q + home + i, 1), :] = row_dot[:, lo:hi]


def keys_kernel(side_ref, qa_ref, qb_ref, st_ref, e_ref, dp_ref, top_ref, gkv_ref, ds_ref, log_ref, dot_ref):
    n_q, block, hd = qa_ref.shape
    n_k, twice, _ = gkv_ref.shape
    run = twice // 2
    rows = (block - META) // 2
    scale = 1.0 / math.sqrt(hd)
    logs = st_ref[:, 0 : 2 * n_q, :]
    high = jnp.max(logs, axis=0)
    log_total = high + jnp.log(jnp.sum(jnp.exp(logs - high[None]), axis=0))
    log_ref[...] = log_total
    dot_ref[...] = jnp.sum(jnp.exp(logs - log_total[None]) * st_ref[:, 2 * n_q :, :], axis=0)
    gk = jnp.zeros((n_k * run, hd), jnp.float32)
    gv = jnp.zeros((n_k * run, hd), jnp.float32)
    for qp_ref, at, d, home in blocks(qa_ref, qb_ref, side_ref[0]):
        q = qp_ref[at : at + 2, 0:rows, :].reshape(2 * rows, hd)
        g = qp_ref[at : at + 2, rows : 2 * rows, :].reshape(2 * rows, hd)
        factor = jnp.concatenate(
            [jnp.exp(top_ref[d + i : d + i + 1, :] - log_ref[pl.ds(home + i, 1), :]) for i in range(2)], axis=1
        )
        dot_row = jnp.concatenate([dot_ref[pl.ds(home + i, 1), :] for i in range(2)], axis=1)
        cols = slice(d * rows, (d + 2) * rows)
        w = e_ref[:, cols] * factor
        ds = (w * (dp_ref[:, cols] - dot_row)).astype(jnp.bfloat16)
        ds_ref[:, cols] = ds
        gk = gk + dot_plain(ds, q)
        gv = gv + dot_plain(w.astype(jnp.bfloat16), g)
    gkv_ref[:, 0:run, :] = (gk * scale).reshape(n_k, run, hd).astype(gkv_ref.dtype)
    gkv_ref[:, run:, :] = gv.reshape(n_k, run, hd).astype(gkv_ref.dtype)


def queries_kernel(kp_ref, ds_ref, own_ref, oth_ref):
    n_q, rows, hd = own_ref.shape
    n_k = kp_ref.shape[0]
    run = (kp_ref.shape[1] - META) // 2
    scale = 1.0 / math.sqrt(hd)
    k = kp_ref[:, 0:run, :].reshape(n_k * run, hd)
    for d in list(range(n_q, 2 * n_q, 2)) + list(range(0, n_q, 2)):
        ref, at = (own_ref, d) if d < n_q else (oth_ref, d - n_q)
        gq = dot_cols(ds_ref[:, d * rows : (d + 2) * rows], k) * scale
        ref[at : at + 2] = gq.reshape(2, rows, hd).astype(ref.dtype)


def finish_kernel(gq_ref, gkv_ref, oq_ref, ok_ref, ov_ref):
    run, hd = ok_ref.shape
    gq = jnp.sum(gq_ref[...].astype(jnp.float32), axis=0)
    for h in range(oq_ref.shape[1] // hd):
        oq_ref[:, h * hd : (h + 1) * hd] = gq[h * run : (h + 1) * run, :]
    gkv = jnp.sum(gkv_ref[...].astype(jnp.float32), axis=0)
    ok_ref[...] = gkv[:run]
    ov_ref[...] = gkv[run:]


VMEM = pl.BlockSpec(memory_space=pltpu.VMEM)
SMEM = pl.BlockSpec(memory_space=pltpu.SMEM)
HBM = pl.BlockSpec(memory_space=pltpu.HBM)


def call(kernel, in_specs, outs, scratch=(), grant=16 * 1024 * 1024, cost=0):
    return pl.pallas_call(
        kernel,
        in_specs=in_specs,
        out_specs=[VMEM] * len(outs),
        out_shape=outs,
        scratch_shapes=list(scratch),
        cost_estimate=pl.CostEstimate(flops=cost, bytes_accessed=0, transcendentals=0) if cost else None,
        compiler_params=pltpu.CompilerParams(vmem_limit_bytes=grant),
    )


def on_device(queries, key_vecs, value_vecs, out_grad, positions, documents):
    n_q, n_k, sides = lax.axis_size("head"), lax.axis_size("far"), lax.axis_size("core")
    run, hd = key_vecs.shape
    heads = queries.shape[1] // hd
    rows = run * heads
    bf, f32 = jnp.bfloat16, jnp.float32
    keys = n_k * run
    struct = jax.ShapeDtypeStruct

    def swap(x, axis):
        return lax.all_to_all(x, axis, split_axis=0, concat_axis=0, tiled=True)

    def other(x):
        return lax.ppermute(x, "core", [(0, 1), (1, 0)])

    side = lax.axis_index("core").astype(jnp.int32).reshape(1)
    args = (positions, documents, queries, out_grad, key_vecs, value_vecs)
    qp, kp = call(
        pack_kernel,
        [HBM] * 6,
        [struct((n_q, 2 * rows + META, hd), bf), struct((n_k, 2 * run + META, hd), bf)],
        [(pltpu.SMEM if a.ndim == 1 else pltpu.VMEM)(a.shape, a.dtype) for a in args]
        + [pltpu.SemaphoreType.DMA((6,))],
        grant=GRANT,
    )(*args)
    qa = swap(qp, "head")
    qb = other(qa)
    kp = swap(kp, "far")
    full = struct((keys, sides * n_q * rows), f32)
    line = struct((sides * n_q, rows), f32)
    st, e, dp, top = call(
        stats_kernel,
        [SMEM] + [VMEM] * 3,
        [struct((sides * n_q, 2 * sides * n_q, rows), f32), full, full, line],
        [pltpu.VMEM((keys, hd), f32)],
    )(side, qa, qb, kp)
    st = swap(st, ("head", "core"))
    gkv, ds = call(
        keys_kernel,
        [SMEM] + [VMEM] * 6,
        [struct((n_k, 2 * run, hd), bf), struct(full.shape, bf)],
        [pltpu.VMEM(line.shape, f32), pltpu.VMEM(line.shape, f32)],
    )(side, qa, qb, st, e, dp, top)
    own, oth = call(
        queries_kernel,
        [VMEM] * 2,
        [struct((n_q, rows, hd), f32), struct((n_q, rows, hd), bf)],
        cost=2 * keys * sides * n_q * rows * hd,
    )(kp, ds)
    oth = other(oth)
    gkv = swap(gkv, "far")
    gq = (own + oth.astype(f32)).astype(bf)
    gq = swap(gq, "head")
    return tuple(
        call(
            finish_kernel,
            [VMEM] * 2,
            [struct((run, heads * hd), f32), struct((run, hd), f32), struct((run, hd), f32)],
        )(gq, gkv)
    )


def solution(mesh):
    n_head, n_ctx = mesh.devices.shape
    fine = Mesh(mesh.devices.reshape(n_head, n_ctx // 2, 2), ("head", "far", "core"))
    tok = P(("head", "far", "core"))
    two = P(("head", "far", "core"), None)
    return jax.shard_map(
        on_device,
        mesh=fine,
        in_specs=(two, two, two, two, tok, tok),
        out_specs=(two, two, two),
        check_vma=False,
    )
```

```python
import math

import jax
import jax.numpy as jnp
from jax import lax
from jax.experimental import pallas as pl
from jax.experimental.pallas import tpu as pltpu
from jax.sharding import Mesh
from jax.sharding import PartitionSpec as P

GRANT = 60 * 1024 * 1024
LOW = -1e30
FLOOR = -1e29
DOC_STEP = 8192.0
META = 8


def dot_rows(a, b):
    return lax.dot_general(a, b, (((1,), (1,)), ((), ())), preferred_element_type=jnp.float32)


def dot_plain(a, b):
    return lax.dot_general(a, b, (((1,), (0,)), ((), ())), preferred_element_type=jnp.float32)


def dot_cols(a, b):
    return lax.dot_general(a, b, (((0,), (0,)), ((), ())), preferred_element_type=jnp.float32)


def pack_kernel(pos_any, doc_any, q_any, g_any, k_any, v_any, qp_ref, kp_ref, *scratch):
    bufs, sems = scratch[:6], scratch[6]
    hbm = (pos_any, doc_any, q_any, g_any, k_any, v_any)
    copies = [pltpu.make_async_copy(src, dst, sems.at[i]) for i, (src, dst) in enumerate(zip(hbm, bufs))]
    for copy in copies:
        copy.start()
    for copy in copies:
        copy.wait()
    pos_ref, doc_ref, q_ref, g_ref, k_ref, v_ref = bufs
    run, hd = k_ref.shape
    heads = q_ref.shape[1] // hd
    n_q, n_k = qp_ref.shape[0], kp_ref.shape[0]
    rows = run * heads
    first = pos_ref[0] // run
    high, low = first // 16, first % 16
    row = lax.broadcasted_iota(jnp.int32, (META, hd), 0)
    lane = lax.broadcasted_iota(jnp.int32, (META, hd), 1)
    tok = lane % run
    docs = jnp.zeros((META, hd), jnp.int32)
    for t in range(run):
        docs = jnp.where(tok == t, doc_ref[t], docs)
    q_meta = jnp.where(row == 0, docs, jnp.where(row == 1, high, jnp.where(row == 2, low, 0)))
    half = hd // 2
    tok_here = jnp.where(lane >= half, row + META, row)
    docs = jnp.zeros((META, hd), jnp.int32)
    for t in range(run):
        docs = jnp.where(tok_here == t, doc_ref[t], docs)
    item = lane % half
    k_meta = jnp.where(item == 0, docs, jnp.where(item == 1, high, jnp.where(item == 2, low, 0)))
    q_meta = q_meta.astype(jnp.float32).astype(jnp.bfloat16)
    k_meta = k_meta.astype(jnp.float32).astype(jnp.bfloat16)
    for h in range(heads):
        q_h = q_ref[:, h * hd : (h + 1) * hd]
        g_h = g_ref[:, h * hd : (h + 1) * hd]
        for d in range(n_q):
            qp_ref[d, h * run : (h + 1) * run, :] = q_h
            qp_ref[d, rows + h * run : rows + (h + 1) * run, :] = g_h
    for d in range(n_q):
        qp_ref[d, 2 * rows : 2 * rows + META, :] = q_meta
    k, v = k_ref[...], v_ref[...]
    for d in range(n_k):
        kp_ref[d, 0:run, :] = k
        kp_ref[d, run : 2 * run, :] = v
        kp_ref[d, 2 * run : 2 * run + META, :] = k_meta


def key_codes(kp_ref, run):
    n_k, _, hd = kp_ref.shape
    meta = kp_ref[:, 2 * run : 2 * run + META, :].astype(jnp.float32).reshape(n_k * META, hd)
    src = lax.broadcasted_iota(jnp.int32, (hd, 2 * hd), 0)
    dst = lax.broadcasted_iota(jnp.int32, (hd, 2 * hd), 1)
    half = hd // 2
    item = src % half
    weight = jnp.where(
        item == 0, DOC_STEP, jnp.where(item == 1, run * 16.0, jnp.where(item == 2, run * 1.0, 0.0))
    )
    weight = jnp.where((src >= half) == (dst >= hd), weight, 0.0)
    codes = dot_plain(meta.astype(jnp.bfloat16), weight.astype(jnp.bfloat16))
    tok = lax.broadcasted_iota(jnp.int32, (n_k, META, hd), 1).astype(jnp.float32)
    lower = codes[:, :hd].reshape(n_k, META, hd) + tok
    upper = codes[:, hd:].reshape(n_k, META, hd) + (tok + META)
    return jnp.concatenate([lower, upper], axis=1).reshape(n_k * run, hd)


def query_codes(qp_ref, d, run):
    rows = (qp_ref.shape[1] - META) // 2
    meta = qp_ref[d, 2 * rows : 2 * rows + META, :].astype(jnp.float32)
    tok = (lax.broadcasted_iota(jnp.int32, (1, rows), 1) % run).astype(jnp.float32)
    base = meta[0:1] * DOC_STEP
    return base, base + meta[1:2] * (run * 16.0) + meta[2:3] * float(run) + tok


def blocks(qa_ref, qb_ref, side):
    n_q = qa_ref.shape[0]
    for d in range(0, 2 * n_q, 2):
        ref, at = (qa_ref, d) if d < n_q else (qb_ref, d - n_q)
        yield ref, at, d, (side if d < n_q else 1 - side) * n_q + at


def stats_kernel(side_ref, qa_ref, qb_ref, kp_ref, out_ref, e_ref, dp_ref, top_ref, code_ref):
    n_q, block, hd = qa_ref.shape
    n_k = kp_ref.shape[0]
    rows = (block - META) // 2
    run = (kp_ref.shape[1] - META) // 2
    scale = 1.0 / math.sqrt(hd)
    code_ref[...] = key_codes(kp_ref, run)
    k = kp_ref[:, 0:run, :].reshape(n_k * run, hd)
    v = kp_ref[:, run : 2 * run, :].reshape(n_k * run, hd)
    for qp_ref, at, d, home in blocks(qa_ref, qb_ref, side_ref[0]):
        q = qp_ref[at : at + 2, 0:rows, :].reshape(2 * rows, hd)
        g = qp_ref[at : at + 2, rows : 2 * rows, :].reshape(2 * rows, hd)
        pairs = [query_codes(qp_ref, at + i, run) for i in range(2)]
        base = jnp.concatenate([p[0] for p in pairs], axis=1)
        top = jnp.concatenate([p[1] for p in pairs], axis=1)
        code = jnp.concatenate([code_ref[...]] * (2 * rows // hd), axis=1)
        seen = (code <= top) & (code >= base)
        s = jnp.where(seen, dot_rows(k, q) * scale, LOW)
        dp = dot_rows(v, g)
        high = jnp.maximum(jnp.max(s, axis=0, keepdims=True), FLOOR)
        e = jnp.exp(s - high)
        cols = slice(d * rows, (d + 2) * rows)
        e_ref[:, cols] = e
        dp_ref[:, cols] = dp
        total = jnp.sum(e, axis=0, keepdims=True)
        cross = jnp.sum(e * dp, axis=0, keepdims=True)
        some = total > 0.0
        safe = jnp.where(some, total, 1.0)
        log_total = jnp.where(some, high + jnp.log(safe), LOW)
        row_dot = jnp.where(some, cross / safe, 0.0)
        for i in range(2):
            lo, hi = i * rows, (i + 1) * rows
            top_ref[d + i : d + i + 1, :] = high[:, lo:hi]
            for to in range(out_ref.shape[0]):
                out_ref[to, pl.ds(home + i, 1), :] = log_total[:, lo:hi]
                out_ref[to, pl.ds(2 * n_q + home + i, 1), :] = row_dot[:, lo:hi]


def keys_kernel(side_ref, qa_ref, qb_ref, st_ref, e_ref, dp_ref, top_ref, gkv_ref, ds_ref, log_ref, dot_ref):
    n_q, block, hd = qa_ref.shape
    n_k, twice, _ = gkv_ref.shape
    run = twice // 2
    rows = (block - META) // 2
    scale = 1.0 / math.sqrt(hd)
    logs = st_ref[:, 0 : 2 * n_q, :]
    high = jnp.max(logs, axis=0)
    log_total = high + jnp.log(jnp.sum(jnp.exp(logs - high[None]), axis=0))
    log_ref[...] = log_total
    dot_ref[...] = jnp.sum(jnp.exp(logs - log_total[None]) * st_ref[:, 2 * n_q :, :], axis=0)
    gk = jnp.zeros((n_k * run, hd), jnp.float32)
    gv = jnp.zeros((n_k * run, hd), jnp.float32)
    for qp_ref, at, d, home in blocks(qa_ref, qb_ref, side_ref[0]):
        q = qp_ref[at : at + 2, 0:rows, :].reshape(2 * rows, hd)
        g = qp_ref[at : at + 2, rows : 2 * rows, :].reshape(2 * rows, hd)
        factor = jnp.concatenate(
            [jnp.exp(top_ref[d + i : d + i + 1, :] - log_ref[pl.ds(home + i, 1), :]) for i in range(2)], axis=1
        )
        dot_row = jnp.concatenate([dot_ref[pl.ds(home + i, 1), :] for i in range(2)], axis=1)
        cols = slice(d * rows, (d + 2) * rows)
        w = e_ref[:, cols] * factor
        ds = (w * (dp_ref[:, cols] - dot_row)).astype(jnp.bfloat16)
        ds_ref[:, cols] = ds
        gk = gk + dot_plain(ds, q)
        gv = gv + dot_plain(w.astype(jnp.bfloat16), g)
    gkv_ref[:, 0:run, :] = (gk * scale).reshape(n_k, run, hd).astype(gkv_ref.dtype)
    gkv_ref[:, run:, :] = gv.reshape(n_k, run, hd).astype(gkv_ref.dtype)


def queries_kernel(kp_ref, ds_ref, own_ref, oth_ref):
    n_q, rows, hd = own_ref.shape
    n_k = kp_ref.shape[0]
    run = (kp_ref.shape[1] - META) // 2
    scale = 1.0 / math.sqrt(hd)
    k = kp_ref[:, 0:run, :].reshape(n_k * run, hd)
    for d in list(range(n_q, 2 * n_q, 2)) + list(range(0, n_q, 2)):
        ref, at = (own_ref, d) if d < n_q else (oth_ref, d - n_q)
        gq = dot_cols(ds_ref[:, d * rows : (d + 2) * rows], k) * scale
        ref[at : at + 2] = gq.reshape(2, rows, hd).astype(ref.dtype)


def finish_kernel(gq_ref, gkv_ref, oq_ref, ok_ref, ov_ref):
    run, hd = ok_ref.shape
    gq = jnp.sum(gq_ref[...].astype(jnp.float32), axis=0)
    for h in range(oq_ref.shape[1] // hd):
        oq_ref[:, h * hd : (h + 1) * hd] = gq[h * run : (h + 1) * run, :]
    gkv = jnp.sum(gkv_ref[...].astype(jnp.float32), axis=0)
    ok_ref[...] = gkv[:run]
    ov_ref[...] = gkv[run:]


VMEM = pl.BlockSpec(memory_space=pltpu.VMEM)
SMEM = pl.BlockSpec(memory_space=pltpu.SMEM)
HBM = pl.BlockSpec(memory_space=pltpu.HBM)


def call(kernel, in_specs, outs, scratch=(), grant=16 * 1024 * 1024, cost=0):
    return pl.pallas_call(
        kernel,
        in_specs=in_specs,
        out_specs=[VMEM] * len(outs),
        out_shape=outs,
        scratch_shapes=list(scratch),
        cost_estimate=pl.CostEstimate(flops=cost, bytes_accessed=0, transcendentals=0) if cost else None,
        compiler_params=pltpu.CompilerParams(vmem_limit_bytes=grant),
    )


def on_device(queries, key_vecs, value_vecs, out_grad, positions, documents):
    n_q, n_k, sides = lax.axis_size("head"), lax.axis_size("far"), lax.axis_size("core")
    run, hd = key_vecs.shape
    heads = queries.shape[1] // hd
    rows = run * heads
    bf, f32 = jnp.bfloat16, jnp.float32
    keys = n_k * run
    struct = jax.ShapeDtypeStruct

    def swap(x, axis):
        return lax.all_to_all(x, axis, split_axis=0, concat_axis=0, tiled=True)

    def other(x):
        return lax.ppermute(x, "core", [(0, 1), (1, 0)])

    side = lax.axis_index("core").astype(jnp.int32).reshape(1)
    args = (positions, documents, queries, out_grad, key_vecs, value_vecs)
    qp, kp = call(
        pack_kernel,
        [HBM] * 6,
        [struct((n_q, 2 * rows + META, hd), bf), struct((n_k, 2 * run + META, hd), bf)],
        [(pltpu.SMEM if a.ndim == 1 else pltpu.VMEM)(a.shape, a.dtype) for a in args]
        + [pltpu.SemaphoreType.DMA((6,))],
        grant=GRANT,
    )(*args)
    qa = swap(qp, "head")
    qb = other(qa)
    kp = swap(kp, "far")
    full = struct((keys, sides * n_q * rows), f32)
    line = struct((sides * n_q, rows), f32)
    st, e, dp, top = call(
        stats_kernel,
        [SMEM] + [VMEM] * 3,
        [struct((sides * n_q, 2 * sides * n_q, rows), f32), full, full, line],
        [pltpu.VMEM((keys, hd), f32)],
    )(side, qa, qb, kp)
    st = swap(st, ("head", "core"))
    gkv, ds = call(
        keys_kernel,
        [SMEM] + [VMEM] * 6,
        [struct((n_k, 2 * run, hd), bf), struct(full.shape, bf)],
        [pltpu.VMEM(line.shape, f32), pltpu.VMEM(line.shape, f32)],
    )(side, qa, qb, st, e, dp, top)
    own, oth = call(
        queries_kernel,
        [VMEM] * 2,
        [struct((n_q, rows, hd), f32), struct((n_q, rows, hd), bf)],
        cost=2 * keys * sides * n_q * rows * hd,
    )(kp, ds)
    gkv = swap(gkv, "far")
    both = lax.all_gather(oth, "core", axis=0, tiled=False)
    oth = jnp.where(side == 0, both[1], both[0])
    gq = (own + oth.astype(f32)).astype(bf)
    gq, gkv = lax.optimization_barrier((gq, gkv))
    gq = swap(gq, "head")
    return tuple(
        call(
            finish_kernel,
            [VMEM] * 2,
            [struct((run, heads * hd), f32), struct((run, hd), f32), struct((run, hd), f32)],
        )(gq, gkv)
    )


def solution(mesh):
    n_head, n_ctx = mesh.devices.shape
    fine = Mesh(mesh.devices.reshape(n_head, n_ctx // 2, 2), ("head", "far", "core"))
    tok = P(("head", "far", "core"))
    two = P(("head", "far", "core"), None)
    return jax.shard_map(
        on_device,
        mesh=fine,
        in_specs=(two, two, two, two, tok, tok),
        out_specs=(two, two, two),
        check_vma=False,
    )
```

```python
import math

import jax
import jax.numpy as jnp
from jax import lax
from jax.experimental import pallas as pl
from jax.experimental.pallas import tpu as pltpu
from jax.sharding import Mesh
from jax.sharding import PartitionSpec as P

GRANT = 60 * 1024 * 1024
LOW = -1e30
FLOOR = -1e29
DOC_STEP = 8192.0
META = 8


def dot_rows(a, b):
    return lax.dot_general(a, b, (((1,), (1,)), ((), ())), preferred_element_type=jnp.float32)


def dot_plain(a, b):
    return lax.dot_general(a, b, (((1,), (0,)), ((), ())), preferred_element_type=jnp.float32)


def dot_cols(a, b):
    return lax.dot_general(a, b, (((0,), (0,)), ((), ())), preferred_element_type=jnp.float32)


def pack_kernel(pos_any, doc_any, q_any, g_any, k_any, v_any, qp_ref, kp_ref, *scratch):
    bufs, sems = scratch[:6], scratch[6]
    hbm = (pos_any, doc_any, q_any, g_any, k_any, v_any)
    copies = [pltpu.make_async_copy(src, dst, sems.at[i]) for i, (src, dst) in enumerate(zip(hbm, bufs))]
    for copy in copies:
        copy.start()
    for copy in copies:
        copy.wait()
    pos_ref, doc_ref, q_ref, g_ref, k_ref, v_ref = bufs
    run, hd = k_ref.shape
    heads = q_ref.shape[1] // hd
    n_q, n_k = qp_ref.shape[0], kp_ref.shape[0]
    rows = run * heads
    first = pos_ref[0] // run
    high, low = first // 16, first % 16
    row = lax.broadcasted_iota(jnp.int32, (META, hd), 0)
    lane = lax.broadcasted_iota(jnp.int32, (META, hd), 1)
    tok = lane % run
    docs = jnp.zeros((META, hd), jnp.int32)
    for t in range(run):
        docs = jnp.where(tok == t, doc_ref[t], docs)
    q_meta = jnp.where(row == 0, docs, jnp.where(row == 1, high, jnp.where(row == 2, low, 0)))
    half = hd // 2
    tok_here = jnp.where(lane >= half, row + META, row)
    docs = jnp.zeros((META, hd), jnp.int32)
    for t in range(run):
        docs = jnp.where(tok_here == t, doc_ref[t], docs)
    item = lane % half
    k_meta = jnp.where(item == 0, docs, jnp.where(item == 1, high, jnp.where(item == 2, low, 0)))
    q_meta = q_meta.astype(jnp.float32).astype(jnp.bfloat16)
    k_meta = k_meta.astype(jnp.float32).astype(jnp.bfloat16)
    for h in range(heads):
        q_h = q_ref[:, h * hd : (h + 1) * hd]
        g_h = g_ref[:, h * hd : (h + 1) * hd]
        for d in range(n_q):
            qp_ref[d, h * run : (h + 1) * run, :] = q_h
            qp_ref[d, rows + h * run : rows + (h + 1) * run, :] = g_h
    for d in range(n_q):
        qp_ref[d, 2 * rows : 2 * rows + META, :] = q_meta
    k, v = k_ref[...], v_ref[...]
    for d in range(n_k):
        kp_ref[d, 0:run, :] = k
        kp_ref[d, run : 2 * run, :] = v
        kp_ref[d, 2 * run : 2 * run + META, :] = k_meta


def key_codes(kp_ref, run):
    n_k, _, hd = kp_ref.shape
    meta = kp_ref[:, 2 * run : 2 * run + META, :].astype(jnp.float32).reshape(n_k * META, hd)
    src = lax.broadcasted_iota(jnp.int32, (hd, 2 * hd), 0)
    dst = lax.broadcasted_iota(jnp.int32, (hd, 2 * hd), 1)
    half = hd // 2
    item = src % half
    weight = jnp.where(
        item == 0, DOC_STEP, jnp.where(item == 1, run * 16.0, jnp.where(item == 2, run * 1.0, 0.0))
    )
    weight = jnp.where((src >= half) == (dst >= hd), weight, 0.0)
    codes = dot_plain(meta.astype(jnp.bfloat16), weight.astype(jnp.bfloat16))
    tok = lax.broadcasted_iota(jnp.int32, (n_k, META, hd), 1).astype(jnp.float32)
    lower = codes[:, :hd].reshape(n_k, META, hd) + tok
    upper = codes[:, hd:].reshape(n_k, META, hd) + (tok + META)
    return jnp.concatenate([lower, upper], axis=1).reshape(n_k * run, hd)


def query_codes(qp_ref, d, run):
    rows = (qp_ref.shape[1] - META) // 2
    meta = qp_ref[d, 2 * rows : 2 * rows + META, :].astype(jnp.float32)
    tok = (lax.broadcasted_iota(jnp.int32, (1, rows), 1) % run).astype(jnp.float32)
    base = meta[0:1] * DOC_STEP
    return base, base + meta[1:2] * (run * 16.0) + meta[2:3] * float(run) + tok


def blocks(qa_ref, qb_ref, side):
    n_q = qa_ref.shape[0]
    for d in range(0, 2 * n_q, 2):
        ref, at = (qa_ref, d) if d < n_q else (qb_ref, d - n_q)
        yield ref, at, d, (side if d < n_q else 1 - side) * n_q + at


def stats_kernel(side_ref, qa_ref, qb_ref, kp_ref, out_ref, e_ref, dp_ref, top_ref, code_ref):
    n_q, block, hd = qa_ref.shape
    n_k = kp_ref.shape[0]
    rows = (block - META) // 2
    run = (kp_ref.shape[1] - META) // 2
    scale = 1.0 / math.sqrt(hd)
    code_ref[...] = key_codes(kp_ref, run)
    k = kp_ref[:, 0:run, :].reshape(n_k * run, hd)
    v = kp_ref[:, run : 2 * run, :].reshape(n_k * run, hd)
    for qp_ref, at, d, home in blocks(qa_ref, qb_ref, side_ref[0]):
        q = qp_ref[at : at + 2, 0:rows, :].reshape(2 * rows, hd)
        g = qp_ref[at : at + 2, rows : 2 * rows, :].reshape(2 * rows, hd)
        pairs = [query_codes(qp_ref, at + i, run) for i in range(2)]
        base = jnp.concatenate([p[0] for p in pairs], axis=1)
        top = jnp.concatenate([p[1] for p in pairs], axis=1)
        code = jnp.concatenate([code_ref[...]] * (2 * rows // hd), axis=1)
        seen = (code <= top) & (code >= base)
        s = jnp.where(seen, dot_rows(k, q) * scale, LOW)
        dp = dot_rows(v, g)
        high = jnp.maximum(jnp.max(s, axis=0, keepdims=True), FLOOR)
        e = jnp.exp(s - high)
        cols = slice(d * rows, (d + 2) * rows)
        e_ref[:, cols] = e
        dp_ref[:, cols] = dp
        total = jnp.sum(e, axis=0, keepdims=True)
        cross = jnp.sum(e * dp, axis=0, keepdims=True)
        some = total > 0.0
        safe = jnp.where(some, total, 1.0)
        log_total = jnp.where(some, high + jnp.log(safe), LOW)
        row_dot = jnp.where(some, cross / safe, 0.0)
        for i in range(2):
            lo, hi = i * rows, (i + 1) * rows
            top_ref[d + i : d + i + 1, :] = high[:, lo:hi]
            for to in range(out_ref.shape[0]):
                out_ref[to, pl.ds(home + i, 1), :] = log_total[:, lo:hi]
                out_ref[to, pl.ds(2 * n_q + home + i, 1), :] = row_dot[:, lo:hi]


def keys_kernel(side_ref, qa_ref, qb_ref, st_ref, e_ref, dp_ref, top_ref, gkv_ref, ds_ref, log_ref, dot_ref):
    n_q, block, hd = qa_ref.shape
    n_k, twice, _ = gkv_ref.shape
    run = twice // 2
    rows = (block - META) // 2
    scale = 1.0 / math.sqrt(hd)
    logs = st_ref[:, 0 : 2 * n_q, :]
    high = jnp.max(logs, axis=0)
    log_total = high + jnp.log(jnp.sum(jnp.exp(logs - high[None]), axis=0))
    log_ref[...] = log_total
    dot_ref[...] = jnp.sum(jnp.exp(logs - log_total[None]) * st_ref[:, 2 * n_q :, :], axis=0)
    gk = jnp.zeros((n_k * run, hd), jnp.float32)
    gv = jnp.zeros((n_k * run, hd), jnp.float32)
    for qp_ref, at, d, home in blocks(qa_ref, qb_ref, side_ref[0]):
        q = qp_ref[at : at + 2, 0:rows, :].reshape(2 * rows, hd)
        g = qp_ref[at : at + 2, rows : 2 * rows, :].reshape(2 * rows, hd)
        factor = jnp.concatenate(
            [jnp.exp(top_ref[d + i : d + i + 1, :] - log_ref[pl.ds(home + i, 1), :]) for i in range(2)], axis=1
        )
        dot_row = jnp.concatenate([dot_ref[pl.ds(home + i, 1), :] for i in range(2)], axis=1)
        cols = slice(d * rows, (d + 2) * rows)
        w = e_ref[:, cols] * factor
        ds = (w * (dp_ref[:, cols] - dot_row)).astype(jnp.bfloat16)
        ds_ref[:, cols] = ds
        gk = gk + dot_plain(ds, q)
        gv = gv + dot_plain(w.astype(jnp.bfloat16), g)
    gkv_ref[:, 0:run, :] = (gk * scale).reshape(n_k, run, hd).astype(gkv_ref.dtype)
    gkv_ref[:, run:, :] = gv.reshape(n_k, run, hd).astype(gkv_ref.dtype)


def queries_kernel(kp_ref, ds_ref, own_ref, oth_ref):
    n_q, rows, hd = own_ref.shape
    n_k = kp_ref.shape[0]
    run = (kp_ref.shape[1] - META) // 2
    scale = 1.0 / math.sqrt(hd)
    k = kp_ref[:, 0:run, :].reshape(n_k * run, hd)
    for d in list(range(n_q, 2 * n_q, 2)) + list(range(0, n_q, 2)):
        ref, at = (own_ref, d) if d < n_q else (oth_ref, d - n_q)
        gq = dot_cols(ds_ref[:, d * rows : (d + 2) * rows], k) * scale
        ref[at : at + 2] = gq.reshape(2, rows, hd).astype(ref.dtype)


def finish_kernel(gq_ref, gkv_ref, oq_ref, ok_ref, ov_ref):
    run, hd = ok_ref.shape
    gq = jnp.sum(gq_ref[...].astype(jnp.float32), axis=0)
    for h in range(oq_ref.shape[1] // hd):
        oq_ref[:, h * hd : (h + 1) * hd] = gq[h * run : (h + 1) * run, :]
    gkv = jnp.sum(gkv_ref[...].astype(jnp.float32), axis=0)
    ok_ref[...] = gkv[:run]
    ov_ref[...] = gkv[run:]


VMEM = pl.BlockSpec(memory_space=pltpu.VMEM)
SMEM = pl.BlockSpec(memory_space=pltpu.SMEM)
HBM = pl.BlockSpec(memory_space=pltpu.HBM)


def call(kernel, in_specs, outs, scratch=(), grant=16 * 1024 * 1024, cost=0):
    return pl.pallas_call(
        kernel,
        in_specs=in_specs,
        out_specs=[VMEM] * len(outs),
        out_shape=outs,
        scratch_shapes=list(scratch),
        cost_estimate=pl.CostEstimate(flops=cost, bytes_accessed=0, transcendentals=0) if cost else None,
        compiler_params=pltpu.CompilerParams(vmem_limit_bytes=grant),
    )


def on_device(queries, key_vecs, value_vecs, out_grad, positions, documents):
    n_q, n_k, sides = lax.axis_size("head"), lax.axis_size("far"), lax.axis_size("core")
    run, hd = key_vecs.shape
    heads = queries.shape[1] // hd
    rows = run * heads
    bf, f32 = jnp.bfloat16, jnp.float32
    keys = n_k * run
    struct = jax.ShapeDtypeStruct

    def swap(x, axis):
        return lax.all_to_all(x, axis, split_axis=0, concat_axis=0, tiled=True)

    def other(x):
        return lax.ppermute(x, "core", [(0, 1), (1, 0)])

    side = lax.axis_index("core").astype(jnp.int32).reshape(1)
    args = (positions, documents, queries, out_grad, key_vecs, value_vecs)
    qp, kp = call(
        pack_kernel,
        [HBM] * 6,
        [struct((n_q, 2 * rows + META, hd), bf), struct((n_k, 2 * run + META, hd), bf)],
        [(pltpu.SMEM if a.ndim == 1 else pltpu.VMEM)(a.shape, a.dtype) for a in args]
        + [pltpu.SemaphoreType.DMA((6,))],
        grant=GRANT,
    )(*args)
    qa = swap(qp, "head")
    qb = other(qa)
    kp = swap(kp, "far")
    full = struct((keys, sides * n_q * rows), f32)
    line = struct((sides * n_q, rows), f32)
    st, e, dp, top = call(
        stats_kernel,
        [SMEM] + [VMEM] * 3,
        [struct((n_q, 2 * sides * n_q, rows), f32), full, full, line],
        [pltpu.VMEM((keys, hd), f32)],
    )(side, qa, qb, kp)
    st = lax.all_gather(swap(st, "head"), "core", axis=0, tiled=True)
    gkv, ds = call(
        keys_kernel,
        [SMEM] + [VMEM] * 6,
        [struct((n_k, 2 * run, hd), bf), struct(full.shape, bf)],
        [pltpu.VMEM(line.shape, f32), pltpu.VMEM(line.shape, f32)],
    )(side, qa, qb, st, e, dp, top)
    own, oth = call(
        queries_kernel,
        [VMEM] * 2,
        [struct((n_q, rows, hd), f32), struct((n_q, rows, hd), bf)],
        cost=2 * keys * sides * n_q * rows * hd,
    )(kp, ds)
    gkv = swap(gkv, "far")
    both = lax.all_gather(oth, "core", axis=0, tiled=False)
    oth = jnp.where(side == 0, both[1], both[0])
    gq = (own + oth.astype(f32)).astype(bf)
    gq, gkv = lax.optimization_barrier((gq, gkv))
    gq = swap(gq, "head")
    return tuple(
        call(
            finish_kernel,
            [VMEM] * 2,
            [struct((run, heads * hd), f32), struct((run, hd), f32), struct((run, hd), f32)],
        )(gq, gkv)
    )


def solution(mesh):
    n_head, n_ctx = mesh.devices.shape
    fine = Mesh(mesh.devices.reshape(n_head, n_ctx // 2, 2), ("head", "far", "core"))
    tok = P(("head", "far", "core"))
    two = P(("head", "far", "core"), None)
    return jax.shard_map(
        on_device,
        mesh=fine,
        in_specs=(two, two, two, two, tok, tok),
        out_specs=(two, two, two),
        check_vma=False,
    )
```

```python
import functools
import math

import jax
import jax.numpy as jnp
from jax import lax
from jax.experimental import pallas as pl
from jax.experimental.pallas import tpu as pltpu
from jax.sharding import Mesh
from jax.sharding import PartitionSpec as P

LOW = -1e30
FLOOR = -1e29
DOC_STEP = 8192.0
META = 8
CHUNK = 256


def dot_rows(a, b):
    return lax.dot_general(a, b, (((1,), (1,)), ((), ())), preferred_element_type=jnp.float32)


def dot_plain(a, b):
    return lax.dot_general(a, b, (((1,), (0,)), ((), ())), preferred_element_type=jnp.float32)


def dot_cols(a, b):
    return lax.dot_general(a, b, (((0,), (0,)), ((), ())), preferred_element_type=jnp.float32)


def pack_kernel(pos_any, doc_any, q_any, g_any, k_any, v_any, qp_ref, kp_hbm, *scratch):
    bufs, sems, kp_ref, out_sem = scratch[:6], scratch[6], scratch[7], scratch[8]
    hbm = (pos_any, doc_any, q_any, g_any, k_any, v_any)
    copies = [pltpu.make_async_copy(src, dst, sems.at[i]) for i, (src, dst) in enumerate(zip(hbm, bufs))]
    for copy in copies:
        copy.start()
    for copy in copies[:2] + copies[4:]:
        copy.wait()
    pos_ref, doc_ref, q_ref, g_ref, k_ref, v_ref = bufs
    run, hd = k_ref.shape
    heads = q_ref.shape[1] // hd
    n_q, n_k = qp_ref.shape[0], kp_ref.shape[0]
    rows = run * heads
    first = pos_ref[0] // run
    high, low = first // 16, first % 16
    row = lax.broadcasted_iota(jnp.int32, (META, hd), 0)
    lane = lax.broadcasted_iota(jnp.int32, (META, hd), 1)
    tok = lane % run
    docs = jnp.zeros((META, hd), jnp.int32)
    for t in range(run):
        docs = jnp.where(tok == t, doc_ref[t], docs)
    q_meta = jnp.where(row == 0, docs, jnp.where(row == 1, high, jnp.where(row == 2, low, 0)))
    half = hd // 2
    tok_here = jnp.where(lane >= half, row + META, row)
    docs = jnp.zeros((META, hd), jnp.int32)
    for t in range(run):
        docs = jnp.where(tok_here == t, doc_ref[t], docs)
    item = lane % half
    k_meta = jnp.where(item == 0, docs, jnp.where(item == 1, high, jnp.where(item == 2, low, 0)))
    q_meta = q_meta.astype(jnp.float32).astype(jnp.bfloat16)
    k_meta = k_meta.astype(jnp.float32).astype(jnp.bfloat16)
    k, v = k_ref[...], v_ref[...]
    for d in range(n_k):
        kp_ref[d, 0:run, :] = k
        kp_ref[d, run : 2 * run, :] = v
        kp_ref[d, 2 * run : 2 * run + META, :] = k_meta
    out = pltpu.make_async_copy(kp_ref, kp_hbm, out_sem.at[0])
    out.start()
    for copy in copies[2:4]:
        copy.wait()
    for h in range(heads):
        q_h = q_ref[:, h * hd : (h + 1) * hd]
        g_h = g_ref[:, h * hd : (h + 1) * hd]
        for d in range(n_q):
            qp_ref[d, h * run : (h + 1) * run, :] = q_h
            qp_ref[d, rows + h * run : rows + (h + 1) * run, :] = g_h
    for d in range(n_q):
        qp_ref[d, 2 * rows : 2 * rows + META, :] = q_meta
    out.wait()


def key_codes(kp_ref, run):
    n_k, _, hd = kp_ref.shape
    meta = kp_ref[:, 2 * run : 2 * run + META, :].astype(jnp.float32).reshape(n_k * META, hd)
    src = lax.broadcasted_iota(jnp.int32, (hd, 2 * hd), 0)
    dst = lax.broadcasted_iota(jnp.int32, (hd, 2 * hd), 1)
    half = hd // 2
    item = src % half
    weight = jnp.where(
        item == 0, DOC_STEP, jnp.where(item == 1, run * 16.0, jnp.where(item == 2, run * 1.0, 0.0))
    )
    weight = jnp.where((src >= half) == (dst >= hd), weight, 0.0)
    codes = dot_plain(meta.astype(jnp.bfloat16), weight.astype(jnp.bfloat16))
    tok = lax.broadcasted_iota(jnp.int32, (n_k, META, hd), 1).astype(jnp.float32)
    lower = codes[:, :hd].reshape(n_k, META, hd) + tok
    upper = codes[:, hd:].reshape(n_k, META, hd) + (tok + META)
    return jnp.concatenate([lower, upper], axis=1).reshape(n_k * run, hd)


def query_codes(qp_ref, d, run):
    rows = (qp_ref.shape[1] - META) // 2
    meta = qp_ref[d, 2 * rows : 2 * rows + META, :].astype(jnp.float32)
    tok = (lax.broadcasted_iota(jnp.int32, (1, rows), 1) % run).astype(jnp.float32)
    base = meta[0:1] * DOC_STEP
    return base, base + meta[1:2] * (run * 16.0) + meta[2:3] * float(run) + tok


def blocks(qa_ref, qb_ref, side):
    n_q = qa_ref.shape[0]
    for d in range(0, 2 * n_q, 2):
        ref, at = (qa_ref, d) if d < n_q else (qb_ref, d - n_q)
        yield ref, at, d, (side if d < n_q else 1 - side) * n_q + at


def stats_kernel(side_ref, qa_ref, qb_ref, kp_ref, out_ref, e_ref, dp_ref, top_ref, code_ref):
    n_q, block, hd = qa_ref.shape
    n_k = kp_ref.shape[0]
    rows = (block - META) // 2
    run = (kp_ref.shape[1] - META) // 2
    scale = 1.0 / math.sqrt(hd)
    code_ref[...] = key_codes(kp_ref, run)
    per = CHUNK // run
    n_c = n_k // per
    for qp_ref, at, d, home in blocks(qa_ref, qb_ref, side_ref[0]):
        q = qp_ref[at : at + 2, 0:rows, :].reshape(2 * rows, hd)
        g = qp_ref[at : at + 2, rows : 2 * rows, :].reshape(2 * rows, hd)
        pairs = [query_codes(qp_ref, at + i, run) for i in range(2)]
        base = jnp.concatenate([p[0] for p in pairs], axis=1)
        top = jnp.concatenate([p[1] for p in pairs], axis=1)
        cols = slice(d * rows, (d + 2) * rows)
        sums = []
        for c in range(n_c):
            at_k, at_c = slice(c * per, (c + 1) * per), slice(c * CHUNK, (c + 1) * CHUNK)
            k = kp_ref[at_k, 0:run, :].reshape(CHUNK, hd)
            v = kp_ref[at_k, run : 2 * run, :].reshape(CHUNK, hd)
            code = jnp.concatenate([code_ref[at_c, :]] * (2 * rows // hd), axis=1)
            seen = (code <= top) & (code >= base)
            s = jnp.where(seen, dot_rows(k, q) * scale, LOW)
            high = jnp.maximum(jnp.max(s, axis=0, keepdims=True), FLOOR)
            e = jnp.exp(s - high)
            e_ref[at_c, cols] = e
            dp = dot_rows(v, g)
            dp_ref[at_c, cols] = dp
            top_ref[c : c + 1, cols] = high
            sums.append((high, jnp.sum(e, axis=0, keepdims=True), jnp.sum(e * dp, axis=0, keepdims=True)))
        high = functools.reduce(jnp.maximum, [x[0] for x in sums])
        share = [jnp.exp(x[0] - high) for x in sums]
        total = sum(f * x[1] for f, x in zip(share, sums))
        cross = sum(f * x[2] for f, x in zip(share, sums))
        some = total > 0.0
        safe = jnp.where(some, total, 1.0)
        log_total = jnp.where(some, high + jnp.log(safe), LOW)
        row_dot = jnp.where(some, cross / safe, 0.0)
        for i in range(2):
            lo, hi = i * rows, (i + 1) * rows
            for to in range(out_ref.shape[0]):
                out_ref[to, pl.ds(home + i, 1), :] = log_total[:, lo:hi]
                out_ref[to, pl.ds(2 * n_q + home + i, 1), :] = row_dot[:, lo:hi]


def keys_kernel(side_ref, qa_ref, qb_ref, st_ref, e_ref, dp_ref, top_ref, gkv_hbm, ds_ref, log_ref, dot_ref, gkv_ref, sems):
    n_q, block, hd = qa_ref.shape
    n_k, twice, _ = gkv_ref.shape
    run = twice // 2
    rows = (block - META) // 2
    scale = 1.0 / math.sqrt(hd)
    logs = st_ref[:, 0 : 2 * n_q, :]
    high = jnp.max(logs, axis=0)
    log_total = high + jnp.log(jnp.sum(jnp.exp(logs - high[None]), axis=0))
    log_ref[...] = log_total
    dot_ref[...] = jnp.sum(jnp.exp(logs - log_total[None]) * st_ref[:, 2 * n_q :, :], axis=0)

    def send(rows_at, i):
        copy = pltpu.make_async_copy(gkv_ref.at[:, rows_at, :], gkv_hbm.at[:, rows_at, :], sems.at[i])
        copy.start()
        return copy

    gv = jnp.zeros((n_k * run, hd), jnp.float32)
    for qp_ref, at, d, home in blocks(qa_ref, qb_ref, side_ref[0]):
        g = qp_ref[at : at + 2, rows : 2 * rows, :].reshape(2 * rows, hd)
        log_row = jnp.concatenate([log_ref[pl.ds(home + i, 1), :] for i in range(2)], axis=1)
        dot_row = jnp.concatenate([dot_ref[pl.ds(home + i, 1), :] for i in range(2)], axis=1)
        cols = slice(d * rows, (d + 2) * rows)
        parts = []
        for c in range(n_k * run // CHUNK):
            at_c = slice(c * CHUNK, (c + 1) * CHUNK)
            w = e_ref[at_c, cols] * jnp.exp(top_ref[c : c + 1, cols] - log_row)
            ds_ref[at_c, cols] = (w * (dp_ref[at_c, cols] - dot_row)).astype(jnp.bfloat16)
            parts.append(w.astype(jnp.bfloat16))
        gv = gv + dot_plain(jnp.concatenate(parts, axis=0), g)
    gkv_ref[:, run:, :] = gv.reshape(n_k, run, hd).astype(gkv_ref.dtype)
    values = send(slice(run, 2 * run), 0)
    gk = jnp.zeros((n_k * run, hd), jnp.float32)
    for qp_ref, at, d, home in blocks(qa_ref, qb_ref, side_ref[0]):
        q = qp_ref[at : at + 2, 0:rows, :].reshape(2 * rows, hd)
        gk = gk + dot_plain(ds_ref[:, d * rows : (d + 2) * rows], q)
    gkv_ref[:, 0:run, :] = (gk * scale).reshape(n_k, run, hd).astype(gkv_ref.dtype)
    keys = send(slice(0, run), 1)
    values.wait()
    keys.wait()


def queries_kernel(kp_ref, ds_ref, own_ref, oth_ref):
    n_q, rows, hd = own_ref.shape
    n_k = kp_ref.shape[0]
    run = (kp_ref.shape[1] - META) // 2
    scale = 1.0 / math.sqrt(hd)
    k = kp_ref[:, 0:run, :].reshape(n_k * run, hd)
    for d in list(range(n_q, 2 * n_q, 2)) + list(range(0, n_q, 2)):
        ref, at = (own_ref, d) if d < n_q else (oth_ref, d - n_q)
        gq = dot_cols(ds_ref[:, d * rows : (d + 2) * rows], k) * scale
        ref[at : at + 2] = gq.reshape(2, rows, hd).astype(ref.dtype)


def finish_kernel(gq_ref, gkv_ref, oq_ref, ok_ref, ov_ref):
    run, hd = ok_ref.shape
    gq = jnp.sum(gq_ref[...].astype(jnp.float32), axis=0)
    for h in range(oq_ref.shape[1] // hd):
        oq_ref[:, h * hd : (h + 1) * hd] = gq[h * run : (h + 1) * run, :]
    gkv = jnp.sum(gkv_ref[...].astype(jnp.float32), axis=0)
    ok_ref[...] = gkv[:run]
    ov_ref[...] = gkv[run:]


VMEM = pl.BlockSpec(memory_space=pltpu.VMEM)
SMEM = pl.BlockSpec(memory_space=pltpu.SMEM)
HBM = pl.BlockSpec(memory_space=pltpu.HBM)


def call(kernel, in_specs, outs, scratch=(), grant=16 * 1024 * 1024, cost=0, out_specs=None):
    return pl.pallas_call(
        kernel,
        in_specs=in_specs,
        out_specs=out_specs or [VMEM] * len(outs),
        out_shape=outs,
        scratch_shapes=list(scratch),
        cost_estimate=pl.CostEstimate(flops=cost, bytes_accessed=0, transcendentals=0) if cost else None,
        compiler_params=pltpu.CompilerParams(vmem_limit_bytes=grant),
    )


def on_device(queries, key_vecs, value_vecs, out_grad, positions, documents):
    n_q, n_k, sides = lax.axis_size("head"), lax.axis_size("far"), lax.axis_size("core")
    run, hd = key_vecs.shape
    heads = queries.shape[1] // hd
    rows = run * heads
    bf, f32 = jnp.bfloat16, jnp.float32
    keys = n_k * run
    struct = jax.ShapeDtypeStruct

    def swap(x, axis):
        return lax.all_to_all(x, axis, split_axis=0, concat_axis=0, tiled=True)

    def other(x):
        return lax.ppermute(x, "core", [(0, 1), (1, 0)])

    side = lax.axis_index("core").astype(jnp.int32).reshape(1)
    args = (positions, documents, queries, out_grad, key_vecs, value_vecs)
    qp, kp = call(
        pack_kernel,
        [HBM] * 6,
        [struct((n_q, 2 * rows + META, hd), bf), pltpu.HBM((n_k, 2 * run + META, hd), bf)],
        [(pltpu.SMEM if a.ndim == 1 else pltpu.VMEM)(a.shape, a.dtype) for a in args]
        + [
            pltpu.SemaphoreType.DMA((6,)),
            pltpu.VMEM((n_k, 2 * run + META, hd), bf),
            pltpu.SemaphoreType.DMA((1,)),
        ],
        out_specs=[VMEM, HBM],
    )(*(pltpu.with_memory_space_constraint(a, pltpu.HBM) for a in args))
    qa = swap(qp, "head")
    qb = other(qa)
    kp = swap(kp, "far")
    full = struct((keys, sides * n_q * rows), f32)
    line = struct((sides * n_q, rows), f32)
    tops = struct((keys // CHUNK, full.shape[1]), f32)
    st, e, dp, top = call(
        stats_kernel,
        [SMEM] + [VMEM] * 3,
        [struct((sides * n_q, 2 * sides * n_q, rows), f32), full, full, tops],
        [pltpu.VMEM((keys, hd), f32)],
    )(side, qa, qb, kp)
    st = swap(st, ("head", "core"))
    gkv, ds = call(
        keys_kernel,
        [SMEM] + [VMEM] * 6,
        [pltpu.HBM((n_k, 2 * run, hd), bf), struct(full.shape, bf)],
        [
            pltpu.VMEM(line.shape, f32),
            pltpu.VMEM(line.shape, f32),
            pltpu.VMEM((n_k, 2 * run, hd), bf),
            pltpu.SemaphoreType.DMA((2,)),
        ],
        out_specs=[HBM, VMEM],
    )(side, qa, qb, st, e, dp, top)
    own, oth = call(
        queries_kernel,
        [VMEM] * 2,
        [struct((n_q, rows, hd), f32), struct((n_q, rows, hd), bf)],
        cost=2 * keys * sides * n_q * rows * hd,
    )(kp, ds)
    gkv = swap(gkv, "far")
    both = lax.all_gather(oth, "core", axis=0, tiled=False)
    oth = jnp.where(side == 0, both[1], both[0])
    gq = (own + oth.astype(f32)).astype(bf)
    gq, gkv = lax.optimization_barrier((gq, gkv))
    gq = swap(gq, "head")
    return tuple(
        call(
            finish_kernel,
            [VMEM] * 2,
            [struct((run, heads * hd), f32), struct((run, hd), f32), struct((run, hd), f32)],
        )(gq, gkv)
    )


def solution(mesh):
    n_head, n_ctx = mesh.devices.shape
    fine = Mesh(mesh.devices.reshape(n_head, n_ctx // 2, 2), ("head", "far", "core"))
    tok = P(("head", "far", "core"))
    two = P(("head", "far", "core"), None)
    return jax.shard_map(
        on_device,
        mesh=fine,
        in_specs=(two, two, two, two, tok, tok),
        out_specs=(two, two, two),
        check_vma=False,
    )
```

```python
import functools
import math

import jax
import jax.numpy as jnp
from jax import lax
from jax.experimental import pallas as pl
from jax.experimental.pallas import tpu as pltpu
from jax.sharding import Mesh
from jax.sharding import PartitionSpec as P

LOW = -1e30
FLOOR = -1e29
DOC_STEP = 8192.0
META = 8
CHUNK = 256


def dot_rows(a, b):
    return lax.dot_general(a, b, (((1,), (1,)), ((), ())), preferred_element_type=jnp.float32)


def dot_plain(a, b):
    return lax.dot_general(a, b, (((1,), (0,)), ((), ())), preferred_element_type=jnp.float32)


def dot_cols(a, b):
    return lax.dot_general(a, b, (((0,), (0,)), ((), ())), preferred_element_type=jnp.float32)


def pack_kernel(pos_any, doc_any, q_any, g_any, k_any, v_any, qp_ref, kp_hbm, *scratch):
    bufs, sems, kp_ref, out_sem = scratch[:6], scratch[6], scratch[7], scratch[8]
    hbm = (pos_any, doc_any, q_any, g_any, k_any, v_any)
    copies = [pltpu.make_async_copy(src, dst, sems.at[i]) for i, (src, dst) in enumerate(zip(hbm, bufs))]
    for copy in copies:
        copy.start()
    for copy in copies[:2] + copies[4:]:
        copy.wait()
    pos_ref, doc_ref, q_ref, g_ref, k_ref, v_ref = bufs
    run, hd = k_ref.shape
    heads = q_ref.shape[1] // hd
    n_q, n_k = qp_ref.shape[0], kp_ref.shape[0]
    rows = run * heads
    first = pos_ref[0] // run
    high, low = first // 16, first % 16
    row = lax.broadcasted_iota(jnp.int32, (META, hd), 0)
    lane = lax.broadcasted_iota(jnp.int32, (META, hd), 1)
    tok = lane % run
    docs = jnp.zeros((META, hd), jnp.int32)
    for t in range(run):
        docs = jnp.where(tok == t, doc_ref[t], docs)
    q_meta = jnp.where(row == 0, docs, jnp.where(row == 1, high, jnp.where(row == 2, low, 0)))
    half = hd // 2
    tok_here = jnp.where(lane >= half, row + META, row)
    docs = jnp.zeros((META, hd), jnp.int32)
    for t in range(run):
        docs = jnp.where(tok_here == t, doc_ref[t], docs)
    item = lane % half
    k_meta = jnp.where(item == 0, docs, jnp.where(item == 1, high, jnp.where(item == 2, low, 0)))
    q_meta = q_meta.astype(jnp.float32).astype(jnp.bfloat16)
    k_meta = k_meta.astype(jnp.float32).astype(jnp.bfloat16)
    k, v = k_ref[...], v_ref[...]
    for d in range(n_k):
        kp_ref[d, 0:run, :] = k
        kp_ref[d, run : 2 * run, :] = v
        kp_ref[d, 2 * run : 2 * run + META, :] = k_meta
    out = pltpu.make_async_copy(kp_ref, kp_hbm, out_sem.at[0])
    out.start()
    for copy in copies[2:4]:
        copy.wait()
    for h in range(heads):
        q_h = q_ref[:, h * hd : (h + 1) * hd]
        g_h = g_ref[:, h * hd : (h + 1) * hd]
        for d in range(n_q):
            qp_ref[d, h * run : (h + 1) * run, :] = q_h
            qp_ref[d, rows + h * run : rows + (h + 1) * run, :] = g_h
    for d in range(n_q):
        qp_ref[d, 2 * rows : 2 * rows + META, :] = q_meta
    out.wait()


def key_codes(kp, run):
    n_k, _, hd = kp.shape
    meta = kp[:, 2 * run : 2 * run + META, :].astype(jnp.float32).reshape(n_k * META, hd)
    src = lax.broadcasted_iota(jnp.int32, (hd, 2 * hd), 0)
    dst = lax.broadcasted_iota(jnp.int32, (hd, 2 * hd), 1)
    half = hd // 2
    item = src % half
    weight = jnp.where(
        item == 0, DOC_STEP, jnp.where(item == 1, run * 16.0, jnp.where(item == 2, run * 1.0, 0.0))
    )
    weight = jnp.where((src >= half) == (dst >= hd), weight, 0.0)
    codes = dot_plain(meta.astype(jnp.bfloat16), weight.astype(jnp.bfloat16))
    tok = lax.broadcasted_iota(jnp.int32, (n_k, META, hd), 1).astype(jnp.float32)
    lower = codes[:, :hd].reshape(n_k, META, hd) + tok
    upper = codes[:, hd:].reshape(n_k, META, hd) + (tok + META)
    return jnp.concatenate([lower, upper], axis=1).reshape(n_k * run, hd)


def query_codes(qp_ref, d, run):
    rows = (qp_ref.shape[1] - META) // 2
    meta = qp_ref[d, 2 * rows : 2 * rows + META, :].astype(jnp.float32)
    tok = (lax.broadcasted_iota(jnp.int32, (1, rows), 1) % run).astype(jnp.float32)
    base = meta[0:1] * DOC_STEP
    return base, base + meta[1:2] * (run * 16.0) + meta[2:3] * float(run) + tok


def stats_kernel(side_ref, qp_ref, kp_ref, out_ref, e_ref, dp_ref, top_ref, code_ref):
    n_q, block, hd = qp_ref.shape
    _, n_k, kp_rows, _ = kp_ref.shape
    rows = (block - META) // 2
    run = (kp_rows - META) // 2
    scale = 1.0 / math.sqrt(hd)
    half = n_k * run
    per = CHUNK // run
    cores = (side_ref[0], 1 - side_ref[0])
    for i, core in enumerate(cores):
        code_ref[i * half : (i + 1) * half, :] = key_codes(kp_ref.at[core], run)
    for d in range(0, n_q, 2):
        q = qp_ref[d : d + 2, 0:rows, :].reshape(2 * rows, hd)
        g = qp_ref[d : d + 2, rows : 2 * rows, :].reshape(2 * rows, hd)
        pairs = [query_codes(qp_ref, d + i, run) for i in range(2)]
        base = jnp.concatenate([p[0] for p in pairs], axis=1)
        top = jnp.concatenate([p[1] for p in pairs], axis=1)
        cols = slice(d * rows, (d + 2) * rows)
        sums = []
        for c in range(2 * half // CHUNK):
            core, at = cores[c * CHUNK // half], (c * CHUNK % half) // run
            at_c = slice(c * CHUNK, (c + 1) * CHUNK)
            k = kp_ref[core, at : at + per, 0:run, :].reshape(CHUNK, hd)
            v = kp_ref[core, at : at + per, run : 2 * run, :].reshape(CHUNK, hd)
            code = jnp.concatenate([code_ref[at_c, :]] * (2 * rows // hd), axis=1)
            seen = (code <= top) & (code >= base)
            s = jnp.where(seen, dot_rows(k, q) * scale, LOW)
            high = jnp.maximum(jnp.max(s, axis=0, keepdims=True), FLOOR)
            e = jnp.exp(s - high)
            e_ref[at_c, cols] = e
            dp = dot_rows(v, g)
            dp_ref[at_c, cols] = dp
            top_ref[c : c + 1, cols] = high
            sums.append((high, jnp.sum(e, axis=0, keepdims=True), jnp.sum(e * dp, axis=0, keepdims=True)))
        high = functools.reduce(jnp.maximum, [x[0] for x in sums])
        share = [jnp.exp(x[0] - high) for x in sums]
        total = sum(f * x[1] for f, x in zip(share, sums))
        cross = sum(f * x[2] for f, x in zip(share, sums))
        some = total > 0.0
        safe = jnp.where(some, total, 1.0)
        log_total = jnp.where(some, high + jnp.log(safe), LOW)
        row_dot = jnp.where(some, cross / safe, 0.0)
        for i in range(2):
            lo, hi = i * rows, (i + 1) * rows
            for to in range(n_q):
                out_ref[to, d + i : d + i + 1, :] = log_total[:, lo:hi]
                out_ref[to, n_q + d + i : n_q + d + i + 1, :] = row_dot[:, lo:hi]


def grads_kernel(
    side_ref, qp_ref, kp_ref, st_ref, e_ref, dp_ref, top_ref, gq_hbm, keep_ref, give_ref, log_ref, dot_ref, ds_ref, gq_ref, sem
):
    n_q, block, hd = qp_ref.shape
    n_k, twice, _ = keep_ref.shape
    run = twice // 2
    rows = (block - META) // 2
    scale = 1.0 / math.sqrt(hd)
    half = n_k * run
    cores = (side_ref[0], 1 - side_ref[0])
    logs = st_ref[:, 0:n_q, :]
    high = jnp.max(logs, axis=0)
    log_total = high + jnp.log(jnp.sum(jnp.exp(logs - high[None]), axis=0))
    log_ref[...] = log_total
    dot_ref[...] = jnp.sum(jnp.exp(logs - log_total[None]) * st_ref[:, n_q:, :], axis=0)
    gv = [jnp.zeros((half, hd), jnp.float32) for _ in cores]
    for d in range(0, n_q, 2):
        g = qp_ref[d : d + 2, rows : 2 * rows, :].reshape(2 * rows, hd)
        log_row = jnp.concatenate([log_ref[d + i : d + i + 1, :] for i in range(2)], axis=1)
        dot_row = jnp.concatenate([dot_ref[d + i : d + i + 1, :] for i in range(2)], axis=1)
        cols = slice(d * rows, (d + 2) * rows)
        gq = jnp.zeros((2 * rows, hd), jnp.float32)
        for i, core in enumerate(cores):
            parts = []
            for c in range(i * half // CHUNK, (i + 1) * half // CHUNK):
                at_c = slice(c * CHUNK, (c + 1) * CHUNK)
                w = e_ref[at_c, cols] * jnp.exp(top_ref[c : c + 1, cols] - log_row)
                ds_ref[at_c, cols] = (w * (dp_ref[at_c, cols] - dot_row)).astype(jnp.bfloat16)
                parts.append(w.astype(jnp.bfloat16))
            gv[i] = gv[i] + dot_plain(jnp.concatenate(parts, axis=0), g)
            k = kp_ref[core, :, 0:run, :].reshape(half, hd)
            gq = gq + dot_cols(ds_ref[i * half : (i + 1) * half, cols], k)
        gq_ref[d : d + 2] = (gq * scale).reshape(2, rows, hd).astype(gq_ref.dtype)
    out = pltpu.make_async_copy(gq_ref, gq_hbm, sem.at[0])
    out.start()
    for i, ref in enumerate((keep_ref, give_ref)):
        gk = jnp.zeros((half, hd), jnp.float32)
        for d in range(0, n_q, 2):
            q = qp_ref[d : d + 2, 0:rows, :].reshape(2 * rows, hd)
            gk = gk + dot_plain(ds_ref[i * half : (i + 1) * half, d * rows : (d + 2) * rows], q)
        ref[:, 0:run, :] = (gk * scale).reshape(n_k, run, hd).astype(ref.dtype)
        ref[:, run:, :] = gv[i].reshape(n_k, run, hd).astype(ref.dtype)
    out.wait()


def finish_kernel(gq_ref, gkv_ref, oq_ref, ok_ref, ov_ref):
    run, hd = ok_ref.shape
    gq = jnp.sum(gq_ref[...].astype(jnp.float32), axis=0)
    for h in range(oq_ref.shape[1] // hd):
        oq_ref[:, h * hd : (h + 1) * hd] = gq[h * run : (h + 1) * run, :]
    gkv = jnp.sum(gkv_ref[...].astype(jnp.float32), axis=0)
    ok_ref[...] = gkv[:run]
    ov_ref[...] = gkv[run:]


VMEM = pl.BlockSpec(memory_space=pltpu.VMEM)
SMEM = pl.BlockSpec(memory_space=pltpu.SMEM)
HBM = pl.BlockSpec(memory_space=pltpu.HBM)


def call(kernel, in_specs, outs, scratch=(), grant=16 * 1024 * 1024, cost=0, out_specs=None):
    return pl.pallas_call(
        kernel,
        in_specs=in_specs,
        out_specs=out_specs or [VMEM] * len(outs),
        out_shape=outs,
        scratch_shapes=list(scratch),
        cost_estimate=pl.CostEstimate(flops=cost, bytes_accessed=0, transcendentals=0) if cost else None,
        compiler_params=pltpu.CompilerParams(vmem_limit_bytes=grant),
    )


def on_device(queries, key_vecs, value_vecs, out_grad, positions, documents):
    n_q, n_k = lax.axis_size("head"), lax.axis_size("far")
    run, hd = key_vecs.shape
    heads = queries.shape[1] // hd
    rows = run * heads
    bf, f32 = jnp.bfloat16, jnp.float32
    keys = n_k * run
    struct = jax.ShapeDtypeStruct

    def swap(x, axis):
        return lax.all_to_all(x, axis, split_axis=0, concat_axis=0, tiled=True)

    side = lax.axis_index("core").astype(jnp.int32).reshape(1)
    args = (positions, documents, queries, out_grad, key_vecs, value_vecs)
    qp, kp = call(
        pack_kernel,
        [HBM] * 6,
        [struct((n_q, 2 * rows + META, hd), bf), pltpu.HBM((n_k, 2 * run + META, hd), bf)],
        [(pltpu.SMEM if a.ndim == 1 else pltpu.VMEM)(a.shape, a.dtype) for a in args]
        + [
            pltpu.SemaphoreType.DMA((6,)),
            pltpu.VMEM((n_k, 2 * run + META, hd), bf),
            pltpu.SemaphoreType.DMA((1,)),
        ],
        out_specs=[VMEM, HBM],
    )(*(pltpu.with_memory_space_constraint(a, pltpu.HBM) for a in args))
    kp = swap(kp, "far")
    qp, kp = lax.optimization_barrier((qp, kp))
    qp = swap(qp, "head")
    kp = lax.all_gather(kp, "core", axis=0, tiled=False)
    full = struct((2 * keys, n_q * rows), f32)
    line = pltpu.VMEM((n_q, rows), f32)
    st, e, dp, top = call(
        stats_kernel,
        [SMEM] + [VMEM] * 2,
        [struct((n_q, 2 * n_q, rows), f32), full, full, struct((2 * keys // CHUNK, n_q * rows), f32)],
        [pltpu.VMEM((2 * keys, hd), f32)],
    )(side, qp, kp)
    st = swap(st, "head")
    gq, keep, give = call(
        grads_kernel,
        [SMEM] + [VMEM] * 6,
        [pltpu.HBM((n_q, rows, hd), bf), struct((n_k, 2 * run, hd), f32), struct((n_k, 2 * run, hd), bf)],
        [line, line, pltpu.VMEM(full.shape, bf), pltpu.VMEM((n_q, rows, hd), bf), pltpu.SemaphoreType.DMA((1,))],
        out_specs=[HBM, VMEM, VMEM],
    )(side, qp, kp, st, e, dp, top)
    gq = swap(gq, "head")
    both = lax.all_gather(give, "core", axis=0, tiled=False)
    gkv = (keep + jnp.where(side[0] == 0, both[1], both[0]).astype(f32)).astype(bf)
    gkv, gq = lax.optimization_barrier((gkv, gq))
    gkv = swap(gkv, "far")
    return tuple(
        call(
            finish_kernel,
            [VMEM] * 2,
            [struct((run, heads * hd), f32), struct((run, hd), f32), struct((run, hd), f32)],
        )(gq, gkv)
    )


def solution(mesh):
    n_head, n_ctx = mesh.devices.shape
    fine = Mesh(mesh.devices.reshape(n_head, n_ctx // 2, 2), ("head", "far", "core"))
    tok = P(("head", "far", "core"))
    two = P(("head", "far", "core"), None)
    return jax.shard_map(
        on_device,
        mesh=fine,
        in_specs=(two, two, two, two, tok, tok),
        out_specs=(two, two, two),
        check_vma=False,
    )
```

```python
import functools
import math

import jax
import jax.numpy as jnp
from jax import lax
from jax.experimental import pallas as pl
from jax.experimental.pallas import tpu as pltpu
from jax.sharding import Mesh
from jax.sharding import PartitionSpec as P

LOW = -1e30
FLOOR = -1e29
DOC_STEP = 8192.0
META = 8
CHUNK = 256


def dot_rows(a, b):
    return lax.dot_general(a, b, (((1,), (1,)), ((), ())), preferred_element_type=jnp.float32)


def dot_plain(a, b):
    return lax.dot_general(a, b, (((1,), (0,)), ((), ())), preferred_element_type=jnp.float32)


def dot_cols(a, b):
    return lax.dot_general(a, b, (((0,), (0,)), ((), ())), preferred_element_type=jnp.float32)


def fetch(hbm, bufs, sems):
    copies = [pltpu.make_async_copy(src, dst, sems.at[i]) for i, (src, dst) in enumerate(zip(hbm, bufs))]
    for copy in copies:
        copy.start()
    for copy in copies:
        copy.wait()


def meta_rows(pos_ref, doc_ref, run, tok, item):
    first = pos_ref[0] // run
    docs = jnp.zeros(tok.shape, jnp.int32)
    for t in range(run):
        docs = jnp.where(tok == t, doc_ref[t], docs)
    meta = jnp.where(item == 0, docs, jnp.where(item == 1, first // 16, jnp.where(item == 2, first % 16, 0)))
    return meta.astype(jnp.float32).astype(jnp.bfloat16)


def pack_keys_kernel(pos_any, doc_any, k_any, v_any, kp_hbm, pos_ref, doc_ref, k_ref, v_ref, sems, kp_ref, out_sem):
    fetch((pos_any, doc_any, k_any, v_any), (pos_ref, doc_ref, k_ref, v_ref), sems)
    run, hd = k_ref.shape
    row = lax.broadcasted_iota(jnp.int32, (META, hd), 0)
    lane = lax.broadcasted_iota(jnp.int32, (META, hd), 1)
    half = hd // 2
    meta = meta_rows(pos_ref, doc_ref, run, jnp.where(lane >= half, row + META, row), lane % half)
    k, v = k_ref[...], v_ref[...]
    for d in range(kp_ref.shape[0]):
        kp_ref[d, 0:run, :] = k
        kp_ref[d, run : 2 * run, :] = v
        kp_ref[d, 2 * run : 2 * run + META, :] = meta
    out = pltpu.make_async_copy(kp_ref, kp_hbm, out_sem.at[0])
    out.start()
    out.wait()


def pack_queries_kernel(pos_any, doc_any, q_any, g_any, qp_hbm, pos_ref, doc_ref, q_ref, g_ref, sems, qp_ref, out_sem):
    fetch((pos_any, doc_any, q_any, g_any), (pos_ref, doc_ref, q_ref, g_ref), sems)
    n_q, block, hd = qp_ref.shape
    rows = (block - META) // 2
    run = q_ref.shape[0]
    row = lax.broadcasted_iota(jnp.int32, (META, hd), 0)
    lane = lax.broadcasted_iota(jnp.int32, (META, hd), 1)
    meta = meta_rows(pos_ref, doc_ref, run, lane % run, row)
    for h in range(rows // run):
        q_h = q_ref[:, h * hd : (h + 1) * hd]
        g_h = g_ref[:, h * hd : (h + 1) * hd]
        for d in range(n_q):
            qp_ref[d, h * run : (h + 1) * run, :] = q_h
            qp_ref[d, rows + h * run : rows + (h + 1) * run, :] = g_h
    for d in range(n_q):
        qp_ref[d, 2 * rows : 2 * rows + META, :] = meta
    out = pltpu.make_async_copy(qp_ref, qp_hbm, out_sem.at[0])
    out.start()
    out.wait()


def key_codes(kp, run):
    n_k, _, hd = kp.shape
    meta = kp[:, 2 * run : 2 * run + META, :].astype(jnp.float32).reshape(n_k * META, hd)
    src = lax.broadcasted_iota(jnp.int32, (hd, 2 * hd), 0)
    dst = lax.broadcasted_iota(jnp.int32, (hd, 2 * hd), 1)
    half = hd // 2
    item = src % half
    weight = jnp.where(
        item == 0, DOC_STEP, jnp.where(item == 1, run * 16.0, jnp.where(item == 2, run * 1.0, 0.0))
    )
    weight = jnp.where((src >= half) == (dst >= hd), weight, 0.0)
    codes = dot_plain(meta.astype(jnp.bfloat16), weight.astype(jnp.bfloat16))
    tok = lax.broadcasted_iota(jnp.int32, (n_k, META, hd), 1).astype(jnp.float32)
    lower = codes[:, :hd].reshape(n_k, META, hd) + tok
    upper = codes[:, hd:].reshape(n_k, META, hd) + (tok + META)
    return jnp.concatenate([lower, upper], axis=1).reshape(n_k * run, hd)


def query_codes(qp_ref, d, run):
    rows = (qp_ref.shape[1] - META) // 2
    meta = qp_ref[d, 2 * rows : 2 * rows + META, :].astype(jnp.float32)
    tok = (lax.broadcasted_iota(jnp.int32, (1, rows), 1) % run).astype(jnp.float32)
    base = meta[0:1] * DOC_STEP
    return base, base + meta[1:2] * (run * 16.0) + meta[2:3] * float(run) + tok


def stats_kernel(side_ref, qp_ref, kp_ref, out_ref, e_ref, dp_ref, top_ref, code_ref):
    n_q, block, hd = qp_ref.shape
    _, n_k, kp_rows, _ = kp_ref.shape
    rows = (block - META) // 2
    run = (kp_rows - META) // 2
    scale = 1.0 / math.sqrt(hd)
    half = n_k * run
    per = CHUNK // run
    cores = (side_ref[0], 1 - side_ref[0])
    for i, core in enumerate(cores):
        code_ref[i * half : (i + 1) * half, :] = key_codes(kp_ref.at[core], run)
    for d in range(0, n_q, 2):
        q = qp_ref[d : d + 2, 0:rows, :].reshape(2 * rows, hd)
        g = qp_ref[d : d + 2, rows : 2 * rows, :].reshape(2 * rows, hd)
        pairs = [query_codes(qp_ref, d + i, run) for i in range(2)]
        base = jnp.concatenate([p[0] for p in pairs], axis=1)
        top = jnp.concatenate([p[1] for p in pairs], axis=1)
        cols = slice(d * rows, (d + 2) * rows)
        sums = []
        for c in range(2 * half // CHUNK):
            core, at = cores[c * CHUNK // half], (c * CHUNK % half) // run
            at_c = slice(c * CHUNK, (c + 1) * CHUNK)
            k = kp_ref[core, at : at + per, 0:run, :].reshape(CHUNK, hd)
            v = kp_ref[core, at : at + per, run : 2 * run, :].reshape(CHUNK, hd)
            code = jnp.concatenate([code_ref[at_c, :]] * (2 * rows // hd), axis=1)
            seen = (code <= top) & (code >= base)
            s = jnp.where(seen, dot_rows(k, q) * scale, LOW)
            high = jnp.maximum(jnp.max(s, axis=0, keepdims=True), FLOOR)
            e = jnp.exp(s - high)
            e_ref[at_c, cols] = e
            dp = dot_rows(v, g)
            dp_ref[at_c, cols] = dp
            top_ref[c : c + 1, cols] = high
            sums.append((high, jnp.sum(e, axis=0, keepdims=True), jnp.sum(e * dp, axis=0, keepdims=True)))
        high = functools.reduce(jnp.maximum, [x[0] for x in sums])
        share = [jnp.exp(x[0] - high) for x in sums]
        total = sum(f * x[1] for f, x in zip(share, sums))
        cross = sum(f * x[2] for f, x in zip(share, sums))
        some = total > 0.0
        safe = jnp.where(some, total, 1.0)
        log_total = jnp.where(some, high + jnp.log(safe), LOW)
        row_dot = jnp.where(some, cross / safe, 0.0)
        for i in range(2):
            lo, hi = i * rows, (i + 1) * rows
            for to in range(n_q):
                out_ref[to, d + i : d + i + 1, :] = log_total[:, lo:hi]
                out_ref[to, n_q + d + i : n_q + d + i + 1, :] = row_dot[:, lo:hi]


def grads_kernel(
    side_ref, qp_ref, kp_ref, st_ref, e_ref, dp_ref, top_ref, gq_hbm, keep_ref, give_ref, log_ref, dot_ref, ds_ref, gq_ref, sem
):
    n_q, block, hd = qp_ref.shape
    n_k, twice, _ = keep_ref.shape
    run = twice // 2
    rows = (block - META) // 2
    scale = 1.0 / math.sqrt(hd)
    half = n_k * run
    cores = (side_ref[0], 1 - side_ref[0])
    logs = st_ref[:, 0:n_q, :]
    high = jnp.max(logs, axis=0)
    log_total = high + jnp.log(jnp.sum(jnp.exp(logs - high[None]), axis=0))
    log_ref[...] = log_total
    dot_ref[...] = jnp.sum(jnp.exp(logs - log_total[None]) * st_ref[:, n_q:, :], axis=0)
    gv = [jnp.zeros((half, hd), jnp.float32) for _ in cores]
    for d in range(0, n_q, 2):
        g = qp_ref[d : d + 2, rows : 2 * rows, :].reshape(2 * rows, hd)
        log_row = jnp.concatenate([log_ref[d + i : d + i + 1, :] for i in range(2)], axis=1)
        dot_row = jnp.concatenate([dot_ref[d + i : d + i + 1, :] for i in range(2)], axis=1)
        cols = slice(d * rows, (d + 2) * rows)
        gq = jnp.zeros((2 * rows, hd), jnp.float32)
        for i, core in enumerate(cores):
            parts = []
            for c in range(i * half // CHUNK, (i + 1) * half // CHUNK):
                at_c = slice(c * CHUNK, (c + 1) * CHUNK)
                w = e_ref[at_c, cols] * jnp.exp(top_ref[c : c + 1, cols] - log_row)
                ds_ref[at_c, cols] = (w * (dp_ref[at_c, cols] - dot_row)).astype(jnp.bfloat16)
                parts.append(w.astype(jnp.bfloat16))
            gv[i] = gv[i] + dot_plain(jnp.concatenate(parts, axis=0), g)
            k = kp_ref[core, :, 0:run, :].reshape(half, hd)
            gq = gq + dot_cols(ds_ref[i * half : (i + 1) * half, cols], k)
        gq_ref[d : d + 2] = (gq * scale).reshape(2, rows, hd).astype(gq_ref.dtype)
    out = pltpu.make_async_copy(gq_ref, gq_hbm, sem.at[0])
    out.start()
    for i, ref in enumerate((keep_ref, give_ref)):
        gk = jnp.zeros((half, hd), jnp.float32)
        for d in range(0, n_q, 2):
            q = qp_ref[d : d + 2, 0:rows, :].reshape(2 * rows, hd)
            gk = gk + dot_plain(ds_ref[i * half : (i + 1) * half, d * rows : (d + 2) * rows], q)
        ref[:, 0:run, :] = (gk * scale).reshape(n_k, run, hd).astype(ref.dtype)
        ref[:, run:, :] = gv[i].reshape(n_k, run, hd).astype(ref.dtype)
    out.wait()


def finish_kernel(gq_ref, gkv_ref, oq_ref, ok_ref, ov_ref):
    run, hd = ok_ref.shape
    gq = jnp.sum(gq_ref[...].astype(jnp.float32), axis=0)
    for h in range(oq_ref.shape[1] // hd):
        oq_ref[:, h * hd : (h + 1) * hd] = gq[h * run : (h + 1) * run, :]
    gkv = jnp.sum(gkv_ref[...].astype(jnp.float32), axis=0)
    ok_ref[...] = gkv[:run]
    ov_ref[...] = gkv[run:]


VMEM = pl.BlockSpec(memory_space=pltpu.VMEM)
SMEM = pl.BlockSpec(memory_space=pltpu.SMEM)
HBM = pl.BlockSpec(memory_space=pltpu.HBM)


def call(kernel, in_specs, outs, scratch=(), grant=16 * 1024 * 1024, cost=0, out_specs=None):
    return pl.pallas_call(
        kernel,
        in_specs=in_specs,
        out_specs=out_specs or [VMEM] * len(outs),
        out_shape=outs,
        scratch_shapes=list(scratch),
        cost_estimate=pl.CostEstimate(flops=cost, bytes_accessed=0, transcendentals=0) if cost else None,
        compiler_params=pltpu.CompilerParams(vmem_limit_bytes=grant),
    )


def on_device(queries, key_vecs, value_vecs, out_grad, positions, documents):
    n_q, n_k = lax.axis_size("head"), lax.axis_size("far")
    run, hd = key_vecs.shape
    heads = queries.shape[1] // hd
    rows = run * heads
    bf, f32 = jnp.bfloat16, jnp.float32
    keys = n_k * run
    struct = jax.ShapeDtypeStruct

    def swap(x, axis):
        return lax.all_to_all(x, axis, split_axis=0, concat_axis=0, tiled=True)

    side = lax.axis_index("core").astype(jnp.int32).reshape(1)
    def pack(kernel, shape, *args, cost=0):
        (packed,) = call(
            kernel,
            [HBM] * len(args),
            [pltpu.HBM(shape, bf)],
            [(pltpu.SMEM if a.ndim == 1 else pltpu.VMEM)(a.shape, a.dtype) for a in args]
            + [pltpu.SemaphoreType.DMA((len(args),)), pltpu.VMEM(shape, bf), pltpu.SemaphoreType.DMA((1,))],
            out_specs=[HBM],
            cost=cost,
        )(*(pltpu.with_memory_space_constraint(a, pltpu.HBM) for a in args))
        return packed

    kp = pack(pack_keys_kernel, (n_k, 2 * run + META, hd), positions, documents, key_vecs, value_vecs)
    q_shape = (n_q, 2 * rows + META, hd)
    qp = pack(pack_queries_kernel, q_shape, positions, documents, queries, out_grad, cost=10**9)
    kp = swap(kp, "far")
    qp, kp = lax.optimization_barrier((qp, kp))
    qp = swap(qp, "head")
    kp = lax.all_gather(kp, "core", axis=0, tiled=False)
    full = struct((2 * keys, n_q * rows), f32)
    line = pltpu.VMEM((n_q, rows), f32)
    st, e, dp, top = call(
        stats_kernel,
        [SMEM] + [VMEM] * 2,
        [struct((n_q, 2 * n_q, rows), f32), full, full, struct((2 * keys // CHUNK, n_q * rows), f32)],
        [pltpu.VMEM((2 * keys, hd), f32)],
    )(side, qp, kp)
    st = swap(st, "head")
    gq, keep, give = call(
        grads_kernel,
        [SMEM] + [VMEM] * 6,
        [pltpu.HBM((n_q, rows, hd), bf), struct((n_k, 2 * run, hd), f32), struct((n_k, 2 * run, hd), bf)],
        [line, line, pltpu.VMEM(full.shape, bf), pltpu.VMEM((n_q, rows, hd), bf), pltpu.SemaphoreType.DMA((1,))],
        out_specs=[HBM, VMEM, VMEM],
    )(side, qp, kp, st, e, dp, top)
    gq = swap(gq, "head")
    both = lax.all_gather(give, "core", axis=0, tiled=False)
    gkv = (keep + jnp.where(side[0] == 0, both[1], both[0]).astype(f32)).astype(bf)
    gkv, gq = lax.optimization_barrier((gkv, gq))
    gkv = swap(gkv, "far")
    return tuple(
        call(
            finish_kernel,
            [VMEM] * 2,
            [struct((run, heads * hd), f32), struct((run, hd), f32), struct((run, hd), f32)],
        )(gq, gkv)
    )


def solution(mesh):
    n_head, n_ctx = mesh.devices.shape
    fine = Mesh(mesh.devices.reshape(n_head, n_ctx // 2, 2), ("head", "far", "core"))
    tok = P(("head", "far", "core"))
    two = P(("head", "far", "core"), None)
    return jax.shard_map(
        on_device,
        mesh=fine,
        in_specs=(two, two, two, two, tok, tok),
        out_specs=(two, two, two),
        check_vma=False,
    )
```

```python
import functools
import math

import jax
import jax.numpy as jnp
from jax import lax
from jax.experimental import pallas as pl
from jax.experimental.pallas import tpu as pltpu
from jax.sharding import Mesh
from jax.sharding import PartitionSpec as P

LOW = -1e30
FLOOR = -1e29
DOC_STEP = 8192.0
META = 8
CHUNK = 256


def dot_rows(a, b):
    return lax.dot_general(a, b, (((1,), (1,)), ((), ())), preferred_element_type=jnp.float32)


def dot_plain(a, b):
    return lax.dot_general(a, b, (((1,), (0,)), ((), ())), preferred_element_type=jnp.float32)


def dot_cols(a, b):
    return lax.dot_general(a, b, (((0,), (0,)), ((), ())), preferred_element_type=jnp.float32)


def fetch(hbm, bufs, sems):
    copies = [pltpu.make_async_copy(src, dst, sems.at[i]) for i, (src, dst) in enumerate(zip(hbm, bufs))]
    for copy in copies:
        copy.start()
    for copy in copies:
        copy.wait()


def meta_rows(pos_ref, doc_ref, run, tok, item):
    first = pos_ref[0] // run
    docs = jnp.zeros(tok.shape, jnp.int32)
    for t in range(run):
        docs = jnp.where(tok == t, doc_ref[t], docs)
    meta = jnp.where(item == 0, docs, jnp.where(item == 1, first // 16, jnp.where(item == 2, first % 16, 0)))
    return meta.astype(jnp.float32).astype(jnp.bfloat16)


def pack_keys_kernel(pos_any, doc_any, k_any, v_any, kp_hbm, pos_ref, doc_ref, k_ref, v_ref, sems, kp_ref, out_sem):
    fetch((pos_any, doc_any, k_any, v_any), (pos_ref, doc_ref, k_ref, v_ref), sems)
    run, hd = k_ref.shape
    row = lax.broadcasted_iota(jnp.int32, (META, hd), 0)
    lane = lax.broadcasted_iota(jnp.int32, (META, hd), 1)
    half = hd // 2
    meta = meta_rows(pos_ref, doc_ref, run, jnp.where(lane >= half, row + META, row), lane % half)
    k, v = k_ref[...], v_ref[...]
    for d in range(kp_ref.shape[0]):
        kp_ref[d, 0:run, :] = k
        kp_ref[d, run : 2 * run, :] = v
        kp_ref[d, 2 * run : 2 * run + META, :] = meta
    out = pltpu.make_async_copy(kp_ref, kp_hbm, out_sem.at[0])
    out.start()
    out.wait()


def pack_queries_kernel(pos_any, doc_any, q_any, g_any, qp_hbm, pos_ref, doc_ref, q_ref, g_ref, sems, qp_ref, out_sem):
    fetch((pos_any, doc_any, q_any, g_any), (pos_ref, doc_ref, q_ref, g_ref), sems)
    n_q, block, hd = qp_ref.shape
    rows = (block - META) // 2
    run = q_ref.shape[0]
    row = lax.broadcasted_iota(jnp.int32, (META, hd), 0)
    lane = lax.broadcasted_iota(jnp.int32, (META, hd), 1)
    meta = meta_rows(pos_ref, doc_ref, run, lane % run, row)
    for h in range(rows // run):
        q_h = q_ref[:, h * hd : (h + 1) * hd]
        g_h = g_ref[:, h * hd : (h + 1) * hd]
        for d in range(n_q):
            qp_ref[d, h * run : (h + 1) * run, :] = q_h
            qp_ref[d, rows + h * run : rows + (h + 1) * run, :] = g_h
    for d in range(n_q):
        qp_ref[d, 2 * rows : 2 * rows + META, :] = meta
    out = pltpu.make_async_copy(qp_ref, qp_hbm, out_sem.at[0])
    out.start()
    out.wait()


def key_codes(kp, run):
    n_k, _, hd = kp.shape
    meta = kp[:, 2 * run : 2 * run + META, :].astype(jnp.float32).reshape(n_k * META, hd)
    src = lax.broadcasted_iota(jnp.int32, (hd, 2 * hd), 0)
    dst = lax.broadcasted_iota(jnp.int32, (hd, 2 * hd), 1)
    half = hd // 2
    item = src % half
    weight = jnp.where(
        item == 0, DOC_STEP, jnp.where(item == 1, run * 16.0, jnp.where(item == 2, run * 1.0, 0.0))
    )
    weight = jnp.where((src >= half) == (dst >= hd), weight, 0.0)
    codes = dot_plain(meta.astype(jnp.bfloat16), weight.astype(jnp.bfloat16))
    tok = lax.broadcasted_iota(jnp.int32, (n_k, META, hd), 1).astype(jnp.float32)
    lower = codes[:, :hd].reshape(n_k, META, hd) + tok
    upper = codes[:, hd:].reshape(n_k, META, hd) + (tok + META)
    return jnp.concatenate([lower, upper], axis=1).reshape(n_k * run, hd)


def query_codes(qp_ref, d, run):
    rows = (qp_ref.shape[1] - META) // 2
    meta = qp_ref[d, 2 * rows : 2 * rows + META, :].astype(jnp.float32)
    tok = (lax.broadcasted_iota(jnp.int32, (1, rows), 1) % run).astype(jnp.float32)
    base = meta[0:1] * DOC_STEP
    return base, base + meta[1:2] * (run * 16.0) + meta[2:3] * float(run) + tok


def stats_kernel(side_ref, qp_ref, kp_ref, out_ref, e_ref, dp_ref, top_ref, code_ref):
    n_q, block, hd = qp_ref.shape
    _, n_k, kp_rows, _ = kp_ref.shape
    rows = (block - META) // 2
    run = (kp_rows - META) // 2
    scale = 1.0 / math.sqrt(hd)
    half = n_k * run
    per = CHUNK // run
    cores = (side_ref[0], 1 - side_ref[0])
    for i, core in enumerate(cores):
        code_ref[i * half : (i + 1) * half, :] = key_codes(kp_ref.at[core], run)
    for d in range(0, n_q, 2):
        q = qp_ref[d : d + 2, 0:rows, :].reshape(2 * rows, hd)
        g = qp_ref[d : d + 2, rows : 2 * rows, :].reshape(2 * rows, hd)
        pairs = [query_codes(qp_ref, d + i, run) for i in range(2)]
        base = jnp.concatenate([p[0] for p in pairs], axis=1)
        top = jnp.concatenate([p[1] for p in pairs], axis=1)
        cols = slice(d * rows, (d + 2) * rows)
        sums = []
        for c in range(2 * half // CHUNK):
            core, at = cores[c * CHUNK // half], (c * CHUNK % half) // run
            at_c = slice(c * CHUNK, (c + 1) * CHUNK)
            k = kp_ref[core, at : at + per, 0:run, :].reshape(CHUNK, hd)
            v = kp_ref[core, at : at + per, run : 2 * run, :].reshape(CHUNK, hd)
            code = jnp.concatenate([code_ref[at_c, :]] * (2 * rows // hd), axis=1)
            seen = (code <= top) & (code >= base)
            s = jnp.where(seen, dot_rows(k, q) * scale, LOW)
            high = jnp.maximum(jnp.max(s, axis=0, keepdims=True), FLOOR)
            e = jnp.exp(s - high)
            e_ref[at_c, cols] = e
            dp = dot_rows(v, g)
            dp_ref[at_c, cols] = dp
            top_ref[c : c + 1, cols] = high
            sums.append((high, jnp.sum(e, axis=0, keepdims=True), jnp.sum(e * dp, axis=0, keepdims=True)))
        high = functools.reduce(jnp.maximum, [x[0] for x in sums])
        share = [jnp.exp(x[0] - high) for x in sums]
        total = sum(f * x[1] for f, x in zip(share, sums))
        cross = sum(f * x[2] for f, x in zip(share, sums))
        some = total > 0.0
        safe = jnp.where(some, total, 1.0)
        log_total = jnp.where(some, high + jnp.log(safe), LOW)
        row_dot = jnp.where(some, cross / safe, 0.0)
        for i in range(2):
            lo, hi = i * rows, (i + 1) * rows
            for to in range(n_q):
                out_ref[to, d + i : d + i + 1, :] = log_total[:, lo:hi]
                out_ref[to, n_q + d + i : n_q + d + i + 1, :] = row_dot[:, lo:hi]


def grads_kernel(
    side_ref, qp_ref, kp_ref, st_ref, e_ref, dp_ref, top_ref, gq_hbm, keep_ref, give_ref, log_ref, dot_ref, ds_ref, gq_ref, sem
):
    n_q, block, hd = qp_ref.shape
    n_k, twice, _ = keep_ref.shape
    run = twice // 2
    rows = (block - META) // 2
    scale = 1.0 / math.sqrt(hd)
    half = n_k * run
    cores = (side_ref[0], 1 - side_ref[0])
    logs = st_ref[:, 0:n_q, :]
    high = jnp.max(logs, axis=0)
    log_total = high + jnp.log(jnp.sum(jnp.exp(logs - high[None]), axis=0))
    log_ref[...] = log_total
    dot_ref[...] = jnp.sum(jnp.exp(logs - log_total[None]) * st_ref[:, n_q:, :], axis=0)
    gv = [jnp.zeros((half, hd), jnp.float32) for _ in cores]
    for d in range(0, n_q, 2):
        g = qp_ref[d : d + 2, rows : 2 * rows, :].reshape(2 * rows, hd)
        log_row = jnp.concatenate([log_ref[d + i : d + i + 1, :] for i in range(2)], axis=1)
        dot_row = jnp.concatenate([dot_ref[d + i : d + i + 1, :] for i in range(2)], axis=1)
        cols = slice(d * rows, (d + 2) * rows)
        gq = jnp.zeros((2 * rows, hd), jnp.float32)
        for i, core in enumerate(cores):
            parts = []
            for c in range(i * half // CHUNK, (i + 1) * half // CHUNK):
                at_c = slice(c * CHUNK, (c + 1) * CHUNK)
                w = e_ref[at_c, cols] * jnp.exp(top_ref[c : c + 1, cols] - log_row)
                ds_ref[at_c, cols] = (w * (dp_ref[at_c, cols] - dot_row)).astype(jnp.bfloat16)
                parts.append(w.astype(jnp.bfloat16))
            gv[i] = gv[i] + dot_plain(jnp.concatenate(parts, axis=0), g)
            k = kp_ref[core, :, 0:run, :].reshape(half, hd)
            gq = gq + dot_cols(ds_ref[i * half : (i + 1) * half, cols], k)
        gq_ref[d : d + 2] = (gq * scale).reshape(2, rows, hd).astype(gq_ref.dtype)
    out = pltpu.make_async_copy(gq_ref, gq_hbm, sem.at[0])
    out.start()
    for i, ref in enumerate((keep_ref, give_ref)):
        gk = jnp.zeros((half, hd), jnp.float32)
        for d in range(0, n_q, 2):
            q = qp_ref[d : d + 2, 0:rows, :].reshape(2 * rows, hd)
            gk = gk + dot_plain(ds_ref[i * half : (i + 1) * half, d * rows : (d + 2) * rows], q)
        ref[:, 0:run, :] = (gk * scale).reshape(n_k, run, hd).astype(ref.dtype)
        ref[:, run:, :] = gv[i].reshape(n_k, run, hd).astype(ref.dtype)
    out.wait()


def finish_kernel(gq_ref, gkv_ref, oq_ref, ok_ref, ov_ref):
    run, hd = ok_ref.shape
    gq = jnp.sum(gq_ref[...].astype(jnp.float32), axis=0)
    for h in range(oq_ref.shape[1] // hd):
        oq_ref[:, h * hd : (h + 1) * hd] = gq[h * run : (h + 1) * run, :]
    gkv = jnp.sum(gkv_ref[...].astype(jnp.float32), axis=0)
    ok_ref[...] = gkv[:run]
    ov_ref[...] = gkv[run:]


VMEM = pl.BlockSpec(memory_space=pltpu.VMEM)
SMEM = pl.BlockSpec(memory_space=pltpu.SMEM)
HBM = pl.BlockSpec(memory_space=pltpu.HBM)


def call(kernel, in_specs, outs, scratch=(), grant=16 * 1024 * 1024, cost=0, out_specs=None):
    return pl.pallas_call(
        kernel,
        in_specs=in_specs,
        out_specs=out_specs or [VMEM] * len(outs),
        out_shape=outs,
        scratch_shapes=list(scratch),
        cost_estimate=pl.CostEstimate(flops=cost, bytes_accessed=0, transcendentals=0) if cost else None,
        compiler_params=pltpu.CompilerParams(vmem_limit_bytes=grant),
    )


def on_device(queries, key_vecs, value_vecs, out_grad, positions, documents):
    n_q, n_k = lax.axis_size("x") * 2, lax.axis_size("far")
    run, hd = key_vecs.shape
    heads = queries.shape[1] // hd
    rows = run * heads
    bf, f32 = jnp.bfloat16, jnp.float32
    keys = n_k * run
    struct = jax.ShapeDtypeStruct

    def swap(x, axis):
        return lax.all_to_all(x, axis, split_axis=0, concat_axis=0, tiled=True)

    side = lax.axis_index("core").astype(jnp.int32).reshape(1)
    def pack(kernel, shape, *args, cost=0):
        (packed,) = call(
            kernel,
            [HBM] * len(args),
            [pltpu.HBM(shape, bf)],
            [(pltpu.SMEM if a.ndim == 1 else pltpu.VMEM)(a.shape, a.dtype) for a in args]
            + [pltpu.SemaphoreType.DMA((len(args),)), pltpu.VMEM(shape, bf), pltpu.SemaphoreType.DMA((1,))],
            out_specs=[HBM],
            cost=cost,
        )(*(pltpu.with_memory_space_constraint(a, pltpu.HBM) for a in args))
        return packed

    kp = pack(pack_keys_kernel, (n_k, 2 * run + META, hd), positions, documents, key_vecs, value_vecs)
    q_shape = (1, 2 * rows + META, hd)
    qp = pack(pack_queries_kernel, q_shape, positions, documents, queries, out_grad, cost=10**9)
    kp = swap(kp, "far")
    qp = lax.all_gather(qp, "near", axis=0, tiled=True)
    qp = jnp.broadcast_to(qp[None], (n_q // 2, *qp.shape))
    qp, kp = lax.optimization_barrier((qp, kp))
    qp = swap(qp, "x").reshape(n_q, 2 * rows + META, hd)
    kp = lax.all_gather(kp, "core", axis=0, tiled=False)
    full = struct((2 * keys, n_q * rows), f32)
    line = pltpu.VMEM((n_q, rows), f32)
    st, e, dp, top = call(
        stats_kernel,
        [SMEM] + [VMEM] * 2,
        [struct((n_q, 2 * n_q, rows), f32), full, full, struct((2 * keys // CHUNK, n_q * rows), f32)],
        [pltpu.VMEM((2 * keys, hd), f32)],
    )(side, qp, kp)
    st = swap(st, ("x", "near"))
    gq, keep, give = call(
        grads_kernel,
        [SMEM] + [VMEM] * 6,
        [pltpu.HBM((n_q, rows, hd), bf), struct((n_k, 2 * run, hd), f32), struct((n_k, 2 * run, hd), bf)],
        [line, line, pltpu.VMEM(full.shape, bf), pltpu.VMEM((n_q, rows, hd), bf), pltpu.SemaphoreType.DMA((1,))],
        out_specs=[HBM, VMEM, VMEM],
    )(side, qp, kp, st, e, dp, top)
    gq = swap(gq, ("x", "near"))
    both = lax.all_gather(give, "core", axis=0, tiled=False)
    gkv = (keep + jnp.where(side[0] == 0, both[1], both[0]).astype(f32)).astype(bf)
    gkv, gq = lax.optimization_barrier((gkv, gq))
    gkv = swap(gkv, "far")
    return tuple(
        call(
            finish_kernel,
            [VMEM] * 2,
            [struct((run, heads * hd), f32), struct((run, hd), f32), struct((run, hd), f32)],
        )(gq, gkv)
    )


def solution(mesh):
    n_head, n_ctx = mesh.devices.shape
    every = ("x", "near", "far", "core")
    fine = Mesh(mesh.devices.reshape(n_head // 2, 2, n_ctx // 2, 2), every)
    tok, two = P(every), P(every, None)
    return jax.shard_map(
        on_device,
        mesh=fine,
        in_specs=(two, two, two, two, tok, tok),
        out_specs=(two, two, two),
        check_vma=False,
    )
```

```python
import functools
import math

import jax
import jax.numpy as jnp
from jax import lax
from jax.experimental import pallas as pl
from jax.experimental.pallas import tpu as pltpu
from jax.sharding import Mesh
from jax.sharding import PartitionSpec as P

LOW = -1e30
FLOOR = -1e29
DOC_STEP = 8192.0
META = 8
CHUNK = 256


def dot_rows(a, b):
    return lax.dot_general(a, b, (((1,), (1,)), ((), ())), preferred_element_type=jnp.float32)


def dot_plain(a, b):
    return lax.dot_general(a, b, (((1,), (0,)), ((), ())), preferred_element_type=jnp.float32)


def dot_cols(a, b):
    return lax.dot_general(a, b, (((0,), (0,)), ((), ())), preferred_element_type=jnp.float32)


def fetch(hbm, bufs, sems):
    copies = [pltpu.make_async_copy(src, dst, sems.at[i]) for i, (src, dst) in enumerate(zip(hbm, bufs))]
    for copy in copies:
        copy.start()
    for copy in copies:
        copy.wait()


def meta_rows(pos_ref, doc_ref, run, tok, item):
    first = pos_ref[0] // run
    docs = jnp.zeros(tok.shape, jnp.int32)
    for t in range(run):
        docs = jnp.where(tok == t, doc_ref[t], docs)
    meta = jnp.where(item == 0, docs, jnp.where(item == 1, first // 16, jnp.where(item == 2, first % 16, 0)))
    return meta.astype(jnp.float32).astype(jnp.bfloat16)


def pack_keys_kernel(pos_any, doc_any, k_any, v_any, kp_hbm, pos_ref, doc_ref, k_ref, v_ref, sems, kp_ref, out_sem):
    fetch((pos_any, doc_any, k_any, v_any), (pos_ref, doc_ref, k_ref, v_ref), sems)
    run, hd = k_ref.shape
    row = lax.broadcasted_iota(jnp.int32, (META, hd), 0)
    lane = lax.broadcasted_iota(jnp.int32, (META, hd), 1)
    half = hd // 2
    meta = meta_rows(pos_ref, doc_ref, run, jnp.where(lane >= half, row + META, row), lane % half)
    k, v = k_ref[...], v_ref[...]
    for d in range(kp_ref.shape[0]):
        kp_ref[d, 0:run, :] = k
        kp_ref[d, run : 2 * run, :] = v
        kp_ref[d, 2 * run : 2 * run + META, :] = meta
    out = pltpu.make_async_copy(kp_ref, kp_hbm, out_sem.at[0])
    out.start()
    out.wait()


def pack_queries_kernel(pos_any, doc_any, q_any, g_any, qp_hbm, pos_ref, doc_ref, q_ref, g_ref, sems, qp_ref, out_sem):
    fetch((pos_any, doc_any, q_any, g_any), (pos_ref, doc_ref, q_ref, g_ref), sems)
    n_q, block, hd = qp_ref.shape
    rows = (block - META) // 2
    run = q_ref.shape[0]
    row = lax.broadcasted_iota(jnp.int32, (META, hd), 0)
    lane = lax.broadcasted_iota(jnp.int32, (META, hd), 1)
    meta = meta_rows(pos_ref, doc_ref, run, lane % run, row)
    for h in range(rows // run):
        q_h = q_ref[:, h * hd : (h + 1) * hd]
        g_h = g_ref[:, h * hd : (h + 1) * hd]
        for d in range(n_q):
            qp_ref[d, h * run : (h + 1) * run, :] = q_h
            qp_ref[d, rows + h * run : rows + (h + 1) * run, :] = g_h
    for d in range(n_q):
        qp_ref[d, 2 * rows : 2 * rows + META, :] = meta
    out = pltpu.make_async_copy(qp_ref, qp_hbm, out_sem.at[0])
    out.start()
    out.wait()


def key_codes(kp, run):
    n_k, _, hd = kp.shape
    meta = kp[:, 2 * run : 2 * run + META, :].astype(jnp.float32).reshape(n_k * META, hd)
    src = lax.broadcasted_iota(jnp.int32, (hd, 2 * hd), 0)
    dst = lax.broadcasted_iota(jnp.int32, (hd, 2 * hd), 1)
    half = hd // 2
    item = src % half
    weight = jnp.where(
        item == 0, DOC_STEP, jnp.where(item == 1, run * 16.0, jnp.where(item == 2, run * 1.0, 0.0))
    )
    weight = jnp.where((src >= half) == (dst >= hd), weight, 0.0)
    codes = dot_plain(meta.astype(jnp.bfloat16), weight.astype(jnp.bfloat16))
    tok = lax.broadcasted_iota(jnp.int32, (n_k, META, hd), 1).astype(jnp.float32)
    lower = codes[:, :hd].reshape(n_k, META, hd) + tok
    upper = codes[:, hd:].reshape(n_k, META, hd) + (tok + META)
    return jnp.concatenate([lower, upper], axis=1).reshape(n_k * run, hd)


def query_codes(qp_ref, d, run):
    rows = (qp_ref.shape[1] - META) // 2
    meta = qp_ref[d, 2 * rows : 2 * rows + META, :].astype(jnp.float32)
    tok = (lax.broadcasted_iota(jnp.int32, (1, rows), 1) % run).astype(jnp.float32)
    base = meta[0:1] * DOC_STEP
    return base, base + meta[1:2] * (run * 16.0) + meta[2:3] * float(run) + tok


def codes_kernel(side_ref, kp_ref, code_ref):
    run = (kp_ref.shape[2] - META) // 2
    half = kp_ref.shape[1] * run
    for i, core in enumerate((side_ref[0], 1 - side_ref[0])):
        code_ref[i * half : (i + 1) * half, :] = key_codes(kp_ref.at[core], run)


def stats_kernel(side_ref, qp_ref, kp_ref, code_ref, out_ref, e_ref, dp_ref, top_ref):
    n_q, block, hd = qp_ref.shape
    _, n_k, kp_rows, _ = kp_ref.shape
    rows = (block - META) // 2
    run = (kp_rows - META) // 2
    scale = 1.0 / math.sqrt(hd)
    half = n_k * run
    per = CHUNK // run
    cores = (side_ref[0], 1 - side_ref[0])
    for d in range(0, n_q, 2):
        q = qp_ref[d : d + 2, 0:rows, :].reshape(2 * rows, hd)
        g = qp_ref[d : d + 2, rows : 2 * rows, :].reshape(2 * rows, hd)
        pairs = [query_codes(qp_ref, d + i, run) for i in range(2)]
        base = jnp.concatenate([p[0] for p in pairs], axis=1)
        top = jnp.concatenate([p[1] for p in pairs], axis=1)
        cols = slice(d * rows, (d + 2) * rows)
        sums = []
        for c in range(2 * half // CHUNK):
            core, at = cores[c * CHUNK // half], (c * CHUNK % half) // run
            at_c = slice(c * CHUNK, (c + 1) * CHUNK)
            k = kp_ref[core, at : at + per, 0:run, :].reshape(CHUNK, hd)
            v = kp_ref[core, at : at + per, run : 2 * run, :].reshape(CHUNK, hd)
            code = jnp.concatenate([code_ref[at_c, :]] * (2 * rows // hd), axis=1)
            seen = (code <= top) & (code >= base)
            s = jnp.where(seen, dot_rows(k, q) * scale, LOW)
            high = jnp.maximum(jnp.max(s, axis=0, keepdims=True), FLOOR)
            e = jnp.exp(s - high)
            e_ref[at_c, cols] = e
            dp = dot_rows(v, g)
            dp_ref[at_c, cols] = dp
            top_ref[c : c + 1, cols] = high
            sums.append((high, jnp.sum(e, axis=0, keepdims=True), jnp.sum(e * dp, axis=0, keepdims=True)))
        high = functools.reduce(jnp.maximum, [x[0] for x in sums])
        share = [jnp.exp(x[0] - high) for x in sums]
        total = sum(f * x[1] for f, x in zip(share, sums))
        cross = sum(f * x[2] for f, x in zip(share, sums))
        some = total > 0.0
        safe = jnp.where(some, total, 1.0)
        log_total = jnp.where(some, high + jnp.log(safe), LOW)
        row_dot = jnp.where(some, cross / safe, 0.0)
        for i in range(2):
            lo, hi = i * rows, (i + 1) * rows
            for to in range(n_q):
                out_ref[to, d + i : d + i + 1, :] = log_total[:, lo:hi]
                out_ref[to, n_q + d + i : n_q + d + i + 1, :] = row_dot[:, lo:hi]


def grads_kernel(
    side_ref, qp_ref, kp_ref, st_ref, e_ref, dp_ref, top_ref, gq_hbm, keep_ref, give_ref, log_ref, dot_ref, ds_ref, gq_ref, sem
):
    n_q, block, hd = qp_ref.shape
    n_k, twice, _ = keep_ref.shape
    run = twice // 2
    rows = (block - META) // 2
    scale = 1.0 / math.sqrt(hd)
    half = n_k * run
    cores = (side_ref[0], 1 - side_ref[0])
    logs = st_ref[:, 0:n_q, :]
    high = jnp.max(logs, axis=0)
    log_total = high + jnp.log(jnp.sum(jnp.exp(logs - high[None]), axis=0))
    log_ref[...] = log_total
    dot_ref[...] = jnp.sum(jnp.exp(logs - log_total[None]) * st_ref[:, n_q:, :], axis=0)
    gv = [jnp.zeros((half, hd), jnp.float32) for _ in cores]
    for d in range(0, n_q, 2):
        g = qp_ref[d : d + 2, rows : 2 * rows, :].reshape(2 * rows, hd)
        log_row = jnp.concatenate([log_ref[d + i : d + i + 1, :] for i in range(2)], axis=1)
        dot_row = jnp.concatenate([dot_ref[d + i : d + i + 1, :] for i in range(2)], axis=1)
        cols = slice(d * rows, (d + 2) * rows)
        gq = jnp.zeros((2 * rows, hd), jnp.float32)
        for i, core in enumerate(cores):
            parts = []
            for c in range(i * half // CHUNK, (i + 1) * half // CHUNK):
                at_c = slice(c * CHUNK, (c + 1) * CHUNK)
                w = e_ref[at_c, cols] * jnp.exp(top_ref[c : c + 1, cols] - log_row)
                ds_ref[at_c, cols] = (w * (dp_ref[at_c, cols] - dot_row)).astype(jnp.bfloat16)
                parts.append(w.astype(jnp.bfloat16))
            gv[i] = gv[i] + dot_plain(jnp.concatenate(parts, axis=0), g)
            k = kp_ref[core, :, 0:run, :].reshape(half, hd)
            gq = gq + dot_cols(ds_ref[i * half : (i + 1) * half, cols], k)
        gq_ref[d : d + 2] = (gq * scale).reshape(2, rows, hd).astype(gq_ref.dtype)
    out = pltpu.make_async_copy(gq_ref, gq_hbm, sem.at[0])
    out.start()
    for i, ref in enumerate((keep_ref, give_ref)):
        gk = jnp.zeros((half, hd), jnp.float32)
        for d in range(0, n_q, 2):
            q = qp_ref[d : d + 2, 0:rows, :].reshape(2 * rows, hd)
            gk = gk + dot_plain(ds_ref[i * half : (i + 1) * half, d * rows : (d + 2) * rows], q)
        ref[:, 0:run, :] = (gk * scale).reshape(n_k, run, hd).astype(ref.dtype)
        ref[:, run:, :] = gv[i].reshape(n_k, run, hd).astype(ref.dtype)
    out.wait()


def finish_kernel(gq_ref, gkv_ref, oq_ref, ok_ref, ov_ref):
    run, hd = ok_ref.shape
    gq = jnp.sum(gq_ref[...].astype(jnp.float32), axis=0)
    for h in range(oq_ref.shape[1] // hd):
        oq_ref[:, h * hd : (h + 1) * hd] = gq[h * run : (h + 1) * run, :]
    gkv = jnp.sum(gkv_ref[...].astype(jnp.float32), axis=0)
    ok_ref[...] = gkv[:run]
    ov_ref[...] = gkv[run:]


VMEM = pl.BlockSpec(memory_space=pltpu.VMEM)
SMEM = pl.BlockSpec(memory_space=pltpu.SMEM)
HBM = pl.BlockSpec(memory_space=pltpu.HBM)


def call(kernel, in_specs, outs, scratch=(), grant=16 * 1024 * 1024, cost=0, out_specs=None):
    return pl.pallas_call(
        kernel,
        in_specs=in_specs,
        out_specs=out_specs or [VMEM] * len(outs),
        out_shape=outs,
        scratch_shapes=list(scratch),
        cost_estimate=pl.CostEstimate(flops=cost, bytes_accessed=0, transcendentals=0) if cost else None,
        compiler_params=pltpu.CompilerParams(vmem_limit_bytes=grant),
    )


def on_device(queries, key_vecs, value_vecs, out_grad, positions, documents):
    n_q, n_k = lax.axis_size("head"), lax.axis_size("far")
    run, hd = key_vecs.shape
    heads = queries.shape[1] // hd
    rows = run * heads
    bf, f32 = jnp.bfloat16, jnp.float32
    keys = n_k * run
    struct = jax.ShapeDtypeStruct

    def swap(x, axis):
        return lax.all_to_all(x, axis, split_axis=0, concat_axis=0, tiled=True)

    side = lax.axis_index("core").astype(jnp.int32).reshape(1)
    def pack(kernel, shape, *args, cost=0):
        (packed,) = call(
            kernel,
            [HBM] * len(args),
            [pltpu.HBM(shape, bf)],
            [(pltpu.SMEM if a.ndim == 1 else pltpu.VMEM)(a.shape, a.dtype) for a in args]
            + [pltpu.SemaphoreType.DMA((len(args),)), pltpu.VMEM(shape, bf), pltpu.SemaphoreType.DMA((1,))],
            out_specs=[HBM],
            cost=cost,
        )(*(pltpu.with_memory_space_constraint(a, pltpu.HBM) for a in args))
        return packed

    kp = pack(pack_keys_kernel, (n_k, 2 * run + META, hd), positions, documents, key_vecs, value_vecs)
    q_shape = (n_q, 2 * rows + META, hd)
    qp = pack(pack_queries_kernel, q_shape, positions, documents, queries, out_grad, cost=10**9)
    kp = swap(kp, "far")
    qp, kp = lax.optimization_barrier((qp, kp))
    qp = swap(qp, "head")
    kp = lax.all_gather(kp, "core", axis=0, tiled=False)
    (code,) = call(codes_kernel, [SMEM, VMEM], [struct((2 * keys, hd), f32)])(side, kp)
    full = struct((2 * keys, n_q * rows), f32)
    line = pltpu.VMEM((n_q, rows), f32)
    st, e, dp, top = call(
        stats_kernel,
        [SMEM] + [VMEM] * 3,
        [struct((n_q, 2 * n_q, rows), f32), full, full, struct((2 * keys // CHUNK, n_q * rows), f32)],
    )(side, qp, kp, code)
    st = swap(st, "head")
    gq, keep, give = call(
        grads_kernel,
        [SMEM] + [VMEM] * 6,
        [pltpu.HBM((n_q, rows, hd), bf), struct((n_k, 2 * run, hd), f32), struct((n_k, 2 * run, hd), bf)],
        [line, line, pltpu.VMEM(full.shape, bf), pltpu.VMEM((n_q, rows, hd), bf), pltpu.SemaphoreType.DMA((1,))],
        out_specs=[HBM, VMEM, VMEM],
    )(side, qp, kp, st, e, dp, top)
    gq = swap(gq, "head")
    both = lax.all_gather(give, "core", axis=0, tiled=False)
    gkv = (keep + jnp.where(side[0] == 0, both[1], both[0]).astype(f32)).astype(bf)
    gkv, gq = lax.optimization_barrier((gkv, gq))
    gkv = swap(gkv, "far")
    return tuple(
        call(
            finish_kernel,
            [VMEM] * 2,
            [struct((run, heads * hd), f32), struct((run, hd), f32), struct((run, hd), f32)],
        )(gq, gkv)
    )


def solution(mesh):
    n_head, n_ctx = mesh.devices.shape
    fine = Mesh(mesh.devices.reshape(n_head, n_ctx // 2, 2), ("head", "far", "core"))
    tok = P(("head", "far", "core"))
    two = P(("head", "far", "core"), None)
    return jax.shard_map(
        on_device,
        mesh=fine,
        in_specs=(two, two, two, two, tok, tok),
        out_specs=(two, two, two),
        check_vma=False,
    )
```

```python
import functools
import math

import jax
import jax.numpy as jnp
from jax import lax
from jax.experimental import pallas as pl
from jax.experimental.pallas import tpu as pltpu
from jax.sharding import Mesh
from jax.sharding import PartitionSpec as P

LOW = -1e30
FLOOR = -1e29
DOC_STEP = 8192.0
META = 8
CHUNK = 256


def dot_rows(a, b):
    return lax.dot_general(a, b, (((1,), (1,)), ((), ())), preferred_element_type=jnp.float32)


def dot_plain(a, b):
    return lax.dot_general(a, b, (((1,), (0,)), ((), ())), preferred_element_type=jnp.float32)


def dot_cols(a, b):
    return lax.dot_general(a, b, (((0,), (0,)), ((), ())), preferred_element_type=jnp.float32)


def fetch(hbm, bufs, sems):
    copies = [pltpu.make_async_copy(src, dst, sems.at[i]) for i, (src, dst) in enumerate(zip(hbm, bufs))]
    for copy in copies:
        copy.start()
    for copy in copies:
        copy.wait()


def meta_rows(pos_ref, doc_ref, run, tok, item):
    first = pos_ref[0] // run
    docs = jnp.zeros(tok.shape, jnp.int32)
    for t in range(run):
        docs = jnp.where(tok == t, doc_ref[t], docs)
    meta = jnp.where(item == 0, docs, jnp.where(item == 1, first // 16, jnp.where(item == 2, first % 16, 0)))
    return meta.astype(jnp.float32).astype(jnp.bfloat16)


def pack_keys_kernel(pos_any, doc_any, k_any, v_any, kp_hbm, pos_ref, doc_ref, k_ref, v_ref, sems, kp_ref, out_sem):
    fetch((pos_any, doc_any, k_any, v_any), (pos_ref, doc_ref, k_ref, v_ref), sems)
    run, hd = k_ref.shape
    row = lax.broadcasted_iota(jnp.int32, (META, hd), 0)
    lane = lax.broadcasted_iota(jnp.int32, (META, hd), 1)
    half = hd // 2
    meta = meta_rows(pos_ref, doc_ref, run, jnp.where(lane >= half, row + META, row), lane % half)
    k, v = k_ref[...], v_ref[...]
    for d in range(kp_ref.shape[0]):
        kp_ref[d, 0:run, :] = k
        kp_ref[d, run : 2 * run, :] = v
        kp_ref[d, 2 * run : 2 * run + META, :] = meta
    out = pltpu.make_async_copy(kp_ref, kp_hbm, out_sem.at[0])
    out.start()
    out.wait()


def pack_queries_kernel(pos_any, doc_any, q_any, g_any, qp_hbm, pos_ref, doc_ref, q_ref, g_ref, sems, qp_ref, out_sem):
    fetch((pos_any, doc_any, q_any, g_any), (pos_ref, doc_ref, q_ref, g_ref), sems)
    n_q, block, hd = qp_ref.shape
    rows = (block - META) // 2
    run = q_ref.shape[0]
    row = lax.broadcasted_iota(jnp.int32, (META, hd), 0)
    lane = lax.broadcasted_iota(jnp.int32, (META, hd), 1)
    meta = meta_rows(pos_ref, doc_ref, run, lane % run, row)
    for h in range(rows // run):
        q_h = q_ref[:, h * hd : (h + 1) * hd]
        g_h = g_ref[:, h * hd : (h + 1) * hd]
        for d in range(n_q):
            qp_ref[d, h * run : (h + 1) * run, :] = q_h
            qp_ref[d, rows + h * run : rows + (h + 1) * run, :] = g_h
    for d in range(n_q):
        qp_ref[d, 2 * rows : 2 * rows + META, :] = meta
    out = pltpu.make_async_copy(qp_ref, qp_hbm, out_sem.at[0])
    out.start()
    out.wait()


def key_codes(kp, run):
    n_k, _, hd = kp.shape
    meta = kp[:, 2 * run : 2 * run + META, :].astype(jnp.float32).reshape(n_k * META, hd)
    src = lax.broadcasted_iota(jnp.int32, (hd, 2 * hd), 0)
    dst = lax.broadcasted_iota(jnp.int32, (hd, 2 * hd), 1)
    half = hd // 2
    item = src % half
    weight = jnp.where(
        item == 0, DOC_STEP, jnp.where(item == 1, run * 16.0, jnp.where(item == 2, run * 1.0, 0.0))
    )
    weight = jnp.where((src >= half) == (dst >= hd), weight, 0.0)
    codes = dot_plain(meta.astype(jnp.bfloat16), weight.astype(jnp.bfloat16))
    tok = lax.broadcasted_iota(jnp.int32, (n_k, META, hd), 1).astype(jnp.float32)
    lower = codes[:, :hd].reshape(n_k, META, hd) + tok
    upper = codes[:, hd:].reshape(n_k, META, hd) + (tok + META)
    return jnp.concatenate([lower, upper], axis=1).reshape(n_k * run, hd)


def query_codes(qp_ref, d, run):
    rows = (qp_ref.shape[1] - META) // 2
    meta = qp_ref[d, 2 * rows : 2 * rows + META, :].astype(jnp.float32)
    tok = (lax.broadcasted_iota(jnp.int32, (1, rows), 1) % run).astype(jnp.float32)
    base = meta[0:1] * DOC_STEP
    return base, base + meta[1:2] * (run * 16.0) + meta[2:3] * float(run) + tok


def stats_kernel(side_ref, qp_ref, kp_ref, out_ref, e_ref, dp_ref, top_ref, code_ref):
    n_q, block, hd = qp_ref.shape
    _, n_k, kp_rows, _ = kp_ref.shape
    rows = (block - META) // 2
    run = (kp_rows - META) // 2
    scale = 1.0 / math.sqrt(hd)
    half = n_k * run
    per = CHUNK // run
    cores = (side_ref[0], 1 - side_ref[0])
    for i, core in enumerate(cores):
        code_ref[i * half : (i + 1) * half, :] = key_codes(kp_ref.at[core], run)
    for d in range(0, n_q, 2):
        q = qp_ref[d : d + 2, 0:rows, :].reshape(2 * rows, hd)
        g = qp_ref[d : d + 2, rows : 2 * rows, :].reshape(2 * rows, hd)
        pairs = [query_codes(qp_ref, d + i, run) for i in range(2)]
        base = jnp.concatenate([p[0] for p in pairs], axis=1)
        top = jnp.concatenate([p[1] for p in pairs], axis=1)
        cols = slice(d * rows, (d + 2) * rows)
        sums = []
        for c in range(2 * half // CHUNK):
            core, at = cores[c * CHUNK // half], (c * CHUNK % half) // run
            at_c = slice(c * CHUNK, (c + 1) * CHUNK)
            k = kp_ref[core, at : at + per, 0:run, :].reshape(CHUNK, hd)
            v = kp_ref[core, at : at + per, run : 2 * run, :].reshape(CHUNK, hd)
            code = jnp.concatenate([code_ref[at_c, :]] * (2 * rows // hd), axis=1)
            seen = (code <= top) & (code >= base)
            s = jnp.where(seen, dot_rows(k, q) * scale, LOW)
            high = jnp.maximum(jnp.max(s, axis=0, keepdims=True), FLOOR)
            e = jnp.exp(s - high)
            e_ref[at_c, cols] = e
            dp = dot_rows(v, g)
            dp_ref[at_c, cols] = dp
            top_ref[c : c + 1, cols] = high
            sums.append((high, jnp.sum(e, axis=0, keepdims=True), jnp.sum(e * dp, axis=0, keepdims=True)))
        high = functools.reduce(jnp.maximum, [x[0] for x in sums])
        share = [jnp.exp(x[0] - high) for x in sums]
        total = sum(f * x[1] for f, x in zip(share, sums))
        cross = sum(f * x[2] for f, x in zip(share, sums))
        some = total > 0.0
        safe = jnp.where(some, total, 1.0)
        log_total = jnp.where(some, high + jnp.log(safe), LOW)
        row_dot = jnp.where(some, cross / safe, 0.0)
        for i in range(2):
            lo, hi = i * rows, (i + 1) * rows
            for to in range(n_q):
                out_ref[to, d + i : d + i + 1, :] = log_total[:, lo:hi]
                out_ref[to, n_q + d + i : n_q + d + i + 1, :] = row_dot[:, lo:hi]


def grads_kernel(
    side_ref, qp_ref, kp_ref, st_ref, e_ref, dp_ref, top_ref, gq_hbm, keep_ref, give_ref, log_ref, dot_ref, ds_ref, gq_ref, sem
):
    n_q, block, hd = qp_ref.shape
    n_k, twice, _ = keep_ref.shape
    run = twice // 2
    rows = (block - META) // 2
    scale = 1.0 / math.sqrt(hd)
    half = n_k * run
    cores = (side_ref[0], 1 - side_ref[0])
    logs = st_ref[:, 0:n_q, :]
    high = jnp.max(logs, axis=0)
    log_total = high + jnp.log(jnp.sum(jnp.exp(logs - high[None]), axis=0))
    log_ref[...] = log_total
    dot_ref[...] = jnp.sum(jnp.exp(logs - log_total[None]) * st_ref[:, n_q:, :], axis=0)
    gv = [jnp.zeros((half, hd), jnp.float32) for _ in cores]
    for d in range(0, n_q, 2):
        g = qp_ref[d : d + 2, rows : 2 * rows, :].reshape(2 * rows, hd)
        log_row = jnp.concatenate([log_ref[d + i : d + i + 1, :] for i in range(2)], axis=1)
        dot_row = jnp.concatenate([dot_ref[d + i : d + i + 1, :] for i in range(2)], axis=1)
        cols = slice(d * rows, (d + 2) * rows)
        gq = jnp.zeros((2 * rows, hd), jnp.float32)
        for i, core in enumerate(cores):
            parts = []
            for c in range(i * half // CHUNK, (i + 1) * half // CHUNK):
                at_c = slice(c * CHUNK, (c + 1) * CHUNK)
                w = e_ref[at_c, cols] * jnp.exp(top_ref[c : c + 1, cols] - log_row)
                ds_ref[at_c, cols] = (w * (dp_ref[at_c, cols] - dot_row)).astype(jnp.bfloat16)
                parts.append(w.astype(jnp.bfloat16))
            gv[i] = gv[i] + dot_plain(jnp.concatenate(parts, axis=0), g)
            k = kp_ref[core, :, 0:run, :].reshape(half, hd)
            gq = gq + dot_cols(ds_ref[i * half : (i + 1) * half, cols], k)
        gq_ref[d : d + 2] = (gq * scale).reshape(2, rows, hd).astype(gq_ref.dtype)
    out = pltpu.make_async_copy(gq_ref, gq_hbm, sem.at[0])
    out.start()
    for i, ref in enumerate((keep_ref, give_ref)):
        gk = jnp.zeros((half, hd), jnp.float32)
        for d in range(0, n_q, 2):
            q = qp_ref[d : d + 2, 0:rows, :].reshape(2 * rows, hd)
            gk = gk + dot_plain(ds_ref[i * half : (i + 1) * half, d * rows : (d + 2) * rows], q)
        ref[:, 0:run, :] = (gk * scale).reshape(n_k, run, hd).astype(ref.dtype)
        ref[:, run:, :] = gv[i].reshape(n_k, run, hd).astype(ref.dtype)
    out.wait()


def finish_queries_kernel(gq_ref, oq_ref):
    run = gq_ref.shape[1] * gq_ref.shape[2] // oq_ref.shape[1]
    hd = gq_ref.shape[2]
    gq = jnp.sum(gq_ref[...].astype(jnp.float32), axis=0)
    for h in range(oq_ref.shape[1] // hd):
        oq_ref[:, h * hd : (h + 1) * hd] = gq[h * run : (h + 1) * run, :]


def finish_keys_kernel(gkv_ref, ok_ref, ov_ref):
    run = ok_ref.shape[0]
    gkv = jnp.sum(gkv_ref[...].astype(jnp.float32), axis=0)
    ok_ref[...] = gkv[:run]
    ov_ref[...] = gkv[run:]


VMEM = pl.BlockSpec(memory_space=pltpu.VMEM)
SMEM = pl.BlockSpec(memory_space=pltpu.SMEM)
HBM = pl.BlockSpec(memory_space=pltpu.HBM)


def call(kernel, in_specs, outs, scratch=(), grant=16 * 1024 * 1024, cost=0, out_specs=None):
    return pl.pallas_call(
        kernel,
        in_specs=in_specs,
        out_specs=out_specs or [VMEM] * len(outs),
        out_shape=outs,
        scratch_shapes=list(scratch),
        cost_estimate=pl.CostEstimate(flops=cost, bytes_accessed=0, transcendentals=0) if cost else None,
        compiler_params=pltpu.CompilerParams(vmem_limit_bytes=grant),
    )


def on_device(queries, key_vecs, value_vecs, out_grad, positions, documents):
    n_q, n_k = lax.axis_size("head"), lax.axis_size("far")
    run, hd = key_vecs.shape
    heads = queries.shape[1] // hd
    rows = run * heads
    bf, f32 = jnp.bfloat16, jnp.float32
    keys = n_k * run
    struct = jax.ShapeDtypeStruct

    def swap(x, axis):
        return lax.all_to_all(x, axis, split_axis=0, concat_axis=0, tiled=True)

    side = lax.axis_index("core").astype(jnp.int32).reshape(1)
    def pack(kernel, shape, *args, cost=0):
        (packed,) = call(
            kernel,
            [HBM] * len(args),
            [pltpu.HBM(shape, bf)],
            [(pltpu.SMEM if a.ndim == 1 else pltpu.VMEM)(a.shape, a.dtype) for a in args]
            + [pltpu.SemaphoreType.DMA((len(args),)), pltpu.VMEM(shape, bf), pltpu.SemaphoreType.DMA((1,))],
            out_specs=[HBM],
            cost=cost,
        )(*(pltpu.with_memory_space_constraint(a, pltpu.HBM) for a in args))
        return packed

    kp = pack(pack_keys_kernel, (n_k, 2 * run + META, hd), positions, documents, key_vecs, value_vecs)
    q_shape = (n_q, 2 * rows + META, hd)
    qp = pack(pack_queries_kernel, q_shape, positions, documents, queries, out_grad, cost=10**9)
    kp = swap(kp, "far")
    qp, kp = lax.optimization_barrier((qp, kp))
    qp = swap(qp, "head")
    kp = lax.all_gather(kp, "core", axis=0, tiled=False)
    full = struct((2 * keys, n_q * rows), f32)
    line = pltpu.VMEM((n_q, rows), f32)
    st, e, dp, top = call(
        stats_kernel,
        [SMEM] + [VMEM] * 2,
        [struct((n_q, 2 * n_q, rows), f32), full, full, struct((2 * keys // CHUNK, n_q * rows), f32)],
        [pltpu.VMEM((2 * keys, hd), f32)],
    )(side, qp, kp)
    st = swap(st, "head")
    gq, keep, give = call(
        grads_kernel,
        [SMEM] + [VMEM] * 6,
        [pltpu.HBM((n_q, rows, hd), bf), struct((n_k, 2 * run, hd), f32), struct((n_k, 2 * run, hd), bf)],
        [line, line, pltpu.VMEM(full.shape, bf), pltpu.VMEM((n_q, rows, hd), bf), pltpu.SemaphoreType.DMA((1,))],
        out_specs=[HBM, VMEM, VMEM],
    )(side, qp, kp, st, e, dp, top)
    gq = swap(gq, "head")
    both = lax.all_gather(give, "core", axis=0, tiled=False)
    gkv = (keep + jnp.where(side[0] == 0, both[1], both[0]).astype(f32)).astype(bf)
    gkv, gq = lax.optimization_barrier((gkv, gq))
    gkv = swap(gkv, "far")
    (oq,) = call(finish_queries_kernel, [VMEM], [struct((run, heads * hd), f32)], cost=10**9)(gq)
    ok, ov = call(finish_keys_kernel, [VMEM], [struct((run, hd), f32)] * 2)(gkv)
    return oq, ok, ov


def solution(mesh):
    n_head, n_ctx = mesh.devices.shape
    fine = Mesh(mesh.devices.reshape(n_head, n_ctx // 2, 2), ("head", "far", "core"))
    tok = P(("head", "far", "core"))
    two = P(("head", "far", "core"), None)
    return jax.shard_map(
        on_device,
        mesh=fine,
        in_specs=(two, two, two, two, tok, tok),
        out_specs=(two, two, two),
        check_vma=False,
    )
```

```python
import functools
import math

import jax
import jax.numpy as jnp
from jax import lax
from jax.experimental import pallas as pl
from jax.experimental.pallas import tpu as pltpu
from jax.sharding import Mesh
from jax.sharding import PartitionSpec as P

LOW = -1e30
FLOOR = -1e29
DOC_STEP = 8192.0
META = 8
CHUNK = 128


def dot_rows(a, b):
    return lax.dot_general(a, b, (((1,), (1,)), ((), ())), preferred_element_type=jnp.float32)


def dot_plain(a, b):
    return lax.dot_general(a, b, (((1,), (0,)), ((), ())), preferred_element_type=jnp.float32)


def dot_cols(a, b):
    return lax.dot_general(a, b, (((0,), (0,)), ((), ())), preferred_element_type=jnp.float32)


def fetch(hbm, bufs, sems):
    copies = [pltpu.make_async_copy(src, dst, sems.at[i]) for i, (src, dst) in enumerate(zip(hbm, bufs))]
    for copy in copies:
        copy.start()
    for copy in copies:
        copy.wait()


def meta_rows(pos_ref, doc_ref, run, tok, item):
    first = pos_ref[0] // run
    docs = jnp.zeros(tok.shape, jnp.int32)
    for t in range(run):
        docs = jnp.where(tok == t, doc_ref[t], docs)
    meta = jnp.where(item == 0, docs, jnp.where(item == 1, first // 16, jnp.where(item == 2, first % 16, 0)))
    return meta.astype(jnp.float32).astype(jnp.bfloat16)


def pack_keys_kernel(pos_any, doc_any, k_any, v_any, kp_hbm, pos_ref, doc_ref, k_ref, v_ref, sems, kp_ref, out_sem):
    fetch((pos_any, doc_any, k_any, v_any), (pos_ref, doc_ref, k_ref, v_ref), sems)
    run, hd = k_ref.shape
    row = lax.broadcasted_iota(jnp.int32, (META, hd), 0)
    lane = lax.broadcasted_iota(jnp.int32, (META, hd), 1)
    half = hd // 2
    meta = meta_rows(pos_ref, doc_ref, run, jnp.where(lane >= half, row + META, row), lane % half)
    k, v = k_ref[...], v_ref[...]
    for d in range(kp_ref.shape[0]):
        kp_ref[d, 0:run, :] = k
        kp_ref[d, run : 2 * run, :] = v
        kp_ref[d, 2 * run : 2 * run + META, :] = meta
    out = pltpu.make_async_copy(kp_ref, kp_hbm, out_sem.at[0])
    out.start()
    out.wait()


def pack_queries_kernel(pos_any, doc_any, q_any, g_any, qp_hbm, pos_ref, doc_ref, q_ref, g_ref, sems, qp_ref, out_sem):
    fetch((pos_any, doc_any, q_any, g_any), (pos_ref, doc_ref, q_ref, g_ref), sems)
    n_q, block, hd = qp_ref.shape
    rows = (block - META) // 2
    run = q_ref.shape[0]
    row = lax.broadcasted_iota(jnp.int32, (META, hd), 0)
    lane = lax.broadcasted_iota(jnp.int32, (META, hd), 1)
    meta = meta_rows(pos_ref, doc_ref, run, lane % run, row)
    for h in range(rows // run):
        q_h = q_ref[:, h * hd : (h + 1) * hd]
        g_h = g_ref[:, h * hd : (h + 1) * hd]
        for d in range(n_q):
            qp_ref[d, h * run : (h + 1) * run, :] = q_h
            qp_ref[d, rows + h * run : rows + (h + 1) * run, :] = g_h
    for d in range(n_q):
        qp_ref[d, 2 * rows : 2 * rows + META, :] = meta
    out = pltpu.make_async_copy(qp_ref, qp_hbm, out_sem.at[0])
    out.start()
    out.wait()


def key_codes(kp, run):
    n_k, _, hd = kp.shape
    meta = kp[:, 2 * run : 2 * run + META, :].astype(jnp.float32).reshape(n_k * META, hd)
    src = lax.broadcasted_iota(jnp.int32, (hd, 2 * hd), 0)
    dst = lax.broadcasted_iota(jnp.int32, (hd, 2 * hd), 1)
    half = hd // 2
    item = src % half
    weight = jnp.where(
        item == 0, DOC_STEP, jnp.where(item == 1, run * 16.0, jnp.where(item == 2, run * 1.0, 0.0))
    )
    weight = jnp.where((src >= half) == (dst >= hd), weight, 0.0)
    codes = dot_plain(meta.astype(jnp.bfloat16), weight.astype(jnp.bfloat16))
    tok = lax.broadcasted_iota(jnp.int32, (n_k, META, hd), 1).astype(jnp.float32)
    lower = codes[:, :hd].reshape(n_k, META, hd) + tok
    upper = codes[:, hd:].reshape(n_k, META, hd) + (tok + META)
    return jnp.concatenate([lower, upper], axis=1).reshape(n_k * run, hd)


def query_codes(qp_ref, d, run):
    rows = (qp_ref.shape[1] - META) // 2
    meta = qp_ref[d, 2 * rows : 2 * rows + META, :].astype(jnp.float32)
    tok = (lax.broadcasted_iota(jnp.int32, (1, rows), 1) % run).astype(jnp.float32)
    base = meta[0:1] * DOC_STEP
    return base, base + meta[1:2] * (run * 16.0) + meta[2:3] * float(run) + tok


def stats_kernel(side_ref, qp_ref, kp_ref, out_ref, e_ref, dp_ref, top_ref, code_ref):
    n_q, block, hd = qp_ref.shape
    _, n_k, kp_rows, _ = kp_ref.shape
    rows = (block - META) // 2
    run = (kp_rows - META) // 2
    scale = 1.0 / math.sqrt(hd)
    half = n_k * run
    per = CHUNK // run
    cores = (side_ref[0], 1 - side_ref[0])
    for i, core in enumerate(cores):
        code_ref[i * half : (i + 1) * half, :] = key_codes(kp_ref.at[core], run)
    for d in range(0, n_q, 2):
        q = qp_ref[d : d + 2, 0:rows, :].reshape(2 * rows, hd)
        g = qp_ref[d : d + 2, rows : 2 * rows, :].reshape(2 * rows, hd)
        pairs = [query_codes(qp_ref, d + i, run) for i in range(2)]
        base = jnp.concatenate([p[0] for p in pairs], axis=1)
        top = jnp.concatenate([p[1] for p in pairs], axis=1)
        cols = slice(d * rows, (d + 2) * rows)
        sums = []
        for c in range(2 * half // CHUNK):
            core, at = cores[c * CHUNK // half], (c * CHUNK % half) // run
            at_c = slice(c * CHUNK, (c + 1) * CHUNK)
            k = kp_ref[core, at : at + per, 0:run, :].reshape(CHUNK, hd)
            v = kp_ref[core, at : at + per, run : 2 * run, :].reshape(CHUNK, hd)
            code = jnp.concatenate([code_ref[at_c, :]] * (2 * rows // hd), axis=1)
            seen = (code <= top) & (code >= base)
            s = jnp.where(seen, dot_rows(k, q) * scale, LOW)
            high = jnp.maximum(jnp.max(s, axis=0, keepdims=True), FLOOR)
            e = jnp.exp(s - high)
            e_ref[at_c, cols] = e
            dp = dot_rows(v, g)
            dp_ref[at_c, cols] = dp
            top_ref[c : c + 1, cols] = high
            sums.append((high, jnp.sum(e, axis=0, keepdims=True), jnp.sum(e * dp, axis=0, keepdims=True)))
        high = functools.reduce(jnp.maximum, [x[0] for x in sums])
        share = [jnp.exp(x[0] - high) for x in sums]
        total = sum(f * x[1] for f, x in zip(share, sums))
        cross = sum(f * x[2] for f, x in zip(share, sums))
        some = total > 0.0
        safe = jnp.where(some, total, 1.0)
        log_total = jnp.where(some, high + jnp.log(safe), LOW)
        row_dot = jnp.where(some, cross / safe, 0.0)
        for i in range(2):
            lo, hi = i * rows, (i + 1) * rows
            for to in range(n_q):
                out_ref[to, d + i : d + i + 1, :] = log_total[:, lo:hi]
                out_ref[to, n_q + d + i : n_q + d + i + 1, :] = row_dot[:, lo:hi]


def grads_kernel(
    side_ref, qp_ref, kp_ref, st_ref, e_ref, dp_ref, top_ref, gq_hbm, keep_ref, give_ref, log_ref, dot_ref, ds_ref, gq_ref, sem
):
    n_q, block, hd = qp_ref.shape
    n_k, twice, _ = keep_ref.shape
    run = twice // 2
    rows = (block - META) // 2
    scale = 1.0 / math.sqrt(hd)
    half = n_k * run
    cores = (side_ref[0], 1 - side_ref[0])
    logs = st_ref[:, 0:n_q, :]
    high = jnp.max(logs, axis=0)
    log_total = high + jnp.log(jnp.sum(jnp.exp(logs - high[None]), axis=0))
    log_ref[...] = log_total
    dot_ref[...] = jnp.sum(jnp.exp(logs - log_total[None]) * st_ref[:, n_q:, :], axis=0)
    gv = [jnp.zeros((half, hd), jnp.float32) for _ in cores]
    for d in range(0, n_q, 2):
        g = qp_ref[d : d + 2, rows : 2 * rows, :].reshape(2 * rows, hd)
        log_row = jnp.concatenate([log_ref[d + i : d + i + 1, :] for i in range(2)], axis=1)
        dot_row = jnp.concatenate([dot_ref[d + i : d + i + 1, :] for i in range(2)], axis=1)
        cols = slice(d * rows, (d + 2) * rows)
        gq = jnp.zeros((2 * rows, hd), jnp.float32)
        for i, core in enumerate(cores):
            parts = []
            for c in range(i * half // CHUNK, (i + 1) * half // CHUNK):
                at_c = slice(c * CHUNK, (c + 1) * CHUNK)
                w = e_ref[at_c, cols] * jnp.exp(top_ref[c : c + 1, cols] - log_row)
                ds_ref[at_c, cols] = (w * (dp_ref[at_c, cols] - dot_row)).astype(jnp.bfloat16)
                parts.append(w.astype(jnp.bfloat16))
            gv[i] = gv[i] + dot_plain(jnp.concatenate(parts, axis=0), g)
            k = kp_ref[core, :, 0:run, :].reshape(half, hd)
            gq = gq + dot_cols(ds_ref[i * half : (i + 1) * half, cols], k)
        gq_ref[d : d + 2] = (gq * scale).reshape(2, rows, hd).astype(gq_ref.dtype)
    out = pltpu.make_async_copy(gq_ref, gq_hbm, sem.at[0])
    out.start()
    for i, ref in enumerate((keep_ref, give_ref)):
        gk = jnp.zeros((half, hd), jnp.float32)
        for d in range(0, n_q, 2):
            q = qp_ref[d : d + 2, 0:rows, :].reshape(2 * rows, hd)
            gk = gk + dot_plain(ds_ref[i * half : (i + 1) * half, d * rows : (d + 2) * rows], q)
        ref[:, 0:run, :] = (gk * scale).reshape(n_k, run, hd).astype(ref.dtype)
        ref[:, run:, :] = gv[i].reshape(n_k, run, hd).astype(ref.dtype)
    out.wait()


def finish_kernel(gq_ref, gkv_ref, oq_ref, ok_ref, ov_ref):
    run, hd = ok_ref.shape
    gq = jnp.sum(gq_ref[...].astype(jnp.float32), axis=0)
    for h in range(oq_ref.shape[1] // hd):
        oq_ref[:, h * hd : (h + 1) * hd] = gq[h * run : (h + 1) * run, :]
    gkv = jnp.sum(gkv_ref[...].astype(jnp.float32), axis=0)
    ok_ref[...] = gkv[:run]
    ov_ref[...] = gkv[run:]


VMEM = pl.BlockSpec(memory_space=pltpu.VMEM)
SMEM = pl.BlockSpec(memory_space=pltpu.SMEM)
HBM = pl.BlockSpec(memory_space=pltpu.HBM)


def call(kernel, in_specs, outs, scratch=(), grant=16 * 1024 * 1024, cost=0, out_specs=None):
    return pl.pallas_call(
        kernel,
        in_specs=in_specs,
        out_specs=out_specs or [VMEM] * len(outs),
        out_shape=outs,
        scratch_shapes=list(scratch),
        cost_estimate=pl.CostEstimate(flops=cost, bytes_accessed=0, transcendentals=0) if cost else None,
        compiler_params=pltpu.CompilerParams(vmem_limit_bytes=grant),
    )


def on_device(queries, key_vecs, value_vecs, out_grad, positions, documents):
    n_q, n_k = lax.axis_size("head"), lax.axis_size("far")
    run, hd = key_vecs.shape
    heads = queries.shape[1] // hd
    rows = run * heads
    bf, f32 = jnp.bfloat16, jnp.float32
    keys = n_k * run
    struct = jax.ShapeDtypeStruct

    def swap(x, axis):
        return lax.all_to_all(x, axis, split_axis=0, concat_axis=0, tiled=True)

    side = lax.axis_index("core").astype(jnp.int32).reshape(1)
    def pack(kernel, shape, *args, cost=0):
        (packed,) = call(
            kernel,
            [HBM] * len(args),
            [pltpu.HBM(shape, bf)],
            [(pltpu.SMEM if a.ndim == 1 else pltpu.VMEM)(a.shape, a.dtype) for a in args]
            + [pltpu.SemaphoreType.DMA((len(args),)), pltpu.VMEM(shape, bf), pltpu.SemaphoreType.DMA((1,))],
            out_specs=[HBM],
            cost=cost,
        )(*(pltpu.with_memory_space_constraint(a, pltpu.HBM) for a in args))
        return packed

    kp = pack(pack_keys_kernel, (n_k, 2 * run + META, hd), positions, documents, key_vecs, value_vecs)
    q_shape = (n_q, 2 * rows + META, hd)
    qp = pack(pack_queries_kernel, q_shape, positions, documents, queries, out_grad, cost=10**9)
    kp = swap(kp, "far")
    qp, kp = lax.optimization_barrier((qp, kp))
    qp = swap(qp, "head")
    kp = lax.all_gather(kp, "core", axis=0, tiled=False)
    full = struct((2 * keys, n_q * rows), f32)
    line = pltpu.VMEM((n_q, rows), f32)
    st, e, dp, top = call(
        stats_kernel,
        [SMEM] + [VMEM] * 2,
        [struct((n_q, 2 * n_q, rows), f32), full, full, struct((2 * keys // CHUNK, n_q * rows), f32)],
        [pltpu.VMEM((2 * keys, hd), f32)],
    )(side, qp, kp)
    st = swap(st, "head")
    gq, keep, give = call(
        grads_kernel,
        [SMEM] + [VMEM] * 6,
        [pltpu.HBM((n_q, rows, hd), bf), struct((n_k, 2 * run, hd), f32), struct((n_k, 2 * run, hd), bf)],
        [line, line, pltpu.VMEM(full.shape, bf), pltpu.VMEM((n_q, rows, hd), bf), pltpu.SemaphoreType.DMA((1,))],
        out_specs=[HBM, VMEM, VMEM],
    )(side, qp, kp, st, e, dp, top)
    gq = swap(gq, "head")
    both = lax.all_gather(give, "core", axis=0, tiled=False)
    gkv = (keep + jnp.where(side[0] == 0, both[1], both[0]).astype(f32)).astype(bf)
    gkv, gq = lax.optimization_barrier((gkv, gq))
    gkv = swap(gkv, "far")
    return tuple(
        call(
            finish_kernel,
            [VMEM] * 2,
            [struct((run, heads * hd), f32), struct((run, hd), f32), struct((run, hd), f32)],
        )(gq, gkv)
    )


def solution(mesh):
    n_head, n_ctx = mesh.devices.shape
    fine = Mesh(mesh.devices.reshape(n_head, n_ctx // 2, 2), ("head", "far", "core"))
    tok = P(("head", "far", "core"))
    two = P(("head", "far", "core"), None)
    return jax.shard_map(
        on_device,
        mesh=fine,
        in_specs=(two, two, two, two, tok, tok),
        out_specs=(two, two, two),
        check_vma=False,
    )
```
